128 devices in a mesh: seq: 16 (over y, x_lo, core), rows: 8 (over x_hi, z).
Axes of the slice: x: 4 (x_hi: 2, x_lo: 2; x = x_hi * 2 + x_lo), y: 4, z: 4, core: 2. Of those that a mesh axis runs over, the one named last changes fastest.
Arguments:
- inputs: bfloat16 [8, 2048, 1024], P('rows', 'seq'), may hold values from -6 to 6
- cotangent: bfloat16 [8, 2048, 1024], P('rows', 'seq'), may hold values from -6 to 6
- group_order: int32 [32], replicated, may hold values from 0 to 31, each once
- ln_gain: float32 [1024], replicated, may hold values from 0.1 to 1.9
- ln_bias: float32 [1024], replicated, may hold values from -3 to 3
- w_qkv: bfloat16 [1024, 3072], replicated, may hold values from -0.1875 to 0.1875
- b_qkv: float32 [3072], replicated, may hold values from -0.3 to 0.3
- w_out: bfloat16 [1024, 1024], replicated, may hold values from -3 to 3
- w_gate: bfloat16 [1024, 2816], replicated, may hold values from -0.1875 to 0.1875
- w_up: bfloat16 [1024, 2816], replicated, may hold values from -0.1875 to 0.1875
- w_down: bfloat16 [2816, 1024], replicated, may hold values from -0.109375 to 0.109375
Outputs:
- output: bfloat16 [8, 2048, 1024], P('rows', 'seq')
- input_grad: bfloat16 [8, 2048, 1024], P('rows', 'seq')
- grad_qkv: float32 [1024, 3072], P(('seq', 'rows'))
- grad_out: float32 [1024, 1024], P(('seq', 'rows'))
- grad_gate: float32 [1024, 2816], P(('seq', 'rows'))
- grad_up: float32 [1024, 2816], P(('seq', 'rows'))
- grad_down: float32 [2816, 1024], P(('seq', 'rows'))
- grad_qkv_bias: float32 [3072], P(('seq', 'rows'))
- grad_ln_gain: float32 [1024], P(('seq', 'rows'))
- grad_ln_bias: float32 [1024], P(('seq', 'rows'))
The draws below stay inside these ranges and needn't reach their ends.
Inputs may be any that keep to these rules, and one draw needn't show every extreme that they name: `group_order`: a permutation of the group numbers 0 to 31.
All inputs are finite; a program needn't handle non-finite values.
Results may differ from the reference program's by a relative error of at most 0.014.
Values may be sent and summed in bfloat16 or wider, within the bound.
No kernel may reach another device: no remote copies, remote signals or barrier semaphores. Data moves between devices by JAX's collectives and lax.ppermute only.
A program may use at most 192 MiB of HBM per device.

```python
import jax
import jax.numpy as jnp
from jax import lax

D = 1024
HEADS = 16
HEAD_DIM = 64
ROT = 16
FF = 2816
GROUP = 64
GROUPS = 32
LENGTH = 2048
SEQS = 8


def levels(own_key, extent, shards, smallest, largest):
    gain, own = 1.0, jax.random.fold_in(own_key, 6)
    for position, parts in shards:
        heights = jnp.exp(jax.random.uniform(jax.random.fold_in(own, position), (parts,), jnp.float32, smallest / len(shards), largest / len(shards)))
        gain = gain * jnp.repeat(heights, extent[position] // parts).reshape([-1 if axis == position else 1 for axis in range(len(extent))])
    return gain


def noise(key, shape, spread, reach, split=(), held_as=jnp.bfloat16):
    array = spread * jax.random.normal(key, shape, jnp.float32)
    if split:
        array = array * levels(key, shape, split, -0.22, 0.18)
    return jnp.clip(array, -reach, reach).astype(held_as)


def setup_inputs(seed: int = 0) -> dict:
    key_of = jax.random.split(jax.random.key(seed), 12)
    inputs = noise(key_of[0], (SEQS, LENGTH, D), 1.0, 6.0, ((0, 8), (1, 16)))
    cotangent = noise(key_of[1], (SEQS, LENGTH, D), 1.0, 6.0, ((0, 8), (1, 16)))
    group_order = jax.random.permutation(key_of[2], GROUPS).astype(jnp.int32)
    ln_gain = jnp.clip(1.0 + 0.18 * jax.random.normal(key_of[3], (D,), jnp.float32), 0.1, 1.9)
    ln_bias = noise(key_of[4], (D,), 0.5, 3.0, (), jnp.float32)
    w_qkv = noise(key_of[5], (D, 3 * D), D ** -0.5, 0.1875)
    b_qkv = noise(key_of[6], (3 * D,), 0.05, 0.3, (), jnp.float32)
    w_out = noise(key_of[7], (D, D), (max(D // 256, 1)) ** -0.5, 3.0)
    w_gate = noise(key_of[8], (D, FF), D ** -0.5, 0.1875)
    w_up = noise(key_of[9], (D, FF), D ** -0.5, 0.1875)
    w_down = noise(key_of[10], (FF, D), FF ** -0.5, 0.109375)
    return {"inputs": inputs, "cotangent": cotangent, "group_order": group_order, "ln_gain": ln_gain, "ln_bias": ln_bias, "w_qkv": w_qkv, "b_qkv": b_qkv, "w_out": w_out, "w_gate": w_gate, "w_up": w_up, "w_down": w_down}


@jax.custom_vjp
def low(v):
    return lax.optimization_barrier(v.astype(jnp.bfloat16)).astype(jnp.float32)

@jax.custom_vjp
def low_back(v):
    return v

def low_keep(v):
    return (low(v), None)

def low_pass(kept, grad):
    return (grad,)

def back_keep(v):
    return (v, None)

def back_low(kept, grad):
    return (low(grad),)
low.defvjp(low_keep, low_pass)
low_back.defvjp(back_keep, back_low)
epsilon = 1e-05
highest = lax.Precision.HIGHEST

def matmul(left, right):
    return jnp.dot(left, right, precision=highest)

def positions_of(group_order):
    rows_all = jnp.arange(LENGTH, dtype=jnp.int32)
    return group_order[rows_all // GROUP] * GROUP + rows_all % GROUP

def rotary_tables(positions):
    half_rot = ROT // 2
    frequency = 10000.0 ** (-jnp.arange(half_rot, dtype=jnp.float32) * (2.0 / ROT))
    angles = positions.astype(jnp.float32)[:, None] * frequency[None, :]
    return (jnp.cos(angles), jnp.sin(angles))

def rotate(tensor, cosine, sine_rows):
    half_rot = ROT // 2
    first_half = tensor[..., :half_rot]
    second_half = tensor[..., half_rot:ROT]
    cos_heads = cosine[:, None, :]
    sin_heads = sine_rows[:, None, :]
    return jnp.concatenate([first_half * cos_heads - second_half * sin_heads, second_half * cos_heads + first_half * sin_heads, tensor[..., ROT:]], -1)

def attend(queries, key_rows, values, positions):
    length = queries.shape[0]
    block_rows = min(512, length)
    query_blocks = queries.reshape(length // block_rows, block_rows, HEADS, HEAD_DIM)
    pos_blocks = positions.reshape(length // block_rows, block_rows)

    def per_block(block_pair):
        block_query, block_pos = block_pair
        scores = jnp.einsum('qhd,khd->hqk', block_query, key_rows, precision=highest)
        scores = low_back(scores)
        visible = positions[None, None, :] <= block_pos[None, :, None]
        masked = jnp.where(visible, scores, -1e+30)
        row_top = lax.optimization_barrier(jnp.max(masked, -1, keepdims=True))
        weights = jnp.where(visible, jnp.exp(masked - row_top), 0.0)
        prob_rows = low(weights / lax.optimization_barrier(jnp.sum(weights, -1, keepdims=True)))
        return jnp.einsum('hqk,khd->qhd', prob_rows, values, precision=highest)
    attended = lax.map(jax.checkpoint(per_block), (query_blocks, pos_blocks))
    return attended.reshape(length, HEADS * HEAD_DIM)

def forward_layer(inputs_f, ln_gain, ln_bias, w_qkv, b_qkv, w_out, w_gate, w_up, w_down, cosine, sine_rows, positions):
    row_mean = lax.optimization_barrier(jnp.mean(inputs_f, -1, keepdims=True))
    centred = inputs_f - row_mean
    inv_std = lax.rsqrt(lax.optimization_barrier(jnp.mean(centred * centred, -1, keepdims=True)) + epsilon)
    hidden_in = low(centred * inv_std * ln_gain + ln_bias)
    qkv_proj = low_back(matmul(hidden_in, w_qkv) + b_qkv)
    length = inputs_f.shape[0]
    heads_shape = (length, HEADS, HEAD_DIM)
    queries = low(rotate(qkv_proj[:, :D].reshape(heads_shape), cosine, sine_rows) * HEAD_DIM ** (-0.5))
    key_rows = low(rotate(qkv_proj[:, D:2 * D].reshape(heads_shape), cosine, sine_rows))
    values = low(qkv_proj[:, 2 * D:].reshape(heads_shape))
    attended = low(low_back(attend(queries, key_rows, values, positions)))
    gate_proj = low_back(matmul(hidden_in, w_gate))
    up_proj = low_back(matmul(hidden_in, w_up))
    activation = low(jax.nn.silu(gate_proj) * up_proj)
    return inputs_f + matmul(attended, w_out) + matmul(activation, w_down)

def reference(inputs, cotangent, group_order, ln_gain, ln_bias, w_qkv, b_qkv, w_out, w_gate, w_up, w_down):
    positions = positions_of(group_order)
    cosine, sine_rows = rotary_tables(positions)
    params = tuple((weight.astype(jnp.float32) for weight in (ln_gain, ln_bias, w_qkv, b_qkv, w_out, w_gate, w_up, w_down)))

    def per_sequence(summed, seq_pair):
        inputs_f = seq_pair[0].astype(jnp.float32)
        grad_rows = seq_pair[1].astype(jnp.float32)

        def layer_call(layer_in, *weights):
            return forward_layer(layer_in, *weights, cosine, sine_rows, positions)
        result, pull_back = jax.vjp(layer_call, inputs_f, *params)
        gradients = pull_back(grad_rows)
        summed = tuple((acc_sum + grad for acc_sum, grad in zip(summed, gradients[1:])))
        return (summed, (result.astype(jnp.bfloat16), gradients[0].astype(jnp.bfloat16)))
    zero_grads = tuple((jnp.zeros_like(weight) for weight in params))
    summed, (output, input_grad) = lax.scan(per_sequence, zero_grads, (inputs, cotangent))
    g_gain, g_bias, g_qkv, g_bqkv, g_out, g_gate, g_up, g_down = summed
    return (output, input_grad, g_qkv, g_out, g_gate, g_up, g_down, g_bqkv, g_gain, g_bias)
```

```python
import functools

import jax
import jax.numpy as jnp
from jax import lax
from jax.experimental import pallas as pl
from jax.experimental.pallas import tpu as pltpu
from jax.sharding import PartitionSpec as P

HEADS = 16
HEAD_DIM = 64
ROT = 16
GROUP = 64
LENGTH = 2048
WIDTH = 1024
FF = 2816
FF_LOCAL = 176
BLOCK = 256
epsilon = 1e-05
f32 = jnp.float32
bf16 = jnp.bfloat16


def dot_nn(a, b):
    return lax.dot_general(a, b, (((1,), (0,)), ((), ())), preferred_element_type=f32)


def dot_nt(a, b):
    return lax.dot_general(a, b, (((1,), (1,)), ((), ())), preferred_element_type=f32)


def dot_tn(a, b):
    return lax.dot_general(a, b, (((0,), (0,)), ((), ())), preferred_element_type=f32)


def rotary_tables():
    half = ROT // 2
    lane = jnp.arange(2 * HEAD_DIM, dtype=jnp.int32) % HEAD_DIM
    frequency = 10000.0 ** (-(lane % half).astype(f32) * (2.0 / ROT))
    angles = jnp.arange(LENGTH, dtype=f32)[:, None] * frequency[None, :]
    cosine, sine = jnp.cos(angles), jnp.sin(angles)
    return (
        jnp.where(lane < ROT, cosine, 1.0),
        jnp.where(lane < half, sine, 0.0),
        jnp.where((lane >= half) & (lane < ROT), sine, 0.0),
    )


def attention_kernel(order, qk_in, vd_in, cos_t, sin_a, sin_b, out_ref, qk, vd, dkv, res):
    groups = LENGTH // GROUP
    for g in range(groups):
        at = pl.multiple_of(order[g] * GROUP, GROUP)
        qk[pl.ds(at, GROUP), :] = qk_in[g * GROUP : (g + 1) * GROUP, :]
        vd[pl.ds(at, GROUP), :] = vd_in[g * GROUP : (g + 1) * GROUP, :]
    lanes = 2 * HEAD_DIM
    raw = qk[...]
    turned = (
        raw * cos_t[...]
        - pltpu.roll(raw, lanes - ROT // 2, 1) * sin_a[...]
        + pltpu.roll(raw, ROT // 2, 1) * sin_b[...]
    )
    q = (turned[:, :HEAD_DIM] * HEAD_DIM**-0.5).astype(bf16)
    k = turned[:, HEAD_DIM:].astype(bf16)
    v = vd[:, :HEAD_DIM]
    do = vd[:, HEAD_DIM:]
    k_t = k.astype(f32).T.astype(bf16)
    v_t = v.astype(f32).T.astype(bf16)
    dkv[...] = jnp.zeros_like(dkv)
    row = lax.broadcasted_iota(jnp.int32, (BLOCK, BLOCK), 0)
    col = lax.broadcasted_iota(jnp.int32, (BLOCK, BLOCK), 1)
    visible = row <= col
    for i in range(LENGTH // BLOCK):
        lo, n = i * BLOCK, (i + 1) * BLOCK
        q_i, do_i = q[lo:n], do[lo:n]
        scores = dot_nt(k[:n], q_i)
        last = jnp.where(visible, scores[lo:], -1e30)
        scores = last if i == 0 else jnp.concatenate([scores[:lo], last], 0)
        top = jnp.max(scores, 0, keepdims=True)
        weights = jnp.exp(scores - top)
        probs = weights * (1.0 / jnp.sum(weights, 0, keepdims=True))
        probs_b = probs.astype(bf16)
        att_t = dot_nn(v_t[:, :n], probs_b)
        grad_p = dot_nt(v[:n], do_i)
        delta = jnp.sum(att_t * do_i.astype(f32).T, 0, keepdims=True)
        grad_s = (probs * (grad_p - delta)).astype(bf16)
        dq_t = dot_nn(k_t[:, :n], grad_s) * HEAD_DIM**-0.5
        dkv[:n, :HEAD_DIM] += dot_nn(grad_s, q_i)
        dkv[:n, HEAD_DIM:] += dot_nn(probs_b, do_i)
        res[lo:n, :] = jnp.concatenate([att_t.T, dq_t.T], 1)
    grads = jnp.concatenate([res[:, HEAD_DIM:], dkv[:, :HEAD_DIM]], 1)
    back = (
        grads * cos_t[...]
        + pltpu.roll(grads, lanes - ROT // 2, 1) * sin_a[...]
        - pltpu.roll(grads, ROT // 2, 1) * sin_b[...]
    )
    qk[...] = back
    vd[...] = jnp.concatenate([res[:, :HEAD_DIM], dkv[:, HEAD_DIM:]], 1).astype(bf16)
    for g in range(groups):
        at = pl.multiple_of(order[g] * GROUP, GROUP)
        out_ref[g * GROUP : (g + 1) * GROUP, :lanes] = qk[pl.ds(at, GROUP), :].astype(bf16)
        out_ref[g * GROUP : (g + 1) * GROUP, lanes:] = vd[pl.ds(at, GROUP), :]


def attention(order, qk, vd, tables):
    lanes = 2 * HEAD_DIM
    vmem = pl.BlockSpec(memory_space=pltpu.VMEM)
    return pl.pallas_call(
        attention_kernel,
        out_shape=jax.ShapeDtypeStruct((LENGTH, 2 * lanes), bf16),
        in_specs=[pl.BlockSpec(memory_space=pltpu.SMEM)] + [vmem] * 5,
        out_specs=vmem,
        scratch_shapes=[
            pltpu.VMEM((LENGTH, lanes), f32),
            pltpu.VMEM((LENGTH, lanes), bf16),
            pltpu.VMEM((LENGTH, lanes), f32),
            pltpu.VMEM((LENGTH, lanes), f32),
        ],
        compiler_params=pltpu.CompilerParams(vmem_limit_bytes=48 * 1024 * 1024),
        cost_estimate=pl.CostEstimate(
            flops=14 * LENGTH * LENGTH * HEAD_DIM // 2 * 8,
            bytes_accessed=8 * 1024 * 1024,
            transcendentals=LENGTH * LENGTH // 2,
        ),
        name="attention",
    )(order, qk, vd, *tables)


def normalise(rows):
    rows = rows.astype(f32)
    mean = jnp.mean(rows, 1, keepdims=True)
    centred = rows - mean
    inv_std = lax.rsqrt(jnp.mean(centred * centred, 1, keepdims=True) + epsilon)
    return centred * inv_std, inv_std


def gated_grads(gate, up, grad_act):
    sig = jax.nn.sigmoid(gate)
    grad_g = grad_act * up * sig * (1.0 + gate * (1.0 - sig))
    grad_u = grad_act * gate * sig
    return grad_g.astype(bf16), grad_u.astype(bf16)


def shards(x, dy, order, ln_gain, ln_bias, w_qkv, b_qkv, w_out, w_gate, w_up, w_down):
    x, dy = x[0], dy[0]
    rows_here = x.shape[0]
    s = lax.axis_index("seq")
    r = lax.axis_index("rows")
    x_all = lax.all_gather(x, "seq", axis=0, tiled=True)
    dy_all = lax.all_gather(dy, "seq", axis=0, tiled=True)

    head = s * HEAD_DIM
    w_qk_s = jnp.concatenate(
        [lax.dynamic_slice_in_dim(w_qkv, head + i * WIDTH, HEAD_DIM, 1) for i in range(3)], 1
    )
    b_qk_s = jnp.concatenate(
        [lax.dynamic_slice_in_dim(b_qkv, head + i * WIDTH, HEAD_DIM, 0) for i in range(3)], 0
    )
    w_out_s = lax.dynamic_slice_in_dim(w_out, head, HEAD_DIM, 0)
    unit_at = s * FF_LOCAL
    w_gu_s = jnp.concatenate(
        [
            lax.dynamic_slice_in_dim(w_gate, unit_at, FF_LOCAL, 1),
            lax.dynamic_slice_in_dim(w_up, unit_at, FF_LOCAL, 1),
        ],
        1,
    )
    w_down_s = lax.dynamic_slice_in_dim(w_down, unit_at, FF_LOCAL, 0)
    tables = rotary_tables()

    unit, inv_std = normalise(x)
    hidden = (unit * ln_gain + ln_bias).astype(bf16)
    gate = dot_nn(hidden, w_gate)
    up = dot_nn(hidden, w_up)
    activation = (jax.nn.silu(gate) * up).astype(bf16)
    result = x.astype(f32) + dot_nn(activation, w_down)
    grad_g, grad_u = gated_grads(gate, up, dot_nt(dy, w_down))
    grad_hidden = dot_nt(grad_g, w_gate) + dot_nt(grad_u, w_up)

    unit_all, _ = normalise(x_all)
    hidden_all = (unit_all * ln_gain + ln_bias).astype(bf16)
    unit_all = unit_all.astype(bf16)
    qkv_s = dot_nn(hidden_all, w_qk_s) + b_qk_s
    grad_att = dot_nt(dy_all, w_out_s)
    vd = jnp.concatenate([qkv_s[:, 2 * HEAD_DIM :], grad_att], 1).astype(bf16)
    heads = attention(order, qkv_s[:, : 2 * HEAD_DIM], vd, tables)

    heads_here = lax.all_to_all(
        heads.reshape(HEADS, rows_here, 4 * HEAD_DIM), "seq", 0, 0, tiled=True
    )

    def columns(at):
        part = heads_here[:, :, at * HEAD_DIM : (at + 1) * HEAD_DIM]
        return part.transpose(1, 0, 2).reshape(rows_here, WIDTH)

    grad_qkv_rows = jnp.concatenate([columns(0), columns(1), columns(3)], 1)
    result = result + dot_nn(columns(2), w_out)
    grad_hidden = grad_hidden + dot_nt(grad_qkv_rows, w_qkv)
    grad_unit = grad_hidden * ln_gain
    grad_norm = inv_std * (
        grad_unit
        - jnp.mean(grad_unit, 1, keepdims=True)
        - unit * jnp.mean(grad_unit * unit, 1, keepdims=True)
    )
    input_grad = (dy.astype(f32) + grad_norm).astype(bf16)

    def weight_terms(grads, weights):
        inner = dot_tn(unit_all, grads)
        total = jnp.sum(grads.astype(f32), 0)
        weights = weights.astype(f32)
        gain_part = jnp.sum(inner * weights, 1)
        bias_part = jnp.sum(weights * total[None, :], 1)
        return ln_gain[:, None] * inner + ln_bias[:, None] * total, total, gain_part, bias_part

    def by_owner(terms):
        width = terms.shape[1]
        return terms.astype(bf16).reshape(16, 8, 8, width).transpose(1, 0, 2, 3).reshape(8, 128, width)

    def sum_rows(terms):
        got = lax.all_to_all(terms, "rows", 0, 0, tiled=True)
        return jnp.sum(got.astype(f32), 0)

    gu = dot_nn(hidden_all, w_gu_s)
    gate_all, up_all = gu[:, :FF_LOCAL], gu[:, FF_LOCAL:]
    act_all = (jax.nn.silu(gate_all) * up_all).astype(bf16)
    gg_all, gu_all = gated_grads(gate_all, up_all, dot_nt(dy_all, w_down_s))
    g_gu, _, gain_1, bias_1 = weight_terms(jnp.concatenate([gg_all, gu_all], 1), w_gu_s)
    block_gu = jnp.concatenate(
        [g_gu, gain_1[:, None], bias_1[:, None], jnp.zeros((WIDTH, 30), f32)], 1
    )
    g_down = dot_tn(act_all, dy_all)
    g_out = dot_tn(heads[:, 2 * HEAD_DIM : 3 * HEAD_DIM], dy_all)
    block_rows = jnp.concatenate(
        [g_out.reshape(8, 8, WIDTH), g_down.reshape(8, 22, WIDTH), jnp.zeros((8, 2, WIDTH), f32)], 1
    ).astype(bf16)
    grads_s = jnp.concatenate([heads[:, : 2 * HEAD_DIM], heads[:, 3 * HEAD_DIM :]], 1)
    g_qkv, total, gain_2, bias_2 = weight_terms(grads_s, w_qk_s)
    extra = jnp.concatenate([total.reshape(8, 24), jnp.zeros((8, 38), f32)], 1)
    block_qkv = jnp.concatenate(
        [g_qkv, jnp.tile(extra, (128, 1)), gain_2[:, None], bias_2[:, None]], 1
    )

    sum_gu = sum_rows(by_owner(block_gu))
    sum_out = sum_rows(block_rows)
    sum_qkv = sum_rows(by_owner(block_qkv))
    both = jnp.concatenate([sum_gu, sum_qkv], 1).astype(bf16).reshape(16, 8, 640)
    mine = lax.all_to_all(both, "seq", 0, 0, tiled=True).astype(f32)

    def wide(at, width):
        return mine[:, :, at : at + width].transpose(1, 0, 2).reshape(8, 16 * width)

    o_gate = wide(0, FF_LOCAL)
    o_up = wide(FF_LOCAL, FF_LOCAL)
    o_qkv = jnp.concatenate([wide(384 + i * HEAD_DIM, HEAD_DIM) for i in range(3)], 1)
    o_gain = jnp.sum(mine[:, :, 352] + mine[:, :, 638], 0)
    o_bias = jnp.sum(mine[:, :, 353] + mine[:, :, 639], 0)
    totals = mine[:, :, 576:600].reshape(16, 3, HEAD_DIM).transpose(1, 0, 2).reshape(3 * WIDTH)
    o_bqkv = lax.dynamic_slice_in_dim(totals, (s * 8 + r) * 24, 24, 0)
    return (
        result.astype(bf16)[None],
        input_grad[None],
        o_qkv,
        sum_out[:8],
        o_gate,
        o_up,
        sum_out[8:30],
        o_bqkv,
        o_gain,
        o_bias,
    )


def solution(mesh):
    rows = P("rows", "seq", None)
    both = P(("seq", "rows"), None)
    flat = P(("seq", "rows"))
    return jax.shard_map(
        shards,
        mesh=mesh,
        in_specs=(rows, rows) + (P(),) * 9,
        out_specs=(rows, rows, both, both, both, both, both, flat, flat, flat),
        check_vma=False,
    )
```

```python
import jax
import jax.numpy as jnp
import numpy as np
from jax import lax
from jax.experimental import pallas as pl
from jax.experimental.pallas import tpu as pltpu
from jax.sharding import PartitionSpec as P

HEADS = 16
HEAD_DIM = 64
ROT = 16
GROUP = 64
LENGTH = 2048
WIDTH = 1024
FF = 2816
FF_LOCAL = 176
BLOCK = 256
SEQ = 16
ROWS = 8
HERE = 128
epsilon = 1e-05
f32 = jnp.float32
bf16 = jnp.bfloat16
SMEM = pl.BlockSpec(memory_space=pltpu.SMEM)
VMEM = pl.BlockSpec(memory_space=pltpu.VMEM)
ANY = pl.BlockSpec(memory_space=pl.ANY)


def dot_nn(a, b):
    return lax.dot_general(a, b, (((1,), (0,)), ((), ())), preferred_element_type=f32)


def dot_nt(a, b):
    return lax.dot_general(a, b, (((1,), (1,)), ((), ())), preferred_element_type=f32)


def dot_tn(a, b):
    return lax.dot_general(a, b, (((0,), (0,)), ((), ())), preferred_element_type=f32)


def params(mib):
    return pltpu.CompilerParams(vmem_limit_bytes=mib * 1024 * 1024)


def cost(gflop, mib, exps=0):
    return pl.CostEstimate(
        flops=int(gflop * 1e9), bytes_accessed=int(mib * 2**20), transcendentals=int(exps)
    )


def normalise(rows):
    rows = rows.astype(f32)
    mean = jnp.mean(rows, 1, keepdims=True)
    centred = rows - mean
    inv_std = lax.rsqrt(jnp.mean(centred * centred, 1, keepdims=True) + epsilon)
    return centred * inv_std, inv_std


def gated(gate, up, grad_act):
    sig = 1.0 / (1.0 + jnp.exp(-gate))
    silu = gate * sig
    grad_g = grad_act * up * (sig * (1.0 + gate - silu))
    grad_u = grad_act * silu
    return (silu * up).astype(bf16), grad_g.astype(bf16), grad_u.astype(bf16)


def rotary_tables():
    half = ROT // 2
    lane = np.arange(2 * HEAD_DIM) % HEAD_DIM
    frequency = np.where(lane < ROT, 10000.0 ** (-(lane % half) * (2.0 / ROT)), 0.0)
    groups = np.arange(LENGTH // GROUP)[:, None] * GROUP * frequency
    inside = np.arange(GROUP)[:, None] * frequency
    parts = (np.cos(groups), np.sin(groups), np.cos(inside), np.sin(inside))
    return [jnp.asarray(part, f32) for part in parts]


def own_kernel(x, dy, gain, bias, wg, wu, wd, out, grad, hid):
    @pl.when(pl.program_id(0) == 0)
    def _():
        unit, _ = normalise(x[...])
        hid[...] = (unit * gain[...] + bias[...]).astype(bf16)
        out[...] = x[...].astype(f32)
        grad[...] = jnp.zeros_like(grad)

    gate = dot_nn(hid[...], wg[...])
    up = dot_nn(hid[...], wu[...])
    act, grad_g, grad_u = gated(gate, up, dot_nt(dy[...], wd[...]))
    out[...] += dot_nn(act, wd[...])
    grad[...] += dot_nt(grad_g, wg[...]) + dot_nt(grad_u, wu[...])


def own_rows(x, dy, gain, bias, w_gate, w_up, w_down):
    whole = pl.BlockSpec((HERE, WIDTH), lambda j: (0, 0))
    vector = pl.BlockSpec((1, WIDTH), lambda j: (0, 0))
    columns = pl.BlockSpec((WIDTH, BLOCK), lambda j: (0, j))
    return pl.pallas_call(
        own_kernel,
        grid=(FF // BLOCK,),
        out_shape=[jax.ShapeDtypeStruct((HERE, WIDTH), f32)] * 2,
        in_specs=[whole, whole, vector, vector, columns, columns]
        + [pl.BlockSpec((BLOCK, WIDTH), lambda j: (j, 0))],
        out_specs=[whole, whole],
        scratch_shapes=[pltpu.VMEM((HERE, WIDTH), bf16)],
        compiler_params=params(60),
        cost_estimate=cost(4.5, 18),
        name="own_rows",
    )(x, dy, gain, bias, w_gate, w_up, w_down)


def project_kernel(pieces, n_refs, slot, order, *refs):
    inputs, refs = refs[:n_refs], refs[n_refs:]
    w_qkv, b_qkv, w_o, gain, bias, cos_g, sin_g, cos_i, sin_i = refs[:9]
    unit_out, hid_out, dy_out, packed = refs[9:13]
    x_all, dy_all, unit, hid, piece_sems, out_sems = refs[13:]
    copies = []
    for i, (which, ref, at, rows, chip, offset) in enumerate(pieces):
        to = pl.multiple_of(slot[chip] * HERE + offset, 16)
        copy = pltpu.make_async_copy(
            inputs[ref].at[pl.ds(at, rows), :],
            (x_all, dy_all)[which].at[pl.ds(to, rows), :],
            piece_sems.at[i],
        )
        copy.start()
        copies.append(copy)
    for copy in copies:
        copy.wait()
    dy_copy = pltpu.make_async_copy(dy_all, dy_out, out_sems.at[2, 0])
    dy_copy.start()
    lanes = 2 * HEAD_DIM
    lane = lax.broadcasted_iota(jnp.int32, (1, lanes), 1)
    low = lane % HEAD_DIM < ROT // 2
    scale = jnp.where(lane < HEAD_DIM, HEAD_DIM**-0.5, 1.0)

    def out_copies(i):
        rows = pl.ds(pl.multiple_of(i * BLOCK, BLOCK), BLOCK)
        return [
            pltpu.make_async_copy(unit.at[rows, :], unit_out.at[rows, :], out_sems.at[0, i]),
            pltpu.make_async_copy(hid.at[rows, :], hid_out.at[rows, :], out_sems.at[1, i]),
        ]

    def step(i, carry):
        rows = pl.ds(pl.multiple_of(i * BLOCK, BLOCK), BLOCK)
        unit_f, _ = normalise(x_all[rows, :])
        hidden = (unit_f * gain[...] + bias[...]).astype(bf16)
        unit[rows, :] = unit_f.astype(bf16)
        hid[rows, :] = hidden
        for copy in out_copies(i):
            copy.start()
        qkv = dot_nn(hidden, w_qkv[...]) + b_qkv[...]
        grad_att = dot_nt(dy_all[rows, :], w_o[...])
        raw = qkv[:, :lanes]
        before, after = pltpu.roll(raw, ROT // 2, 1), pltpu.roll(raw, lanes - ROT // 2, 1)
        for g in range(BLOCK // GROUP):
            at = pl.ds(order[i * (BLOCK // GROUP) + g], 1)
            cg, sg = cos_g[at, :], sin_g[at, :]
            cosine = cg * cos_i[...] - sg * sin_i[...]
            sine = sg * cos_i[...] + cg * sin_i[...]
            part = slice(g * GROUP, (g + 1) * GROUP)
            turned = raw[part] * cosine + jnp.where(low, -after[part], before[part]) * sine
            packed[pl.ds(pl.multiple_of(i * BLOCK + g * GROUP, GROUP), GROUP), :lanes] = (
                turned * scale
            ).astype(bf16)
        packed[rows, lanes:] = jnp.concatenate(
            [qkv[:, lanes : lanes + HEAD_DIM], grad_att], 1
        ).astype(bf16)
        return carry

    lax.fori_loop(0, LENGTH // BLOCK, step, 0, unroll=2)
    for i in range(LENGTH // BLOCK):
        for copy in out_copies(i):
            copy.wait()
    dy_copy.wait()


def project(slot, order, arrays, pieces, w_qkv, b_qkv, w_o, gain, bias, tables):
    big = (LENGTH, WIDTH)
    return pl.pallas_call(
        lambda *refs: project_kernel(pieces, len(arrays), *refs),
        out_shape=[jax.ShapeDtypeStruct(big, bf16)] * 3
        + [jax.ShapeDtypeStruct((LENGTH, 4 * HEAD_DIM), bf16)],
        in_specs=[SMEM] * 2 + [ANY] * len(arrays) + [VMEM] * 9,
        out_specs=[ANY] * 3 + [VMEM],
        scratch_shapes=[pltpu.VMEM(big, bf16)] * 4
        + [
            pltpu.SemaphoreType.DMA((len(pieces),)),
            pltpu.SemaphoreType.DMA((3, LENGTH // BLOCK)),
        ],
        compiler_params=params(28),
        cost_estimate=cost(2, 20),
        name="project",
    )(slot, order, *arrays, w_qkv, b_qkv, w_o, gain, bias, *tables)


def attention_kernel(order, packed, cos_g, sin_g, cos_i, sin_i, out_ref, rows_in, dkv, res, turn):
    groups = LENGTH // GROUP
    for g in range(groups):
        at = pl.multiple_of(order[g] * GROUP, GROUP)
        rows_in[pl.ds(at, GROUP), :] = packed[g * GROUP : (g + 1) * GROUP, :]
    q = rows_in[:, :HEAD_DIM]
    k = rows_in[:, HEAD_DIM : 2 * HEAD_DIM]
    v = rows_in[:, 2 * HEAD_DIM : 3 * HEAD_DIM]
    do = rows_in[:, 3 * HEAD_DIM :]
    k_t = k.astype(f32).T.astype(bf16)
    v_t = v.astype(f32).T.astype(bf16)
    dkv[...] = jnp.zeros_like(dkv)
    row = lax.broadcasted_iota(jnp.int32, (BLOCK, BLOCK), 0)
    col = lax.broadcasted_iota(jnp.int32, (BLOCK, BLOCK), 1)
    visible = row <= col
    for i in range(LENGTH // BLOCK):
        lo, n = i * BLOCK, (i + 1) * BLOCK
        q_i, do_i = q[lo:n], do[lo:n]
        scores = dot_nt(k[:n], q_i)
        last = jnp.where(visible, scores[lo:], -1e30)
        scores = last if i == 0 else jnp.concatenate([scores[:lo], last], 0)
        top = jnp.max(scores, 0, keepdims=True)
        weights = jnp.exp(scores - top)
        inverse = 1.0 / jnp.sum(weights, 0, keepdims=True)
        weights_b = weights.astype(bf16)
        att_t = dot_nn(v_t[:, :n], weights_b) * inverse
        grad_p = dot_nt(v[:n], do_i)
        do_f = do_i.astype(f32)
        delta = jnp.sum(att_t * do_f.T, 0, keepdims=True)
        grad_s = (weights * (grad_p - delta)).astype(bf16)
        dq_t = dot_nn(k_t[:, :n], grad_s) * (inverse * HEAD_DIM**-0.5)
        scale = column(inverse)
        dkv[:n, :HEAD_DIM] += dot_nn(grad_s, (q_i.astype(f32) * scale).astype(bf16))
        dkv[:n, HEAD_DIM:] += dot_nn(weights_b, (do_f * scale).astype(bf16))
        res[lo:n, :] = jnp.concatenate([att_t.T, dq_t.T], 1)
    lanes = 2 * HEAD_DIM
    low = lax.broadcasted_iota(jnp.int32, (1, lanes), 1) % HEAD_DIM < ROT // 2
    for g in range(groups):
        part = slice(g * GROUP, (g + 1) * GROUP)
        cg, sg = cos_g[g : g + 1, :], sin_g[g : g + 1, :]
        cosine = cg * cos_i[...] - sg * sin_i[...]
        sine = sg * cos_i[...] + cg * sin_i[...]
        grads = jnp.concatenate([res[part, HEAD_DIM:], dkv[part, :HEAD_DIM]], 1)
        after = pltpu.roll(grads, lanes - ROT // 2, 1)
        before = pltpu.roll(grads, ROT // 2, 1)
        turn[part, :lanes] = (
            grads * cosine + jnp.where(low, after, -before) * sine
        ).astype(bf16)
        turn[part, lanes:] = jnp.concatenate(
            [dkv[part, HEAD_DIM:], res[part, :HEAD_DIM]], 1
        ).astype(bf16)
    for g in range(groups):
        at = pl.multiple_of(order[g] * GROUP, GROUP)
        out_ref[g * GROUP : (g + 1) * GROUP, :] = turn[pl.ds(at, GROUP), :]


def attention(order, packed, tables):
    lanes = 2 * HEAD_DIM
    return pl.pallas_call(
        attention_kernel,
        out_shape=jax.ShapeDtypeStruct((LENGTH, 2 * lanes), bf16),
        in_specs=[SMEM] + [VMEM] * 5,
        out_specs=VMEM,
        scratch_shapes=[
            pltpu.VMEM((LENGTH, 2 * lanes), bf16),
            pltpu.VMEM((LENGTH, lanes), f32),
            pltpu.VMEM((LENGTH, lanes), f32),
            pltpu.VMEM((LENGTH, 2 * lanes), bf16),
        ],
        compiler_params=params(28),
        cost_estimate=cost(15, 8, LENGTH * LENGTH // 2),
        name="attention",
    )(order, packed, *tables)


def column(row):
    return jnp.broadcast_to(row, (8, row.shape[1])).T[:, :1]


def weights_kernel(
    unit_in, hid_in, dy_in, heads, w_qkv, w_g, w_u, w_d, gain, bias, block,
    unit, hid, dy, acts, grads_g, grads_u, stage, sems,
):
    blocks = LENGTH // BLOCK

    def copies(i):
        rows = pl.ds(pl.multiple_of(i * BLOCK, BLOCK), BLOCK)
        return [
            pltpu.make_async_copy(src.at[rows, :], to.at[rows, :], sems.at[j, i])
            for j, (src, to) in enumerate(((hid_in, hid), (dy_in, dy), (unit_in, unit)))
        ]

    for j in range(3):
        for i in range(blocks):
            copies(i)[j].start()

    def step(i, totals):
        rows = pl.ds(pl.multiple_of(i * BLOCK, BLOCK), BLOCK)
        for copy in copies(i)[:2]:
            copy.wait()
        gate = dot_nn(hid[rows, :], w_g[...])
        up = dot_nn(hid[rows, :], w_u[...])
        act, grad_g, grad_u = gated(gate, up, dot_nt(dy[rows, :], w_d[...]))
        acts[rows, :] = act
        grads_g[rows, :] = grad_g
        grads_u[rows, :] = grad_u
        return (
            totals[0] + jnp.sum(grad_g.astype(f32), 0, keepdims=True),
            totals[1] + jnp.sum(grad_u.astype(f32), 0, keepdims=True),
        )

    zero = jnp.zeros((1, FF_LOCAL), f32)
    totals = lax.fori_loop(0, blocks, step, (zero, zero), unroll=2)
    for i in range(blocks):
        copies(i)[2].wait()
    gain_col, bias_col = column(gain[...]), column(bias[...])
    grads_all = heads[...]
    total_h = jnp.sum(grads_all.astype(f32), 0, keepdims=True)
    inner = [dot_tn(grads, unit[...]).T for grads in (grads_g[...], grads_u[...], grads_all)]
    terms, gain_part, bias_part = [], 0.0, 0.0
    for one, weights, total in zip(inner, (w_g, w_u, w_qkv), totals + (total_h,)):
        wide = weights[...].astype(f32)
        terms.append(one * gain_col + bias_col * total)
        gain_part += jnp.sum(one * wide, 1, keepdims=True)
        bias_part += jnp.sum(wide * total, 1, keepdims=True)
    row8 = lax.broadcasted_iota(jnp.int32, (8, 256), 0)
    lane8 = lax.broadcasted_iota(jnp.int32, (8, 256), 1)
    spread = jnp.where((lane8 // 24 == row8) & (lane8 < 192), total_h, 0.0).astype(bf16)
    pick_row = lax.broadcasted_iota(jnp.int32, (256, 256), 0)
    pick_lane = lax.broadcasted_iota(jnp.int32, (256, 256), 1)
    pick = ((pick_row % 24 + 192 == pick_lane) & (pick_row < 192)).astype(bf16)
    extra = dot_nn(spread, pick)
    lane = lax.broadcasted_iota(jnp.int32, (1, 256), 1)
    last = jnp.where(lane < 192, terms[2], 0.0).reshape(HERE, 8, 256) + extra[None]
    stage[:, :384] = jnp.concatenate(
        terms[:2] + [gain_part, bias_part, jnp.zeros((WIDTH, 30), f32)], 1
    )
    stage[:, 384:] = last.reshape(WIDTH, 256)
    down_all = dot_tn(acts[...], dy[...])
    out_all = dot_tn(grads_all[:, 3 * HEAD_DIM :], dy[...])
    for r in range(ROWS):
        for s in range(0, SEQ, 2):
            first, second = (s * ROWS + r) * 8, ((s + 1) * ROWS + r) * 8
            block[r, s * 8 : s * 8 + 16, :] = jnp.concatenate(
                [stage[first : first + 8, :], stage[second : second + 8, :]], 0
            ).astype(bf16)
        both = jnp.concatenate(
            [out_all[r * 8 : r * 8 + 8], down_all[r * 22 : (r + 1) * 22], jnp.zeros((2, WIDTH), f32)],
            0,
        ).astype(bf16)
        block[r, HERE : HERE + 32, :] = both[:, :640]
        block[r, HERE + 32 :, :384] = both[:, 640:]
        block[r, HERE + 32 :, 384:] = jnp.zeros((32, 256), bf16)


def weight_grads(unit, hid, dy, heads, w_qkv, w_g, w_u, w_d, gain, bias):
    big = (LENGTH, WIDTH)
    return pl.pallas_call(
        weights_kernel,
        out_shape=jax.ShapeDtypeStruct((ROWS, 192, 640), bf16),
        in_specs=[ANY] * 3 + [VMEM] * 7,
        out_specs=VMEM,
        scratch_shapes=[pltpu.VMEM(big, bf16)] * 3
        + [pltpu.VMEM((LENGTH, FF_LOCAL), bf16)] * 3
        + [pltpu.VMEM((WIDTH, 640), f32), pltpu.SemaphoreType.DMA((3, LENGTH // BLOCK))],
        compiler_params=params(40),
        cost_estimate=cost(8, 20),
        name="weight_grads",
    )(unit, hid, dy, heads, w_qkv, w_g, w_u, w_d, gain, bias)


def final_kernel(heads, x, dy, part, grad, gain, w_out, w_qkv, out, input_grad, att, rows, total):
    step = pl.program_id(0)

    @pl.when(step == 0)
    def _():
        for h in range(HEADS):
            here = heads[h * HERE : (h + 1) * HERE, :]
            at = h * HEAD_DIM
            for i in range(3):
                lo = i * WIDTH + at
                rows[:, lo : lo + HEAD_DIM] = here[:, i * HEAD_DIM : (i + 1) * HEAD_DIM]
            att[:, at : at + HEAD_DIM] = here[:, 3 * HEAD_DIM :]

    columns = pl.ds(pl.multiple_of(step * BLOCK, BLOCK), BLOCK)
    out[:, columns] = (part[:, columns] + dot_nn(att[...], w_out[...])).astype(bf16)
    total[:, columns] = grad[:, columns] + dot_nt(rows[...], w_qkv[...])

    @pl.when(step == pl.num_programs(0) - 1)
    def _():
        unit, inv_std = normalise(x[...])
        grad_unit = total[...] * gain[...]
        grad_norm = inv_std * (
            grad_unit
            - jnp.mean(grad_unit, 1, keepdims=True)
            - unit * jnp.mean(grad_unit * unit, 1, keepdims=True)
        )
        input_grad[...] = (dy[...].astype(f32) + grad_norm).astype(bf16)


def final_rows(heads, x, dy, part, grad, gain, w_out, w_qkv):
    fixed = lambda shape: pl.BlockSpec(shape, lambda j: (0,) * len(shape))
    own = fixed((HERE, WIDTH))
    return pl.pallas_call(
        final_kernel,
        grid=(WIDTH // BLOCK,),
        out_shape=[jax.ShapeDtypeStruct((HERE, WIDTH), bf16)] * 2,
        in_specs=[fixed((LENGTH, 256)), own, own, own, own, fixed((1, WIDTH))]
        + [pl.BlockSpec((WIDTH, BLOCK), lambda j: (0, j))]
        + [pl.BlockSpec((BLOCK, 3 * WIDTH), lambda j: (j, 0))],
        out_specs=[own, own],
        scratch_shapes=[
            pltpu.VMEM((HERE, WIDTH), bf16),
            pltpu.VMEM((HERE, 3 * WIDTH), bf16),
            pltpu.VMEM((HERE, WIDTH), f32),
        ],
        compiler_params=params(24),
        cost_estimate=cost(1.1, 10),
        name="final_rows",
    )(heads, x, dy, part, grad, gain, w_out, w_qkv)


def sum_kernel(got, send, down, out):
    total = got[0].astype(f32)
    for r in range(1, ROWS):
        total += got[r].astype(f32)
    send[...] = total[:HERE].astype(bf16)
    first, second = total[HERE : HERE + 32], total[HERE + 32 :, :384]
    out[:, :640] = first[:8]
    out[:, 640:] = second[:8]
    down[:, :640] = first[8:30]
    down[:, 640:] = second[8:30]


def sum_rows(got):
    return pl.pallas_call(
        sum_kernel,
        out_shape=[
            jax.ShapeDtypeStruct((HERE, 640), bf16),
            jax.ShapeDtypeStruct((22, WIDTH), f32),
            jax.ShapeDtypeStruct((8, WIDTH), f32),
        ],
        in_specs=[VMEM],
        out_specs=[VMEM] * 3,
        compiler_params=params(16),
        cost_estimate=cost(0.001, 2),
        name="sum_rows",
    )(got)


def layout_kernel(mine, qkv, gate, up, vectors, extra):
    total = jnp.zeros((8, 256), f32)
    more = jnp.zeros((8, 128), f32)
    for s in range(SEQ):
        here = mine[s * 8 : (s + 1) * 8, :].astype(f32)
        gate[:, s * FF_LOCAL : (s + 1) * FF_LOCAL] = here[:, :FF_LOCAL]
        up[:, s * FF_LOCAL : (s + 1) * FF_LOCAL] = here[:, FF_LOCAL : 2 * FF_LOCAL]
        for i in range(3):
            lo = i * WIDTH + s * HEAD_DIM
            qkv[:, lo : lo + HEAD_DIM] = here[:, 384 + i * HEAD_DIM : 384 + (i + 1) * HEAD_DIM]
        total += here[:, 384:]
        more += here[:, 256:384]
        extra[s * 8 : (s + 1) * 8, :] = here[:, 576:600]
    vectors[:, 0:1] = total[:, 216:217] + more[:, 96:97]
    vectors[:, 1:2] = total[:, 217:218] + more[:, 97:98]


def last_layout(mine):
    return pl.pallas_call(
        layout_kernel,
        out_shape=[
            jax.ShapeDtypeStruct((8, 3 * WIDTH), f32),
            jax.ShapeDtypeStruct((8, FF), f32),
            jax.ShapeDtypeStruct((8, FF), f32),
            jax.ShapeDtypeStruct((8, 2), f32),
            jax.ShapeDtypeStruct((HERE, 24), f32),
        ],
        in_specs=[VMEM],
        out_specs=[VMEM] * 5,
        compiler_params=params(16),
        cost_estimate=cost(0.001, 1),
        name="last_layout",
    )(mine)


PLACES = [(across, up) for across in (0, 1) for up in (-1, 0, 1, 2)]
CORE = [(i, i ^ 1) for i in range(SEQ)]
PAIR = [(i, i ^ 2) for i in range(SEQ)]
UP = [(i, (i + 4) % SEQ) for i in range(SEQ)]
DOWN = [(i, (i + 12) % SEQ) for i in range(SEQ)]


def send(value, to):
    return lax.ppermute(value, "seq", to)


def gather(x, dy, early):
    half = HERE
    own = jnp.concatenate([x, dy], 0)
    below = send(own, UP)
    above = send(own, DOWN)
    pair = send(own, PAIR)
    below, pair, early = lax.optimization_barrier((below, pair, early))
    far = send(below, UP)
    across_above = send(pair, DOWN)
    across_below = send(below, PAIR)
    cuts = (0, 80, 160, 256)
    last = [
        send(block[cuts[i] : cuts[i + 1]], to)
        for i, (block, to) in enumerate(((across_below, UP), (across_above, DOWN), (far, PAIR)))
    ]
    arrays = [own, below, above, pair, far, across_above, across_below] + last
    chips = [(0, 0), (0, -1), (0, 1), (1, 0), (0, 2), (1, 1), (1, -1)]
    pieces = []
    for a, chip in enumerate(chips):
        pieces += [(0, a, 0, half, chip, 0), (1, a, half, half, chip, 0)]
    end = (1, 2)
    pieces += [(0, 7, 0, 80, end, 0), (0, 8, 0, 48, end, 80), (1, 8, 48, 32, end, 0), (1, 9, 0, 96, end, 32)]
    n = len(arrays)
    swapped = [send(a, CORE) for a in arrays]
    table = []
    for core in range(2):
        for which, a, at, rows, chip, offset in pieces:
            table.append((which, a + core * n, at, rows, PLACES.index(chip) + core * 8, offset))
    return arrays + swapped, table, early


def shards(x, dy, order, ln_gain, ln_bias, w_qkv, b_qkv, w_out, w_gate, w_up, w_down):
    x, dy = x[0], dy[0]
    s = lax.axis_index("seq")
    r = lax.axis_index("rows")
    slot = jnp.stack(
        [
            ((s // 4 + up) % 4) * 4 + ((s // 2 % 2) ^ across) * 2 + (s % 2 ^ core)
            for core in range(2)
            for across, up in PLACES
        ]
    ).astype(jnp.int32)
    gain, bias = ln_gain[None, :], ln_bias[None, :]

    def cut(array, at, size, axis):
        return lax.dynamic_slice_in_dim(array, at, size, axis)

    head, unit_at = s * HEAD_DIM, s * FF_LOCAL
    w_qkv_s = jnp.concatenate(
        [cut(w_qkv, head + i * WIDTH, HEAD_DIM, 1) for i in range(3)]
        + [jnp.zeros((WIDTH, HEAD_DIM), bf16)],
        1,
    )
    b_qkv_s = jnp.concatenate(
        [cut(b_qkv, head + i * WIDTH, HEAD_DIM, 0) for i in range(3)] + [jnp.zeros((HEAD_DIM,), f32)]
    )[None, :]
    w_out_s = cut(w_out, head, HEAD_DIM, 0)
    w_gate_s = cut(w_gate, unit_at, FF_LOCAL, 1)
    w_up_s = cut(w_up, unit_at, FF_LOCAL, 1)
    w_down_s = cut(w_down, unit_at, FF_LOCAL, 0)
    early = (slot, w_qkv_s, b_qkv_s, w_gate_s, w_up_s, w_down_s, w_out_s)
    arrays, pieces, early = gather(x, dy, early)
    slot, w_qkv_s, b_qkv_s, w_gate_s, w_up_s, w_down_s, w_out_s = early

    tables = rotary_tables()
    unit, hid, dy_all, packed = project(
        slot, order, arrays, pieces, w_qkv_s, b_qkv_s, w_out_s, gain, bias, tables
    )
    heads = attention(order, packed, tables)
    heads_here = lax.all_to_all(heads, "seq", 0, 0, tiled=True)
    block = weight_grads(
        unit, hid, dy_all, heads, w_qkv_s, w_gate_s, w_up_s, w_down_s, gain, bias
    )
    block, heads_here = lax.optimization_barrier((block, heads_here))
    got = lax.all_to_all(block, "rows", 0, 0, tiled=True)
    x_late, _ = lax.optimization_barrier((x, heads_here))
    part, grad = own_rows(x_late, dy, gain, bias, w_gate, w_up, w_down)
    output, input_grad = final_rows(heads_here, x, dy, part, grad, gain, w_out, w_qkv)
    got, output, input_grad = lax.optimization_barrier((got, output, input_grad))
    outgoing, o_down, o_out = sum_rows(got)
    mine = lax.all_to_all(outgoing, "seq", 0, 0, tiled=True)
    o_qkv, o_gate, o_up, vectors, extra = last_layout(mine)
    totals = extra.reshape(SEQ, 3, HEAD_DIM).transpose(1, 0, 2).reshape(3 * WIDTH)
    o_bqkv = lax.dynamic_slice_in_dim(totals, (s * ROWS + r) * 24, 24, 0)
    return (
        output[None],
        input_grad[None],
        o_qkv,
        o_out,
        o_gate,
        o_up,
        o_down,
        o_bqkv,
        vectors[:, 0],
        vectors[:, 1],
    )


def solution(mesh):
    rows = P("rows", "seq", None)
    both = P(("seq", "rows"), None)
    flat = P(("seq", "rows"))
    return jax.shard_map(
        shards,
        mesh=mesh,
        in_specs=(rows, rows) + (P(),) * 9,
        out_specs=(rows, rows, both, both, both, both, both, flat, flat, flat),
        check_vma=False,
    )
```

```python
import jax
import jax.numpy as jnp
import numpy as np
from jax import lax
from jax.experimental import pallas as pl
from jax.experimental.pallas import tpu as pltpu
from jax.sharding import PartitionSpec as P

HEADS = 16
HEAD_DIM = 64
ROT = 16
GROUP = 64
LENGTH = 2048
WIDTH = 1024
FF = 2816
FF_LOCAL = 176
BLOCK = 256
SEQ = 16
ROWS = 8
HERE = 128
epsilon = 1e-05
f32 = jnp.float32
bf16 = jnp.bfloat16
SMEM = pl.BlockSpec(memory_space=pltpu.SMEM)
VMEM = pl.BlockSpec(memory_space=pltpu.VMEM)
ANY = pl.BlockSpec(memory_space=pl.ANY)


def dot_nn(a, b):
    return lax.dot_general(a, b, (((1,), (0,)), ((), ())), preferred_element_type=f32)


def dot_nt(a, b):
    return lax.dot_general(a, b, (((1,), (1,)), ((), ())), preferred_element_type=f32)


def dot_tn(a, b):
    return lax.dot_general(a, b, (((0,), (0,)), ((), ())), preferred_element_type=f32)


def params(mib):
    return pltpu.CompilerParams(vmem_limit_bytes=mib * 1024 * 1024)


def cost(gflop, mib, exps=0):
    return pl.CostEstimate(
        flops=int(gflop * 1e9), bytes_accessed=int(mib * 2**20), transcendentals=int(exps)
    )


def normalise(rows):
    rows = rows.astype(f32)
    mean = jnp.mean(rows, 1, keepdims=True)
    centred = rows - mean
    inv_std = lax.rsqrt(jnp.mean(centred * centred, 1, keepdims=True) + epsilon)
    return centred * inv_std, inv_std


def gated(gate, up, grad_act):
    sig = 1.0 / (1.0 + jnp.exp(-gate))
    silu = gate * sig
    grad_g = grad_act * up * (sig * (1.0 + gate - silu))
    grad_u = grad_act * silu
    return (silu * up).astype(bf16), grad_g.astype(bf16), grad_u.astype(bf16)


def rotary_tables():
    half = ROT // 2
    lane = np.arange(2 * HEAD_DIM) % HEAD_DIM
    frequency = np.where(lane < ROT, 10000.0 ** (-(lane % half) * (2.0 / ROT)), 0.0)
    groups = np.arange(LENGTH // GROUP)[:, None] * GROUP * frequency
    inside = np.arange(GROUP)[:, None] * frequency
    parts = (np.cos(groups), np.sin(groups), np.cos(inside), np.sin(inside))
    return jnp.asarray(np.concatenate(parts), f32)


def group_rotation(table, group):
    count = LENGTH // GROUP
    cos_g, sin_g = table[pl.ds(group, 1), :], table[pl.ds(group + count, 1), :]
    cos_i = table[2 * count : 2 * count + GROUP, :]
    sin_i = table[2 * count + GROUP :, :]
    return cos_g * cos_i - sin_g * sin_i, sin_g * cos_i + cos_g * sin_i


def own_kernel(x, dy, gain, bias, wg, wu, wd, out, grad, hid):
    @pl.when(pl.program_id(0) == 0)
    def _():
        unit, _ = normalise(x[...])
        hid[...] = (unit * gain[...] + bias[...]).astype(bf16)
        out[...] = x[...].astype(f32)
        grad[...] = jnp.zeros_like(grad)

    gate = dot_nn(hid[...], wg[...])
    up = dot_nn(hid[...], wu[...])
    act, grad_g, grad_u = gated(gate, up, dot_nt(dy[...], wd[...]))
    out[...] += dot_nn(act, wd[...])
    grad[...] += dot_nt(grad_g, wg[...]) + dot_nt(grad_u, wu[...])


def own_rows(x, dy, gain, bias, w_gate, w_up, w_down):
    whole = pl.BlockSpec((HERE, WIDTH), lambda j: (0, 0))
    vector = pl.BlockSpec((1, WIDTH), lambda j: (0, 0))
    columns = pl.BlockSpec((WIDTH, BLOCK), lambda j: (0, j))
    return pl.pallas_call(
        own_kernel,
        grid=(FF // BLOCK,),
        out_shape=[jax.ShapeDtypeStruct((HERE, WIDTH), f32)] * 2,
        in_specs=[whole, whole, vector, vector, columns, columns]
        + [pl.BlockSpec((BLOCK, WIDTH), lambda j: (j, 0))],
        out_specs=[whole, whole],
        scratch_shapes=[pltpu.VMEM((HERE, WIDTH), bf16)],
        compiler_params=params(60),
        cost_estimate=cost(0.001, 0.001),
        name="own_rows",
    )(x, dy, gain, bias, w_gate, w_up, w_down)


def heads_kernel(
    slot, order, x, dy, w_q, w_k, w_v, w_o, b_q, b_k, b_v, gain, bias,
    table, out, hid, cosine, sine,
):
    lanes = 2 * HEAD_DIM
    lane = lax.broadcasted_iota(jnp.int32, (1, lanes), 1)
    low = lane % HEAD_DIM < ROT // 2
    scale = jnp.where(lane < HEAD_DIM, HEAD_DIM**-0.5, 1.0)

    @pl.when(pl.program_id(0) == 0)
    def _():
        unit, _ = normalise(x[...])
        hid[...] = (unit * gain[...] + bias[...]).astype(bf16)
        for g in range(HERE // GROUP):
            rows = slice(g * GROUP, (g + 1) * GROUP)
            group = order[slot[0] * (HERE // GROUP) + g]
            cosine[rows, :], sine[rows, :] = group_rotation(table, group)

    q = dot_nn(hid[...], w_q[...]) + b_q[...]
    k = dot_nn(hid[...], w_k[...]) + b_k[...]
    v = dot_nn(hid[...], w_v[...]) + b_v[...]
    grad_att = dot_nt(dy[...], w_o[...])
    for h in range(BLOCK // HEAD_DIM):
        part = slice(h * HEAD_DIM, (h + 1) * HEAD_DIM)
        raw = jnp.concatenate([q[:, part], k[:, part]], 1)
        before, after = pltpu.roll(raw, ROT // 2, 1), pltpu.roll(raw, lanes - ROT // 2, 1)
        turned = (raw * cosine[...] + jnp.where(low, -after, before) * sine[...]) * scale
        rows = slice(h * HERE, (h + 1) * HERE)
        out[rows, :lanes] = turned.astype(bf16)
        out[rows, lanes:] = jnp.concatenate([v[:, part], grad_att[:, part]], 1).astype(bf16)


def own_heads(slot, order, x, dy, w_qkv, w_out, b_qkv, gain, bias, table):
    fixed = lambda shape: pl.BlockSpec(shape, lambda j: (0,) * len(shape))
    own, vector = fixed((HERE, WIDTH)), fixed((1, WIDTH))
    steps = WIDTH // BLOCK

    def part(rows, i):
        return pl.BlockSpec((rows, BLOCK), lambda j: (0, i * steps + j))

    return pl.pallas_call(
        heads_kernel,
        grid=(steps,),
        out_shape=jax.ShapeDtypeStruct((LENGTH, 4 * HEAD_DIM), bf16),
        in_specs=[SMEM] * 2
        + [own, own, part(WIDTH, 0), part(WIDTH, 1), part(WIDTH, 2)]
        + [pl.BlockSpec((BLOCK, WIDTH), lambda j: (j, 0)), part(1, 0), part(1, 1), part(1, 2)]
        + [vector, vector, fixed(table.shape)],
        out_specs=pl.BlockSpec((4 * HERE, 4 * HEAD_DIM), lambda j: (j, 0)),
        scratch_shapes=[
            pltpu.VMEM((HERE, WIDTH), bf16),
            pltpu.VMEM((HERE, 2 * HEAD_DIM), f32),
            pltpu.VMEM((HERE, 2 * HEAD_DIM), f32),
        ],
        compiler_params=params(60),
        cost_estimate=cost(1.1, 9),
        name="own_heads",
    )(slot, order, x, dy, w_qkv, w_qkv, w_qkv, w_out, b_qkv, b_qkv, b_qkv, gain, bias, table)


def attention_kernel(*refs):
    order, packed, table, out_ref, rows_in, dkv, res, turn = refs[-8:]
    groups = LENGTH // GROUP
    for g in range(groups):
        at = pl.multiple_of(order[g] * GROUP, GROUP)
        rows_in[pl.ds(at, GROUP), :] = packed[g * GROUP : (g + 1) * GROUP, :]
    q = rows_in[:, :HEAD_DIM]
    k = rows_in[:, HEAD_DIM : 2 * HEAD_DIM]
    v = rows_in[:, 2 * HEAD_DIM : 3 * HEAD_DIM]
    do = rows_in[:, 3 * HEAD_DIM :]
    k_t = k.astype(f32).T.astype(bf16)
    v_t = v.astype(f32).T.astype(bf16)
    dkv[...] = jnp.zeros_like(dkv)
    row = lax.broadcasted_iota(jnp.int32, (BLOCK, BLOCK), 0)
    col = lax.broadcasted_iota(jnp.int32, (BLOCK, BLOCK), 1)
    visible = row <= col
    for i in range(LENGTH // BLOCK):
        lo, n = i * BLOCK, (i + 1) * BLOCK
        q_i, do_i = q[lo:n], do[lo:n]
        scores = dot_nt(k[:n], q_i)
        last = jnp.where(visible, scores[lo:], -1e30)
        scores = last if i == 0 else jnp.concatenate([scores[:lo], last], 0)
        top = jnp.max(scores, 0, keepdims=True)
        weights = jnp.exp(scores - top)
        inverse = 1.0 / jnp.sum(weights, 0, keepdims=True)
        weights_b = weights.astype(bf16)
        att_t = dot_nn(v_t[:, :n], weights_b) * inverse
        grad_p = dot_nt(v[:n], do_i)
        do_f = do_i.astype(f32)
        delta = jnp.sum(att_t * do_f.T, 0, keepdims=True)
        grad_s = (weights * (grad_p - delta)).astype(bf16)
        dq_t = dot_nn(k_t[:, :n], grad_s) * (inverse * HEAD_DIM**-0.5)
        scale = column(inverse)
        dkv[:n, :HEAD_DIM] += dot_nn(grad_s, (q_i.astype(f32) * scale).astype(bf16))
        dkv[:n, HEAD_DIM:] += dot_nn(weights_b, (do_f * scale).astype(bf16))
        res[lo:n, :] = jnp.concatenate([att_t.T, dq_t.T], 1)
    lanes = 2 * HEAD_DIM
    low = lax.broadcasted_iota(jnp.int32, (1, lanes), 1) % HEAD_DIM < ROT // 2
    for g in range(groups):
        part = slice(g * GROUP, (g + 1) * GROUP)
        cosine, sine = group_rotation(table, g)
        grads = jnp.concatenate([res[part, HEAD_DIM:], dkv[part, :HEAD_DIM]], 1)
        after = pltpu.roll(grads, lanes - ROT // 2, 1)
        before = pltpu.roll(grads, ROT // 2, 1)
        turn[part, :lanes] = (
            grads * cosine + jnp.where(low, after, -before) * sine
        ).astype(bf16)
        turn[part, lanes:] = jnp.concatenate(
            [dkv[part, HEAD_DIM:], res[part, :HEAD_DIM]], 1
        ).astype(bf16)
    for g in range(groups):
        at = pl.multiple_of(order[g] * GROUP, GROUP)
        out_ref[g * GROUP : (g + 1) * GROUP, :] = turn[pl.ds(at, GROUP), :]


def attention(order, packed, table, first=()):
    lanes = 2 * HEAD_DIM
    return pl.pallas_call(
        attention_kernel,
        out_shape=jax.ShapeDtypeStruct((LENGTH, 2 * lanes), bf16),
        in_specs=[ANY] * len(first) + [SMEM] + [VMEM] * 2,
        out_specs=VMEM,
        scratch_shapes=[
            pltpu.VMEM((LENGTH, 2 * lanes), bf16),
            pltpu.VMEM((LENGTH, lanes), f32),
            pltpu.VMEM((LENGTH, lanes), f32),
            pltpu.VMEM((LENGTH, 2 * lanes), bf16),
        ],
        compiler_params=params(60),
        cost_estimate=cost(15, 8, LENGTH * LENGTH // 2),
        name="attention",
    )(*first, order, packed, table)


def cut_kernel(slot, w_qkv, w_gate, w_up, out_qkv, out_gate, out_up, wide_qkv, wide_gu, sems):
    here = slot[0]
    first = here * FF_LOCAL
    tile = jnp.minimum(first // 128, (FF - 384) // 128) * 128
    copies = []
    for i in range(3):
        lanes = pl.ds(pl.multiple_of(here // 2 * 128 + i * WIDTH, 128), 128)
        to = wide_qkv.at[:, i * 128 : (i + 1) * 128]
        copies.append(pltpu.make_async_copy(w_qkv.at[:, lanes], to, sems.at[i]))
    for i, source in enumerate((w_gate, w_up)):
        lanes = pl.ds(pl.multiple_of(tile, 128), 384)
        copies.append(pltpu.make_async_copy(source.at[:, lanes], wide_gu.at[i], sems.at[3 + i]))
    for copy in copies:
        copy.start()
    row = lax.broadcasted_iota(jnp.int32, (384, 256), 0)
    lane = lax.broadcasted_iota(jnp.int32, (384, 256), 1)
    source = lane // HEAD_DIM * 128 + here % 2 * HEAD_DIM + lane % HEAD_DIM
    pick_qkv = ((row == source) & (lane < 3 * HEAD_DIM)).astype(bf16)
    pick_gu = (row == lane + (first - tile)).astype(bf16)[:, :FF_LOCAL]
    for copy in copies:
        copy.wait()
    out_qkv[...] = dot_nn(wide_qkv[...], pick_qkv).astype(bf16)
    out_gate[...] = dot_nn(wide_gu[0], pick_gu).astype(bf16)
    out_up[...] = dot_nn(wide_gu[1], pick_gu).astype(bf16)


def cut_weights(slot, w_qkv, w_gate, w_up):
    return pl.pallas_call(
        cut_kernel,
        out_shape=[
            jax.ShapeDtypeStruct((WIDTH, 256), bf16),
            jax.ShapeDtypeStruct((WIDTH, FF_LOCAL), bf16),
            jax.ShapeDtypeStruct((WIDTH, FF_LOCAL), bf16),
        ],
        in_specs=[SMEM] + [ANY] * 3,
        out_specs=[VMEM] * 3,
        scratch_shapes=[
            pltpu.VMEM((WIDTH, 384), bf16),
            pltpu.VMEM((2, WIDTH, 384), bf16),
            pltpu.SemaphoreType.DMA((5,)),
        ],
        compiler_params=params(60),
        cost_estimate=cost(0.001, 0.001),
        name="cut_weights",
    )(slot, w_qkv, w_gate, w_up)


def column(row):
    return jnp.broadcast_to(row, (8, row.shape[1])).T[:, :1]


def weights_kernel(pieces, n_refs, slot, *refs):
    inputs, refs = refs[:n_refs], refs[n_refs:]
    heads_in, w_qkv, w_g, w_u, w_d_in, gain, bias, block_out = refs[:8]
    x_all, dy, unit, heads, acts, grads_g, grads_u, stage, w_d, block = refs[8:18]
    piece_sems, head_sems, out_sems, weight_sem = refs[18:]
    here = slot[0]
    w_d_copy = pltpu.make_async_copy(
        w_d_in.at[pl.ds(pl.multiple_of(here * FF_LOCAL, 16), FF_LOCAL), :], w_d, weight_sem
    )
    w_d_copy.start()
    copies = []
    for i, (which, ref, at, rows, chip, offset) in enumerate(pieces):
        copy = pltpu.make_async_copy(
            inputs[ref].at[pl.ds(at, rows), :],
            (x_all, dy)[which].at[pl.ds(chip * HERE + offset, rows), :],
            piece_sems.at[i],
        )
        copy.start()
        copies.append(copy)
    for i in range(SEQ):
        copy = pltpu.make_async_copy(
            heads_in.at[pl.ds(pl.multiple_of(slot[i] * HERE, HERE), HERE), :],
            heads.at[pl.ds(i * HERE, HERE), :],
            head_sems.at[i],
        )
        copy.start()
        copies.append(copy)
    for copy in copies + [w_d_copy]:
        copy.wait()
    totals = [0.0, 0.0]
    for i in range(LENGTH // BLOCK):
        rows = slice(i * BLOCK, (i + 1) * BLOCK)
        unit_f, _ = normalise(x_all[rows, :])
        hid = (unit_f * gain[...] + bias[...]).astype(bf16)
        unit[rows, :] = unit_f.astype(bf16)
        gate = dot_nn(hid, w_g[...])
        up = dot_nn(hid, w_u[...])
        act, grad_g, grad_u = gated(gate, up, dot_nt(dy[rows, :], w_d[...]))
        acts[rows, :] = act
        grads_g[rows, :] = grad_g
        grads_u[rows, :] = grad_u
        totals[0] += jnp.sum(grad_g.astype(f32), 0, keepdims=True)
        totals[1] += jnp.sum(grad_u.astype(f32), 0, keepdims=True)
    gain_col, bias_col = column(gain[...]), column(bias[...])
    grads_all = heads[:, : 3 * HEAD_DIM]
    total_h = jnp.sum(grads_all.astype(f32), 0, keepdims=True)
    inner = [dot_tn(grads, unit[...]).T for grads in (grads_g[...], grads_u[...], grads_all)]
    terms, gain_part, bias_part = [], 0.0, 0.0
    for one, weights, total in zip(inner, (w_g, w_u, w_qkv), totals + [total_h]):
        wide = weights[:, : one.shape[1]].astype(f32)
        terms.append(one * gain_col + bias_col * total)
        gain_part += jnp.sum(one * wide, 1, keepdims=True)
        bias_part += jnp.sum(wide * total, 1, keepdims=True)
    at_row = lax.broadcasted_iota(jnp.int32, (192, HERE), 0)
    owner = (at_row // HEAD_DIM * WIDTH + here * HEAD_DIM + at_row % HEAD_DIM) // 24
    mine = owner == lax.broadcasted_iota(jnp.int32, (192, HERE), 1)
    at_row = lax.broadcasted_iota(jnp.int32, (192, 256), 0)
    place = (at_row // HEAD_DIM * WIDTH + here * HEAD_DIM + at_row % HEAD_DIM) % 24 + 192
    pick = (place == lax.broadcasted_iota(jnp.int32, (192, 256), 1)).astype(bf16)
    extra = dot_tn(jnp.where(mine, column(total_h), 0.0).astype(bf16), pick)
    first_row = lax.broadcasted_iota(jnp.int32, (1, 8, 1), 1) == 0
    last = jnp.concatenate([terms[2], jnp.zeros((WIDTH, 64), f32)], 1).reshape(HERE, 8, 256)
    last += jnp.where(first_row, extra[:, None, :], 0.0)
    stage[:, :384] = jnp.concatenate(
        terms[:2] + [gain_part, bias_part, jnp.zeros((WIDTH, 30), f32)], 1
    )
    stage[:, 384:] = last.reshape(WIDTH, 256)
    down_all = dot_tn(acts[...], dy[...])
    out_all = dot_tn(heads[:, 3 * HEAD_DIM :], dy[...])
    outs = []
    for r in range(ROWS):
        for s in range(0, SEQ, 2):
            first, second = (s * ROWS + r) * 8, ((s + 1) * ROWS + r) * 8
            block[r, s * 8 : s * 8 + 16, :] = jnp.concatenate(
                [stage[first : first + 8, :], stage[second : second + 8, :]], 0
            ).astype(bf16)
        both = jnp.concatenate(
            [out_all[r * 8 : r * 8 + 8], down_all[r * 22 : (r + 1) * 22], jnp.zeros((2, WIDTH), f32)],
            0,
        ).astype(bf16)
        block[r, HERE : HERE + 32, :] = both[:, :640]
        block[r, HERE + 32 :, :384] = both[:, 640:]
        block[r, HERE + 32 :, 384:] = jnp.zeros((32, 256), bf16)
        outs.append(pltpu.make_async_copy(block.at[r], block_out.at[r], out_sems.at[r]))
        outs[r].start()
    for copy in outs:
        copy.wait()


def weight_grads(slot, arrays, pieces, heads, w_qkv, w_g, w_u, w_d, gain, bias):
    big = (LENGTH, WIDTH)
    return pl.pallas_call(
        lambda *refs: weights_kernel(pieces, len(arrays), *refs),
        out_shape=jax.ShapeDtypeStruct((ROWS, 192, 640), bf16),
        in_specs=[SMEM] + [ANY] * (len(arrays) + 1) + [VMEM] * 3 + [ANY] + [VMEM] * 2,
        out_specs=ANY,
        scratch_shapes=[pltpu.VMEM(big, bf16)] * 3
        + [pltpu.VMEM((LENGTH, 4 * HEAD_DIM), bf16)]
        + [pltpu.VMEM((LENGTH, FF_LOCAL), bf16)] * 3
        + [
            pltpu.VMEM((WIDTH, 640), f32),
            pltpu.VMEM((FF_LOCAL, WIDTH), bf16),
            pltpu.VMEM((ROWS, 192, 640), bf16),
            pltpu.SemaphoreType.DMA((len(pieces),)),
            pltpu.SemaphoreType.DMA((SEQ,)),
            pltpu.SemaphoreType.DMA((ROWS,)),
            pltpu.SemaphoreType.DMA,
        ],
        compiler_params=params(60),
        cost_estimate=cost(8, 20),
        name="weight_grads",
    )(slot, *arrays, heads, w_qkv, w_g, w_u, w_d, gain, bias)


def final_kernel(heads, x, dy, part, grad, gain, w_out, w_qkv, out, input_grad, att, rows, total):
    step = pl.program_id(0)

    @pl.when(step == 0)
    def _():
        for h in range(HEADS):
            here = heads[h * HERE : (h + 1) * HERE, :]
            at = h * HEAD_DIM
            for i in range(3):
                lo = i * WIDTH + at
                rows[:, lo : lo + HEAD_DIM] = here[:, i * HEAD_DIM : (i + 1) * HEAD_DIM]
            att[:, at : at + HEAD_DIM] = here[:, 3 * HEAD_DIM :]

    columns = pl.ds(pl.multiple_of(step * BLOCK, BLOCK), BLOCK)
    out[:, columns] = (part[:, columns] + dot_nn(att[...], w_out[...])).astype(bf16)
    total[:, columns] = grad[:, columns] + dot_nt(rows[...], w_qkv[...])

    @pl.when(step == pl.num_programs(0) - 1)
    def _():
        unit, inv_std = normalise(x[...])
        grad_unit = total[...] * gain[...]
        grad_norm = inv_std * (
            grad_unit
            - jnp.mean(grad_unit, 1, keepdims=True)
            - unit * jnp.mean(grad_unit * unit, 1, keepdims=True)
        )
        input_grad[...] = (dy[...].astype(f32) + grad_norm).astype(bf16)


def final_rows(heads, x, dy, part, grad, gain, w_out, w_qkv):
    fixed = lambda shape: pl.BlockSpec(shape, lambda j: (0,) * len(shape))
    own = fixed((HERE, WIDTH))
    return pl.pallas_call(
        final_kernel,
        grid=(WIDTH // BLOCK,),
        out_shape=[jax.ShapeDtypeStruct((HERE, WIDTH), bf16)] * 2,
        in_specs=[fixed((LENGTH, 256)), own, own, own, own, fixed((1, WIDTH))]
        + [pl.BlockSpec((WIDTH, BLOCK), lambda j: (0, j))]
        + [pl.BlockSpec((BLOCK, 3 * WIDTH), lambda j: (j, 0))],
        out_specs=[own, own],
        scratch_shapes=[
            pltpu.VMEM((HERE, WIDTH), bf16),
            pltpu.VMEM((HERE, 3 * WIDTH), bf16),
            pltpu.VMEM((HERE, WIDTH), f32),
        ],
        compiler_params=params(60),
        cost_estimate=cost(1.1, 10),
        name="final_rows",
    )(heads, x, dy, part, grad, gain, w_out, w_qkv)


def sum_kernel(got, send, down, out):
    total = got[0].astype(f32)
    for r in range(1, ROWS):
        total += got[r].astype(f32)
    send[...] = total[:HERE].astype(bf16)
    first, second = total[HERE : HERE + 32], total[HERE + 32 :, :384]
    out[:, :640] = first[:8]
    out[:, 640:] = second[:8]
    down[:, :640] = first[8:30]
    down[:, 640:] = second[8:30]


def sum_rows(got):
    return pl.pallas_call(
        sum_kernel,
        out_shape=[
            jax.ShapeDtypeStruct((HERE, 640), bf16),
            jax.ShapeDtypeStruct((22, WIDTH), f32),
            jax.ShapeDtypeStruct((8, WIDTH), f32),
        ],
        in_specs=[VMEM],
        out_specs=[VMEM] * 3,
        compiler_params=params(16),
        cost_estimate=cost(0.001, 2),
        name="sum_rows",
    )(got)


def layout_kernel(mine, qkv, gate, up, vectors, sums):
    total = jnp.zeros((8, 256), f32)
    more = jnp.zeros((8, 128), f32)
    for s in range(SEQ):
        here = mine[s * 8 : (s + 1) * 8, :].astype(f32)
        gate[:, s * FF_LOCAL : (s + 1) * FF_LOCAL] = here[:, :FF_LOCAL]
        up[:, s * FF_LOCAL : (s + 1) * FF_LOCAL] = here[:, FF_LOCAL : 2 * FF_LOCAL]
        for i in range(3):
            lo = i * WIDTH + s * HEAD_DIM
            qkv[:, lo : lo + HEAD_DIM] = here[:, 384 + i * HEAD_DIM : 384 + (i + 1) * HEAD_DIM]
        total += here[:, 384:]
        more += here[:, 256:384]
    vectors[...] = more.T[96:98, :]
    sums[...] = total[0:1, 192:216]


def last_layout(mine):
    return pl.pallas_call(
        layout_kernel,
        out_shape=[
            jax.ShapeDtypeStruct((8, 3 * WIDTH), f32),
            jax.ShapeDtypeStruct((8, FF), f32),
            jax.ShapeDtypeStruct((8, FF), f32),
            jax.ShapeDtypeStruct((2, 8), f32),
            jax.ShapeDtypeStruct((1, 24), f32),
        ],
        in_specs=[VMEM],
        out_specs=[VMEM] * 5,
        compiler_params=params(16),
        cost_estimate=cost(0.001, 1),
        name="last_layout",
    )(mine)


PLACES = [(0, 0), (0, -1), (0, 1), (1, 0), (0, 2), (1, 1), (1, -1), (1, 2)]
CORE = [(i, i ^ 1) for i in range(SEQ)]
PAIR = [(i, i ^ 2) for i in range(SEQ)]
UP = [(i, (i + 4) % SEQ) for i in range(SEQ)]
DOWN = [(i, (i + 12) % SEQ) for i in range(SEQ)]


def send(value, to):
    return lax.ppermute(value, "seq", to)


def gather(x, dy, exchange, after):
    half = HERE
    own = jnp.concatenate([x, dy], 0)
    below = send(own, UP)
    above = send(own, DOWN)
    pair = send(own, PAIR)
    late = exchange((below, above, pair))
    far = send(below, UP)
    across_above = send(pair, DOWN)
    across_below = send(below, PAIR)
    far, _ = lax.optimization_barrier((far, late))
    opposite = send(far, PAIR)
    arrays = [own, below, above, pair, far, across_above, across_below, opposite]
    late, arrays[4:] = after(late, arrays[4:])
    arrays += [send(a, CORE) for a in arrays]
    table = []
    for i in range(len(PLACES)):
        for core in range(2):
            for which in range(2):
                table.append((which, i + core * len(PLACES), which * half, half, 2 * i + core, 0))
    return arrays, table, late


def shards(x, dy, order, ln_gain, ln_bias, w_qkv, b_qkv, w_out, w_gate, w_up, w_down):
    x, dy = x[0], dy[0]
    s = lax.axis_index("seq")
    slot = jnp.stack(
        [
            ((s // 4 + up) % 4) * 4 + ((s // 2 % 2) ^ across) * 2 + (s % 2 ^ core)
            for across, up in PLACES
            for core in range(2)
        ]
    ).astype(jnp.int32)
    gain, bias = ln_gain[None, :], ln_bias[None, :]

    table = rotary_tables()
    packed = own_heads(slot, order, x, dy, w_qkv, w_out, b_qkv[None, :], gain, bias, table)
    part, grad = own_rows(x, dy, gain, bias, w_gate, w_up, w_down)
    w_qkv_s, w_gate_s, w_up_s = cut_weights(slot, w_qkv, w_gate, w_up)

    def exchange(first):
        ready, _ = lax.optimization_barrier((packed, first))
        return lax.all_to_all(ready, "seq", 0, 0, tiled=True)

    def attend(packed_here, arrays):
        heads = attention(order, packed_here, table, (part, w_gate_s))
        return lax.optimization_barrier((heads, arrays))

    arrays, pieces, heads = gather(x, dy, exchange, attend)
    heads_here = lax.all_to_all(heads, "seq", 0, 0, tiled=True)
    block = weight_grads(
        slot, arrays, pieces, heads, w_qkv_s, w_gate_s, w_up_s, w_down, gain, bias
    )
    block, heads_here = lax.optimization_barrier((block, heads_here))
    got = lax.all_to_all(block, "rows", 0, 0, tiled=True)
    output, input_grad = final_rows(heads_here, x, dy, part, grad, gain, w_out, w_qkv)
    got, output, input_grad = lax.optimization_barrier((got, output, input_grad))
    outgoing, o_down, o_out = sum_rows(got)
    mine = lax.all_to_all(outgoing, "seq", 0, 0, tiled=True)
    o_qkv, o_gate, o_up, vectors, sums = last_layout(mine)
    return (
        output[None],
        input_grad[None],
        o_qkv,
        o_out,
        o_gate,
        o_up,
        o_down,
        sums[0],
        vectors[0],
        vectors[1],
    )


def solution(mesh):
    rows = P("rows", "seq", None)
    both = P(("seq", "rows"), None)
    flat = P(("seq", "rows"))
    return jax.shard_map(
        shards,
        mesh=mesh,
        in_specs=(rows, rows) + (P(),) * 9,
        out_specs=(rows, rows, both, both, both, both, both, flat, flat, flat),
        check_vma=False,
    )
```

```python
import jax
import jax.numpy as jnp
import numpy as np
from jax import lax
from jax.experimental import pallas as pl
from jax.experimental.pallas import tpu as pltpu
from jax.sharding import PartitionSpec as P

HEADS = 16
HEAD_DIM = 64
ROT = 16
GROUP = 64
LENGTH = 2048
WIDTH = 1024
FF = 2816
FF_LOCAL = 176
BLOCK = 256
SEQ = 16
ROWS = 8
HERE = 128
epsilon = 1e-05
f32 = jnp.float32
bf16 = jnp.bfloat16
SMEM = pl.BlockSpec(memory_space=pltpu.SMEM)
VMEM = pl.BlockSpec(memory_space=pltpu.VMEM)
ANY = pl.BlockSpec(memory_space=pl.ANY)


def dot_nn(a, b):
    return lax.dot_general(a, b, (((1,), (0,)), ((), ())), preferred_element_type=f32)


def dot_nt(a, b):
    return lax.dot_general(a, b, (((1,), (1,)), ((), ())), preferred_element_type=f32)


def dot_tn(a, b):
    return lax.dot_general(a, b, (((0,), (0,)), ((), ())), preferred_element_type=f32)


def dot_tt(a, b):
    return lax.dot_general(a, b, (((0,), (1,)), ((), ())), preferred_element_type=f32)


def params(mib):
    return pltpu.CompilerParams(vmem_limit_bytes=mib * 1024 * 1024)


def cost(gflop, mib, exps=0):
    return pl.CostEstimate(
        flops=int(gflop * 1e9), bytes_accessed=int(mib * 2**20), transcendentals=int(exps)
    )


def normalise(rows):
    rows = rows.astype(f32)
    mean = jnp.mean(rows, 1, keepdims=True)
    centred = rows - mean
    inv_std = lax.rsqrt(jnp.mean(centred * centred, 1, keepdims=True) + epsilon)
    return centred * inv_std, inv_std


def gated(gate, up, grad_act):
    sig = 1.0 / (1.0 + jnp.exp(-gate))
    silu = gate * sig
    grad_g = grad_act * up * (sig * (1.0 + gate - silu))
    grad_u = grad_act * silu
    return (silu * up).astype(bf16), grad_g.astype(bf16), grad_u.astype(bf16)


def rotary_tables():
    half = ROT // 2
    lane = np.arange(2 * HEAD_DIM) % HEAD_DIM
    frequency = np.where(lane < ROT, 10000.0 ** (-(lane % half) * (2.0 / ROT)), 0.0)
    groups = np.arange(LENGTH // GROUP)[:, None] * GROUP * frequency
    inside = np.arange(GROUP)[:, None] * frequency
    parts = (np.cos(groups), np.sin(groups), np.cos(inside), np.sin(inside))
    return jnp.asarray(np.concatenate(parts), f32)


def group_rotation(table, group):
    count = LENGTH // GROUP
    cos_g, sin_g = table[pl.ds(group, 1), :], table[pl.ds(group + count, 1), :]
    cos_i = table[2 * count : 2 * count + GROUP, :]
    sin_i = table[2 * count + GROUP :, :]
    return cos_g * cos_i - sin_g * sin_i, sin_g * cos_i + cos_g * sin_i


def own_kernel(x, dy, gain, bias, wg_in, wu_in, wd_in, out, grad, wg, wu, wd, sems):
    groups = ((0, 512), (512, 1280), (1280, 2048), (2048, 2816))
    copies = []
    for i, (lo, hi) in enumerate(groups):
        part = slice(lo, hi)
        pairs = ((wg_in.at[:, part], wg.at[:, part]), (wu_in.at[:, part], wu.at[:, part]))
        pairs += ((wd_in.at[part, :], wd.at[part, :]),)
        copies.append([pltpu.make_async_copy(*pair, sems.at[j, i]) for j, pair in enumerate(pairs)])
        for copy in copies[i]:
            copy.start()
    unit, _ = normalise(x[...])
    hid = (unit * gain[...] + bias[...]).astype(bf16)
    for i, (lo, hi) in enumerate(groups):
        for copy in copies[i]:
            copy.wait()
        part = slice(lo, hi)
        gate, up = dot_nn(hid, wg[:, part]), dot_nn(hid, wu[:, part])
        act, grad_g, grad_u = gated(gate, up, dot_nt(dy[...], wd[part, :]))
        more = dot_nt(grad_g, wg[:, part]) + dot_nt(grad_u, wu[:, part])
        out[...] = (x[...].astype(f32) if i == 0 else out[...]) + dot_nn(act, wd[part, :])
        grad[...] = more if i == 0 else grad[...] + more


def own_rows(x, dy, gain, bias, w_gate, w_up, w_down):
    return pl.pallas_call(
        own_kernel,
        out_shape=[jax.ShapeDtypeStruct((HERE, WIDTH), f32)] * 2,
        in_specs=[VMEM] * 4 + [ANY] * 3,
        out_specs=[VMEM] * 2,
        scratch_shapes=[
            pltpu.VMEM((WIDTH, FF), bf16),
            pltpu.VMEM((WIDTH, FF), bf16),
            pltpu.VMEM((FF, WIDTH), bf16),
            pltpu.SemaphoreType.DMA((3, 4)),
        ],
        compiler_params=params(60),
        cost_estimate=cost(4.5, 18),
        name="own_rows",
    )(x, dy, gain, bias, w_gate, w_up, w_down)


def heads_kernel(
    slot, order, x, dy, w_q, w_k, w_v, w_o, b_q, b_k, b_v, gain, bias,
    table, out, hid, cosine, sine,
):
    lanes = 2 * HEAD_DIM
    lane = lax.broadcasted_iota(jnp.int32, (1, lanes), 1)
    low = lane % HEAD_DIM < ROT // 2
    scale = jnp.where(lane < HEAD_DIM, HEAD_DIM**-0.5, 1.0)

    @pl.when(pl.program_id(0) == 0)
    def _():
        unit, _ = normalise(x[...])
        hid[...] = (unit * gain[...] + bias[...]).astype(bf16)
        for g in range(HERE // GROUP):
            rows = slice(g * GROUP, (g + 1) * GROUP)
            group = order[slot[0] * (HERE // GROUP) + g]
            cosine[rows, :], sine[rows, :] = group_rotation(table, group)

    q = dot_nn(hid[...], w_q[...]) + b_q[...]
    k = dot_nn(hid[...], w_k[...]) + b_k[...]
    v = dot_nn(hid[...], w_v[...]) + b_v[...]
    grad_att = dot_nt(dy[...], w_o[...])
    for h in range(BLOCK // HEAD_DIM):
        part = slice(h * HEAD_DIM, (h + 1) * HEAD_DIM)
        raw = jnp.concatenate([q[:, part], k[:, part]], 1)
        before, after = pltpu.roll(raw, ROT // 2, 1), pltpu.roll(raw, lanes - ROT // 2, 1)
        turned = (raw * cosine[...] + jnp.where(low, -after, before) * sine[...]) * scale
        rows = slice(h * HERE, (h + 1) * HERE)
        out[rows, :lanes] = turned.astype(bf16)
        out[rows, lanes:] = jnp.concatenate([v[:, part], grad_att[:, part]], 1).astype(bf16)


def own_heads(slot, order, x, dy, w_qkv, w_out, b_qkv, gain, bias, table):
    fixed = lambda shape: pl.BlockSpec(shape, lambda j: (0,) * len(shape))
    own, vector = fixed((HERE, WIDTH)), fixed((1, WIDTH))
    steps = WIDTH // BLOCK

    def part(rows, i):
        return pl.BlockSpec((rows, BLOCK), lambda j: (0, i * steps + j))

    return pl.pallas_call(
        heads_kernel,
        grid=(steps,),
        out_shape=jax.ShapeDtypeStruct((LENGTH, 4 * HEAD_DIM), bf16),
        in_specs=[SMEM] * 2
        + [own, own, part(WIDTH, 0), part(WIDTH, 1), part(WIDTH, 2)]
        + [pl.BlockSpec((BLOCK, WIDTH), lambda j: (j, 0)), part(1, 0), part(1, 1), part(1, 2)]
        + [vector, vector, fixed(table.shape)],
        out_specs=pl.BlockSpec((4 * HERE, 4 * HEAD_DIM), lambda j: (j, 0)),
        scratch_shapes=[
            pltpu.VMEM((HERE, WIDTH), bf16),
            pltpu.VMEM((HERE, 2 * HEAD_DIM), f32),
            pltpu.VMEM((HERE, 2 * HEAD_DIM), f32),
        ],
        compiler_params=params(60),
        cost_estimate=cost(1.1, 9),
        name="own_heads",
    )(slot, order, x, dy, w_qkv, w_qkv, w_qkv, w_out, b_qkv, b_qkv, b_qkv, gain, bias, table)


def attention_kernel(*refs):
    order, packed, table, out_ref, rows_in, cols_in, cols, turn = refs[-8:]
    groups = LENGTH // GROUP
    for g in range(groups):
        at = pl.multiple_of(order[g] * GROUP, GROUP)
        rows_in[pl.ds(at, GROUP), :] = packed[g * GROUP : (g + 1) * GROUP, :]
    cols_in[...] = rows_in[...].T
    k = rows_in[:, HEAD_DIM : 2 * HEAD_DIM]
    v = rows_in[:, 2 * HEAD_DIM : 3 * HEAD_DIM]
    q_t, k_t, v_t, do_t = (cols_in.at[i * HEAD_DIM : (i + 1) * HEAD_DIM, :] for i in range(4))
    dq_t, dk_t, dv_t, att_t = (cols.at[i * HEAD_DIM : (i + 1) * HEAD_DIM, :] for i in range(4))
    row = lax.broadcasted_iota(jnp.int32, (BLOCK, BLOCK), 0)
    col = lax.broadcasted_iota(jnp.int32, (BLOCK, BLOCK), 1)
    visible = row <= col
    def products(i):
        here, n = slice(i * BLOCK, (i + 1) * BLOCK), (i + 1) * BLOCK
        return dot_nn(k[:n], q_t[:, here]), dot_nn(v[:n], do_t[:, here])

    def softmax(i, scores):
        lo = i * BLOCK
        last = jnp.where(visible, scores[lo:], -1e30)
        scores = last if i == 0 else jnp.concatenate([scores[:lo], last], 0)
        top = jnp.max(scores, 0, keepdims=True)
        weights = jnp.exp(scores - top)
        inverse = 1.0 / jnp.sum(weights, 0, keepdims=True)
        return weights, weights.astype(bf16), inverse

    order_of = list(reversed(range(LENGTH // BLOCK)))
    ahead = products(order_of[0])
    for j, i in enumerate(order_of):
        lo, n = i * BLOCK, (i + 1) * BLOCK
        here, seen = slice(lo, n), slice(0, n)
        scores, grad_p = ahead
        if j + 1 < len(order_of):
            ahead = products(order_of[j + 1])
        weights, weights_b, inverse = softmax(i, scores)
        att = dot_nn(v_t[:, seen], weights_b) * inverse
        do_f = do_t[:, here].astype(f32)
        delta = jnp.sum(weights * grad_p, 0, keepdims=True) * inverse
        grad_s = (weights * (grad_p - delta)).astype(bf16)
        dv = dot_nt((do_f * inverse).astype(bf16), weights_b)
        att_t[:, here] = att
        dq_t[:, here] = dot_nn(k_t[:, seen], grad_s) * (inverse * HEAD_DIM**-0.5)
        dk = dot_nt((q_t[:, here].astype(f32) * inverse).astype(bf16), grad_s)
        if n == LENGTH:
            dk_t[...], dv_t[...] = dk, dv
        else:
            dk_t[:, seen] += dk
            dv_t[:, seen] += dv
    half = ROT // 2
    cosine, sine = table[:half, :], table[half:, :]
    for part in (dq_t, dk_t):
        first, second = part[:half, :], part[half:ROT, :]
        part[:half, :] = first * cosine + second * sine
        part[half:ROT, :] = second * cosine - first * sine
    turn[...] = cols[...].T.astype(bf16)
    for g in range(groups):
        at = pl.multiple_of(order[g] * GROUP, GROUP)
        out_ref[g * GROUP : (g + 1) * GROUP, :] = turn[pl.ds(at, GROUP), :]


def position_table():
    half = ROT // 2
    angles = 10000.0 ** (-np.arange(half)[:, None] * (2.0 / ROT)) * np.arange(LENGTH)
    return jnp.asarray(np.concatenate([np.cos(angles), np.sin(angles)]), f32)


def attention(order, packed, first=()):
    size = 4 * HEAD_DIM
    return pl.pallas_call(
        attention_kernel,
        out_shape=jax.ShapeDtypeStruct((LENGTH, size), bf16),
        in_specs=[ANY] * len(first) + [SMEM] + [VMEM] * 2,
        out_specs=VMEM,
        scratch_shapes=[
            pltpu.VMEM((LENGTH, size), bf16),
            pltpu.VMEM((size, LENGTH), bf16),
            pltpu.VMEM((size, LENGTH), f32),
            pltpu.VMEM((LENGTH, size), bf16),
        ],
        compiler_params=params(60),
        cost_estimate=cost(15, 8, LENGTH * LENGTH // 2),
        name="attention",
    )(*first, order, packed, position_table())


def cut_kernel(slot, w_qkv, w_gate, w_up, out_qkv, out_gu, wide_qkv, wide_gu, sems):
    here = slot[0]
    first = here * FF_LOCAL
    tile = jnp.minimum(first // 128, (FF - 384) // 128) * 128
    copies = []
    for i in range(3):
        lanes = pl.ds(pl.multiple_of(here // 2 * 128 + i * WIDTH, 128), 128)
        to = wide_qkv.at[:, i * 128 : (i + 1) * 128]
        copies.append(pltpu.make_async_copy(w_qkv.at[:, lanes], to, sems.at[i]))
    for i, source in enumerate((w_gate, w_up)):
        lanes = pl.ds(pl.multiple_of(tile, 128), 384)
        copies.append(pltpu.make_async_copy(source.at[:, lanes], wide_gu.at[i], sems.at[3 + i]))
    for copy in copies:
        copy.start()
    row = lax.broadcasted_iota(jnp.int32, (384, 256), 0)
    lane = lax.broadcasted_iota(jnp.int32, (384, 256), 1)
    source = lane // HEAD_DIM * 128 + here % 2 * HEAD_DIM + lane % HEAD_DIM
    pick_qkv = (row == source).astype(bf16)[:, : 3 * HEAD_DIM]
    pick_gu = (row == lane + (first - tile)).astype(bf16)[:, :FF_LOCAL]
    for copy in copies:
        copy.wait()
    out_qkv[...] = dot_tt(pick_qkv, wide_qkv[...]).astype(bf16)
    out_gu[:FF_LOCAL, :] = dot_tt(pick_gu, wide_gu[0]).astype(bf16)
    out_gu[FF_LOCAL:, :] = dot_tt(pick_gu, wide_gu[1]).astype(bf16)


def cut_weights(slot, w_qkv, w_gate, w_up):
    return pl.pallas_call(
        cut_kernel,
        out_shape=[
            jax.ShapeDtypeStruct((3 * HEAD_DIM, WIDTH), bf16),
            jax.ShapeDtypeStruct((2 * FF_LOCAL, WIDTH), bf16),
        ],
        in_specs=[SMEM] + [ANY] * 3,
        out_specs=[VMEM] * 2,
        scratch_shapes=[
            pltpu.VMEM((WIDTH, 384), bf16),
            pltpu.VMEM((2, WIDTH, 384), bf16),
            pltpu.SemaphoreType.DMA((5,)),
        ],
        compiler_params=params(60),
        cost_estimate=cost(0.001, 0.001),
        name="cut_weights",
    )(slot, w_qkv, w_gate, w_up)


def column(row):
    return jnp.broadcast_to(row, (8, row.shape[1])).T[:, :1]


def piece_copies(pieces, inputs, x_all, dy, sems):
    return [
        pltpu.make_async_copy(
            inputs[ref].at[pl.ds(which * HERE, HERE), :],
            (x_all, dy)[which].at[pl.ds(to * HERE, HERE), :],
            sems.at[i],
        )
        for i, (which, ref, to) in enumerate(pieces)
    ]


def down_copy(slot, source, to, sem):
    rows = pl.ds(pl.multiple_of(slot[0] * FF_LOCAL, 16), FF_LOCAL)
    return pltpu.make_async_copy(source.at[rows, :], to, sem)


def gate_blocks(count, x_all, dy, unit, w_gu, w_d, gain, bias, keep):
    total = 0.0
    for i in range(count):
        rows = slice(i * BLOCK, (i + 1) * BLOCK)
        unit_f, _ = normalise(x_all[rows, :])
        hid = (unit_f * gain[...] + bias[...]).astype(bf16)
        unit[rows, :] = unit_f.astype(bf16)
        gu = dot_nt(w_gu[...], hid)
        act, grad_g, grad_u = gated(gu[:FF_LOCAL], gu[FF_LOCAL:], dot_nt(w_d[...], dy[rows, :]))
        grads = jnp.concatenate([grad_g, grad_u], 0)
        keep(i, act, grads)
        total += jnp.sum(grads.astype(f32), 1, keepdims=True)
    return total


def first_kernel(pieces, n_refs, slot, *refs):
    inputs, refs = refs[:n_refs], refs[n_refs:]
    w_gu, w_d_in, gain, bias, unit, acts, grads, sums, x_all, dy, w_d, sems, sem = refs
    copies = piece_copies(pieces, inputs, x_all, dy, sems)
    copies.append(down_copy(slot, w_d_in, w_d, sem))
    for copy in copies:
        copy.start()
    for copy in copies:
        copy.wait()

    def keep(i, act, grad):
        acts[:, i * BLOCK : (i + 1) * BLOCK] = act
        grads[:, i * BLOCK : (i + 1) * BLOCK] = grad

    total = gate_blocks(x_all.shape[0] // BLOCK, x_all, dy, unit, w_gu, w_d, gain, bias, keep)
    sums[...] = jnp.broadcast_to(total, sums.shape)


def first_half(slot, arrays, pieces, w_gu, w_d, gain, bias):
    half = LENGTH // 2
    return pl.pallas_call(
        lambda *refs: first_kernel(pieces, len(arrays), *refs),
        out_shape=[
            jax.ShapeDtypeStruct((half, WIDTH), bf16),
            jax.ShapeDtypeStruct((FF_LOCAL, half), bf16),
            jax.ShapeDtypeStruct((2 * FF_LOCAL, half), bf16),
            jax.ShapeDtypeStruct((2 * FF_LOCAL, 128), f32),
        ],
        in_specs=[SMEM] + [ANY] * len(arrays) + [VMEM] + [ANY] + [VMEM] * 2,
        out_specs=[VMEM] * 4,
        scratch_shapes=[
            pltpu.VMEM((half, WIDTH), bf16),
            pltpu.VMEM((half, WIDTH), bf16),
            pltpu.VMEM((FF_LOCAL, WIDTH), bf16),
            pltpu.SemaphoreType.DMA((len(pieces),)),
            pltpu.SemaphoreType.DMA,
        ],
        compiler_params=params(60),
        cost_estimate=cost(0.001, 0.001),
        name="first_half",
    )(slot, *arrays, w_gu, w_d, gain, bias)


def weights_kernel(pieces, n_refs, slot, *refs):
    inputs, refs = refs[:n_refs], refs[n_refs:]
    heads_in, w_qkv, w_gu, w_d_in, gain, bias = refs[:6]
    unit_in, acts_in, grads_in, sums, block_out = refs[6:11]
    x_all, dy, unit, heads, left, right, stage, w_d, block = refs[11:20]
    piece_sems, head_sems, out_sems, first_sems, weight_sem = refs[20:]
    hidden, both = FF_LOCAL, 2 * FF_LOCAL
    here = slot[0]
    half = LENGTH // 2
    late = (dy.at[half:, :], unit.at[half:, :])
    copies = piece_copies(pieces, inputs, x_all, dy, piece_sems)
    now = [copy for copy, piece in zip(copies, pieces) if piece[2] >= SEQ // 2]
    now.append(down_copy(slot, w_d_in, w_d, weight_sem))
    later = [copy for copy, piece in zip(copies, pieces) if piece[0] and piece[2] < SEQ // 2]
    later.append(pltpu.make_async_copy(unit_in, unit.at[:half, :], first_sems.at[0]))
    later.append(pltpu.make_async_copy(acts_in, right.at[:hidden, :half], first_sems.at[1]))
    later.append(pltpu.make_async_copy(grads_in, left.at[:both, :half], first_sems.at[2]))
    for i in range(SEQ):
        rows = pl.ds(pl.multiple_of(slot[i] * HERE, HERE), HERE)
        to = heads.at[i * HERE : (i + 1) * HERE, :]
        later.append(pltpu.make_async_copy(heads_in.at[rows, :], to, head_sems.at[i]))
    for copy in now + later:
        copy.start()
    for copy in now:
        copy.wait()

    def keep(i, act, grad):
        at = slice(half + i * BLOCK, half + (i + 1) * BLOCK)
        right[:hidden, at] = act
        left[:both, at] = grad

    total = gate_blocks(half // BLOCK, x_all.at[half:, :], *late, w_gu, w_d, gain, bias, keep)
    total += sums[:, :1]
    for copy in later:
        copy.wait()
    heads_t = heads[...].T
    left[both:, :] = heads_t[: 3 * HEAD_DIM]
    right[hidden:, :] = heads_t[3 * HEAD_DIM :]
    total_h = jnp.sum(heads_t[: 3 * HEAD_DIM].astype(f32), 1, keepdims=True)
    inner = dot_nn(left[...], unit[...])
    total = jnp.concatenate([total, total_h], 0)
    wide = jnp.concatenate([w_gu[...], w_qkv[...]], 0).astype(f32)
    terms = inner * gain[...] + bias[...] * total
    gain_part = jnp.sum(inner * wide, 0, keepdims=True)
    bias_part = jnp.sum(wide * total, 0, keepdims=True)
    at_row = lax.broadcasted_iota(jnp.int32, (192, WIDTH), 0)
    column_at = at_row // HEAD_DIM * WIDTH + here * HEAD_DIM + at_row % HEAD_DIM
    mine = column_at // 24 * 8 == lax.broadcasted_iota(jnp.int32, (192, WIDTH), 1)
    at_lane = lax.broadcasted_iota(jnp.int32, (32, 192), 1)
    column_at = at_lane // HEAD_DIM * WIDTH + here * HEAD_DIM + at_lane % HEAD_DIM
    pick = (column_at % 24 + 2 == lax.broadcasted_iota(jnp.int32, (32, 192), 0)).astype(bf16)
    extra = dot_nn(pick, jnp.where(mine, total_h, 0.0).astype(bf16))
    row32 = lax.broadcasted_iota(jnp.int32, (32, WIDTH), 0)
    extra += jnp.where(row32 == 0, gain_part, jnp.where(row32 == 1, bias_part, 0.0))
    stage[...] = jnp.concatenate([terms[:both], extra, terms[both:]], 0).T
    products = dot_nn(right[...], dy[...])
    down_all, out_all = products[:hidden], products[hidden:]
    outs = []

    def two(s, lanes):
        first, second = (s * ROWS + r) * 8, ((s + 1) * ROWS + r) * 8
        return jnp.concatenate([stage[first : first + 8, lanes], stage[second : second + 8, lanes]], 0)

    for r in range(ROWS):
        for s in range(0, SEQ, 2):
            for i in range(4):
                lanes = slice(i * 128, (i + 1) * 128)
                block[r, i * HERE + s * 8 : i * HERE + s * 8 + 16, :] = two(s, lanes).astype(bf16)
        for s in range(0, SEQ // 2, 2):
            lanes = slice(512, 576)
            block[r, 512 + s * 8 : 528 + s * 8, :] = jnp.concatenate(
                [two(s, lanes), two(s + 8, lanes)], 1
            ).astype(bf16)
        last = jnp.concatenate(
            [out_all[r * 8 : r * 8 + 8], down_all[r * 22 : (r + 1) * 22], jnp.zeros((2, WIDTH), f32)],
            0,
        ).astype(bf16)
        for i in range(8):
            block[r, 576 + i * 32 : 608 + i * 32, :] = last[:, i * 128 : (i + 1) * 128]
        outs.append(pltpu.make_async_copy(block.at[r], block_out.at[r], out_sems.at[r]))
        outs[r].start()
    for copy in outs:
        copy.wait()


def weight_grads(slot, arrays, pieces, heads, w_qkv, w_gu, w_d, gain, bias, first):
    big = (LENGTH, WIDTH)
    return pl.pallas_call(
        lambda *refs: weights_kernel(pieces, len(arrays), *refs),
        out_shape=jax.ShapeDtypeStruct((ROWS, 832, 128), bf16),
        in_specs=[SMEM] + [ANY] * (len(arrays) + 1) + [VMEM] * 2 + [ANY] + [VMEM] * 2 + [ANY] * 3 + [VMEM],
        out_specs=ANY,
        scratch_shapes=[pltpu.VMEM(big, bf16)] * 3
        + [
            pltpu.VMEM((LENGTH, 4 * HEAD_DIM), bf16),
            pltpu.VMEM((2 * FF_LOCAL + 3 * HEAD_DIM, LENGTH), bf16),
            pltpu.VMEM((FF_LOCAL + HEAD_DIM, LENGTH), bf16),
            pltpu.VMEM((WIDTH, 576), f32),
            pltpu.VMEM((FF_LOCAL, WIDTH), bf16),
            pltpu.VMEM((ROWS, 832, 128), bf16),
            pltpu.SemaphoreType.DMA((len(pieces),)),
            pltpu.SemaphoreType.DMA((SEQ,)),
            pltpu.SemaphoreType.DMA((ROWS,)),
            pltpu.SemaphoreType.DMA((3,)),
            pltpu.SemaphoreType.DMA,
        ],
        compiler_params=params(60),
        cost_estimate=cost(8, 20),
        name="weight_grads",
    )(slot, *arrays, heads, w_qkv, w_gu, w_d, gain, bias, *first)


def final_kernel(heads, x, dy, part, grad, gain, w_out, w_qkv, out, input_grad, att, rows, total):
    step = pl.program_id(0)

    @pl.when(step == 0)
    def _():
        for h in range(HEADS):
            here = heads[h * HERE : (h + 1) * HERE, :]
            at = h * HEAD_DIM
            for i in range(3):
                lo = i * WIDTH + at
                rows[:, lo : lo + HEAD_DIM] = here[:, i * HEAD_DIM : (i + 1) * HEAD_DIM]
            att[:, at : at + HEAD_DIM] = here[:, 3 * HEAD_DIM :]

    columns = pl.ds(pl.multiple_of(step * BLOCK, BLOCK), BLOCK)
    out[:, columns] = (part[:, columns] + dot_nn(att[...], w_out[...])).astype(bf16)
    total[:, columns] = grad[:, columns] + dot_nt(rows[...], w_qkv[...])

    @pl.when(step == pl.num_programs(0) - 1)
    def _():
        unit, inv_std = normalise(x[...])
        grad_unit = total[...] * gain[...]
        grad_norm = inv_std * (
            grad_unit
            - jnp.mean(grad_unit, 1, keepdims=True)
            - unit * jnp.mean(grad_unit * unit, 1, keepdims=True)
        )
        input_grad[...] = (dy[...].astype(f32) + grad_norm).astype(bf16)


def final_rows(heads, x, dy, part, grad, gain, w_out, w_qkv):
    fixed = lambda shape: pl.BlockSpec(shape, lambda j: (0,) * len(shape))
    own = fixed((HERE, WIDTH))
    return pl.pallas_call(
        final_kernel,
        grid=(WIDTH // BLOCK,),
        out_shape=[jax.ShapeDtypeStruct((HERE, WIDTH), bf16)] * 2,
        in_specs=[fixed((LENGTH, 256)), own, own, own, own, fixed((1, WIDTH))]
        + [pl.BlockSpec((WIDTH, BLOCK), lambda j: (0, j))]
        + [pl.BlockSpec((BLOCK, 3 * WIDTH), lambda j: (j, 0))],
        out_specs=[own, own],
        scratch_shapes=[
            pltpu.VMEM((HERE, WIDTH), bf16),
            pltpu.VMEM((HERE, 3 * WIDTH), bf16),
            pltpu.VMEM((HERE, WIDTH), f32),
        ],
        compiler_params=params(60),
        cost_estimate=cost(1.1, 10),
        name="final_rows",
    )(heads, x, dy, part, grad, gain, w_out, w_qkv)


def sum_kernel(got, send, down, out):
    total = got[0].astype(f32)
    for r in range(1, ROWS):
        total += got[r].astype(f32)
    for i in range(4):
        send[:, i * 128 : (i + 1) * 128] = total[i * HERE : (i + 1) * HERE].astype(bf16)
    left = jnp.concatenate([total[512:576, :64], total[512:576, 64:]], 0)
    send[:, 512:] = jnp.concatenate([left, jnp.zeros((HERE, 64), f32)], 1).astype(bf16)
    for i in range(8):
        lanes = slice(i * 128, (i + 1) * 128)
        out[:, lanes] = total[576 + i * 32 : 584 + i * 32]
        down[:, lanes] = total[584 + i * 32 : 606 + i * 32]


def sum_rows(got):
    return pl.pallas_call(
        sum_kernel,
        out_shape=[
            jax.ShapeDtypeStruct((HERE, 640), bf16),
            jax.ShapeDtypeStruct((22, WIDTH), f32),
            jax.ShapeDtypeStruct((8, WIDTH), f32),
        ],
        in_specs=[VMEM],
        out_specs=[VMEM] * 3,
        compiler_params=params(16),
        cost_estimate=cost(0.001, 2),
        name="sum_rows",
    )(got)


def layout_kernel(mine, qkv, gate, up, vectors, sums):
    more = jnp.zeros((8, 128), f32)
    for s in range(SEQ):
        here = mine[s * 8 : (s + 1) * 8, :].astype(f32)
        gate[:, s * FF_LOCAL : (s + 1) * FF_LOCAL] = here[:, :FF_LOCAL]
        up[:, s * FF_LOCAL : (s + 1) * FF_LOCAL] = here[:, FF_LOCAL : 2 * FF_LOCAL]
        for i in range(3):
            lo = i * WIDTH + s * HEAD_DIM
            qkv[:, lo : lo + HEAD_DIM] = here[:, 384 + i * HEAD_DIM : 384 + (i + 1) * HEAD_DIM]
        more += here[:, 256:384]
    vectors[...] = more.T[96:98, :]
    sums[...] = more[0:1, 98:122]


def last_layout(mine):
    return pl.pallas_call(
        layout_kernel,
        out_shape=[
            jax.ShapeDtypeStruct((8, 3 * WIDTH), f32),
            jax.ShapeDtypeStruct((8, FF), f32),
            jax.ShapeDtypeStruct((8, FF), f32),
            jax.ShapeDtypeStruct((2, 8), f32),
            jax.ShapeDtypeStruct((1, 24), f32),
        ],
        in_specs=[VMEM],
        out_specs=[VMEM] * 5,
        compiler_params=params(16),
        cost_estimate=cost(0.001, 1),
        name="last_layout",
    )(mine)


PLACES = [(0, 0), (0, -1), (0, 1), (1, 0), (0, 2), (1, 1), (1, -1), (1, 2)]
CORE = [(i, i ^ 1) for i in range(SEQ)]
PAIR = [(i, i ^ 2) for i in range(SEQ)]
UP = [(i, (i + 4) % SEQ) for i in range(SEQ)]
DOWN = [(i, (i + 12) % SEQ) for i in range(SEQ)]
DOWN_PAIR = [(i, (i + 12) % SEQ ^ 2) for i in range(SEQ)]


def send(value, to):
    return lax.ppermute(value, "seq", to)


def gather(x, dy, exchange, after):
    own = jnp.concatenate([x, dy], 0)
    below = send(own, UP)
    above = send(own, DOWN)
    pair = send(own, PAIR)
    late = exchange((below, above, pair))
    far = send(below, UP)
    across_below = send(below, PAIR)
    across_above = send(pair, DOWN)
    opposite = send(above, DOWN_PAIR)
    arrays = [own, below, above, pair, far, across_above, across_below, opposite]
    first = [both for a in arrays[:4] for both in (a, send(a, CORE))]
    late, rest = after(late, first, arrays[4:])
    return first, [both for a in rest for both in (a, send(a, CORE))], late


def pieces_of(count):
    return [(which, i, i) for i in range(count) for which in range(2)]


def shards(x, dy, order, ln_gain, ln_bias, w_qkv, b_qkv, w_out, w_gate, w_up, w_down):
    x, dy = x[0], dy[0]
    s = lax.axis_index("seq")
    slot = jnp.stack(
        [
            ((s // 4 + up) % 4) * 4 + ((s // 2 % 2) ^ across) * 2 + (s % 2 ^ core)
            for across, up in PLACES
            for core in range(2)
        ]
    ).astype(jnp.int32)
    gain, bias = ln_gain[None, :], ln_bias[None, :]

    table = rotary_tables()
    packed = own_heads(slot, order, x, dy, w_qkv, w_out, b_qkv[None, :], gain, bias, table)
    w_qkv_s, w_gu_s = cut_weights(slot, w_qkv, w_gate, w_up)

    def exchange(first):
        ready, _ = lax.optimization_barrier((packed, (first, w_gu_s)))
        return lax.all_to_all(ready, "seq", 0, 0, tiled=True)

    def attend(packed_here, early, arrays):
        first = first_half(
            slot, early, pieces_of(len(early)), w_gu_s, w_down, gain, bias
        )
        heads = attention(order, packed_here, first)
        (heads, first), arrays = lax.optimization_barrier(((heads, first), arrays))
        return (heads, first), arrays

    early, arrays, (heads, first) = gather(x, dy, exchange, attend)
    heads_here = lax.all_to_all(heads, "seq", 0, 0, tiled=True)
    arrays = early + arrays
    block = weight_grads(
        slot, arrays, pieces_of(SEQ), heads, w_qkv_s, w_gu_s, w_down, gain, bias, first
    )
    block, heads_here = lax.optimization_barrier((block, heads_here))
    got = lax.all_to_all(block, "rows", 0, 0, tiled=True)
    x_late, _ = lax.optimization_barrier((x, heads_here))
    part, grad = own_rows(x_late, dy, gain, bias, w_gate, w_up, w_down)
    output, input_grad = final_rows(heads_here, x, dy, part, grad, gain, w_out, w_qkv)
    got, output, input_grad = lax.optimization_barrier((got, output, input_grad))
    outgoing, o_down, o_out = sum_rows(got)
    mine = lax.all_to_all(outgoing, "seq", 0, 0, tiled=True)
    o_qkv, o_gate, o_up, vectors, sums = last_layout(mine)
    return (
        output[None],
        input_grad[None],
        o_qkv,
        o_out,
        o_gate,
        o_up,
        o_down,
        sums[0],
        vectors[0],
        vectors[1],
    )


def solution(mesh):
    rows = P("rows", "seq", None)
    both = P(("seq", "rows"), None)
    flat = P(("seq", "rows"))
    return jax.shard_map(
        shards,
        mesh=mesh,
        in_specs=(rows, rows) + (P(),) * 9,
        out_specs=(rows, rows, both, both, both, both, both, flat, flat, flat),
        check_vma=False,
    )
```

```python
import jax
import jax.numpy as jnp
import numpy as np
from jax import lax
from jax.experimental import pallas as pl
from jax.experimental.pallas import tpu as pltpu
from jax.sharding import PartitionSpec as P

HEADS = 16
HEAD_DIM = 64
ROT = 16
GROUP = 64
LENGTH = 2048
WIDTH = 1024
FF = 2816
FF_LOCAL = 176
BLOCK = 256
SEQ = 16
ROWS = 8
HERE = 128
epsilon = 1e-05
f32 = jnp.float32
bf16 = jnp.bfloat16
SMEM = pl.BlockSpec(memory_space=pltpu.SMEM)
VMEM = pl.BlockSpec(memory_space=pltpu.VMEM)
ANY = pl.BlockSpec(memory_space=pl.ANY)


def dot_nn(a, b):
    return lax.dot_general(a, b, (((1,), (0,)), ((), ())), preferred_element_type=f32)


def dot_nt(a, b):
    return lax.dot_general(a, b, (((1,), (1,)), ((), ())), preferred_element_type=f32)


def dot_tn(a, b):
    return lax.dot_general(a, b, (((0,), (0,)), ((), ())), preferred_element_type=f32)


def dot_tt(a, b):
    return lax.dot_general(a, b, (((0,), (1,)), ((), ())), preferred_element_type=f32)


def params(mib):
    return pltpu.CompilerParams(vmem_limit_bytes=mib * 1024 * 1024)


def cost(gflop, mib, exps=0):
    return pl.CostEstimate(
        flops=int(gflop * 1e9), bytes_accessed=int(mib * 2**20), transcendentals=int(exps)
    )


def normalise(rows):
    rows = rows.astype(f32)
    mean = jnp.mean(rows, 1, keepdims=True)
    centred = rows - mean
    inv_std = lax.rsqrt(jnp.mean(centred * centred, 1, keepdims=True) + epsilon)
    return centred * inv_std, inv_std


def gated(gate, up, grad_act):
    sig = 1.0 / (1.0 + jnp.exp(-gate))
    silu = gate * sig
    grad_g = grad_act * up * (sig * (1.0 + gate - silu))
    grad_u = grad_act * silu
    return (silu * up).astype(bf16), grad_g.astype(bf16), grad_u.astype(bf16)


def rotary_tables():
    half = ROT // 2
    lane = np.arange(2 * HEAD_DIM) % HEAD_DIM
    frequency = np.where(lane < ROT, 10000.0 ** (-(lane % half) * (2.0 / ROT)), 0.0)
    groups = np.arange(LENGTH // GROUP)[:, None] * GROUP * frequency
    inside = np.arange(GROUP)[:, None] * frequency
    parts = (np.cos(groups), np.sin(groups), np.cos(inside), np.sin(inside))
    return jnp.asarray(np.concatenate(parts), f32)


def group_rotation(table, group):
    count = LENGTH // GROUP
    cos_g, sin_g = table[pl.ds(group, 1), :], table[pl.ds(group + count, 1), :]
    cos_i = table[2 * count : 2 * count + GROUP, :]
    sin_i = table[2 * count + GROUP :, :]
    return cos_g * cos_i - sin_g * sin_i, sin_g * cos_i + cos_g * sin_i


def own_kernel(x, dy, gain, bias, wg_in, wu_in, wd_in, out, grad, wg, wu, wd, sems):
    groups = ((0, 512), (512, 1280), (1280, 2048), (2048, 2816))
    copies = []
    for i, (lo, hi) in enumerate(groups):
        part = slice(lo, hi)
        pairs = ((wg_in.at[:, part], wg.at[:, part]), (wu_in.at[:, part], wu.at[:, part]))
        pairs += ((wd_in.at[part, :], wd.at[part, :]),)
        copies.append([pltpu.make_async_copy(*pair, sems.at[j, i]) for j, pair in enumerate(pairs)])
        for copy in copies[i]:
            copy.start()
    unit, _ = normalise(x[...])
    hid = (unit * gain[...] + bias[...]).astype(bf16)
    for i, (lo, hi) in enumerate(groups):
        for copy in copies[i]:
            copy.wait()
        part = slice(lo, hi)
        gate, up = dot_nn(hid, wg[:, part]), dot_nn(hid, wu[:, part])
        act, grad_g, grad_u = gated(gate, up, dot_nt(dy[...], wd[part, :]))
        more = dot_nt(grad_g, wg[:, part]) + dot_nt(grad_u, wu[:, part])
        out[...] = (x[...].astype(f32) if i == 0 else out[...]) + dot_nn(act, wd[part, :])
        grad[...] = more if i == 0 else grad[...] + more


def own_rows(x, dy, gain, bias, w_gate, w_up, w_down):
    return pl.pallas_call(
        own_kernel,
        out_shape=[jax.ShapeDtypeStruct((HERE, WIDTH), f32)] * 2,
        in_specs=[VMEM] * 4 + [ANY] * 3,
        out_specs=[VMEM] * 2,
        scratch_shapes=[
            pltpu.VMEM((WIDTH, FF), bf16),
            pltpu.VMEM((WIDTH, FF), bf16),
            pltpu.VMEM((FF, WIDTH), bf16),
            pltpu.SemaphoreType.DMA((3, 4)),
        ],
        compiler_params=params(60),
        cost_estimate=cost(4.5, 18),
        name="own_rows",
    )(x, dy, gain, bias, w_gate, w_up, w_down)


def heads_kernel(
    order, x, dy, w_q, w_k, w_v, w_o, b_q, b_k, b_v, gain, bias,
    table, out, hid, cosine, sine,
):
    lanes = 2 * HEAD_DIM
    lane = lax.broadcasted_iota(jnp.int32, (1, lanes), 1)
    low = lane % HEAD_DIM < ROT // 2
    scale = jnp.where(lane < HEAD_DIM, HEAD_DIM**-0.5, 1.0)

    @pl.when(pl.program_id(0) == 0)
    def _():
        unit, _ = normalise(x[...])
        hid[...] = (unit * gain[...] + bias[...]).astype(bf16)
        for g in range(HERE // GROUP):
            rows = slice(g * GROUP, (g + 1) * GROUP)
            group = order[lax.axis_index("seq") * (HERE // GROUP) + g]
            cosine[rows, :], sine[rows, :] = group_rotation(table, group)

    q = dot_nn(hid[...], w_q[...]) + b_q[...]
    k = dot_nn(hid[...], w_k[...]) + b_k[...]
    v = dot_nn(hid[...], w_v[...]) + b_v[...]
    grad_att = dot_nt(dy[...], w_o[...])
    for h in range(BLOCK // HEAD_DIM):
        part = slice(h * HEAD_DIM, (h + 1) * HEAD_DIM)
        raw = jnp.concatenate([q[:, part], k[:, part]], 1)
        before, after = pltpu.roll(raw, ROT // 2, 1), pltpu.roll(raw, lanes - ROT // 2, 1)
        turned = (raw * cosine[...] + jnp.where(low, -after, before) * sine[...]) * scale
        rows = slice(h * HERE, (h + 1) * HERE)
        out[rows, :lanes] = turned.astype(bf16)
        out[rows, lanes:] = jnp.concatenate([v[:, part], grad_att[:, part]], 1).astype(bf16)


def own_heads(order, x, dy, w_qkv, w_out, b_qkv, gain, bias, table):
    fixed = lambda shape: pl.BlockSpec(shape, lambda j: (0,) * len(shape))
    own, vector = fixed((HERE, WIDTH)), fixed((1, WIDTH))
    steps = WIDTH // BLOCK

    def part(rows, i):
        return pl.BlockSpec((rows, BLOCK), lambda j: (0, i * steps + j))

    return pl.pallas_call(
        heads_kernel,
        grid=(steps,),
        out_shape=jax.ShapeDtypeStruct((LENGTH, 4 * HEAD_DIM), bf16),
        in_specs=[SMEM]
        + [own, own, part(WIDTH, 0), part(WIDTH, 1), part(WIDTH, 2)]
        + [pl.BlockSpec((BLOCK, WIDTH), lambda j: (j, 0)), part(1, 0), part(1, 1), part(1, 2)]
        + [vector, vector, fixed(table.shape)],
        out_specs=pl.BlockSpec((4 * HERE, 4 * HEAD_DIM), lambda j: (j, 0)),
        scratch_shapes=[
            pltpu.VMEM((HERE, WIDTH), bf16),
            pltpu.VMEM((HERE, 2 * HEAD_DIM), f32),
            pltpu.VMEM((HERE, 2 * HEAD_DIM), f32),
        ],
        compiler_params=params(60),
        cost_estimate=cost(1.1, 9),
        name="own_heads",
    )(order, x, dy, w_qkv, w_qkv, w_qkv, w_out, b_qkv, b_qkv, b_qkv, gain, bias, table)


def attention_kernel(*refs):
    order, packed, table, out_ref, rows_in, cols_in, cols, turn = refs[-8:]
    groups = LENGTH // GROUP
    for g in range(groups):
        at = pl.multiple_of(order[g] * GROUP, GROUP)
        rows_in[pl.ds(at, GROUP), :] = packed[g * GROUP : (g + 1) * GROUP, :]
    cols_in[...] = rows_in[...].T
    k = rows_in[:, HEAD_DIM : 2 * HEAD_DIM]
    v = rows_in[:, 2 * HEAD_DIM : 3 * HEAD_DIM]
    q_t, k_t, v_t, do_t = (cols_in.at[i * HEAD_DIM : (i + 1) * HEAD_DIM, :] for i in range(4))
    dq_t, dk_t, dv_t, att_t = (cols.at[i * HEAD_DIM : (i + 1) * HEAD_DIM, :] for i in range(4))
    row = lax.broadcasted_iota(jnp.int32, (BLOCK, BLOCK), 0)
    col = lax.broadcasted_iota(jnp.int32, (BLOCK, BLOCK), 1)
    visible = row <= col
    def products(i):
        here, n = slice(i * BLOCK, (i + 1) * BLOCK), (i + 1) * BLOCK
        return dot_nn(k[:n], q_t[:, here]), dot_nn(v[:n], do_t[:, here])

    def softmax(i, scores):
        lo = i * BLOCK
        last = jnp.where(visible, scores[lo:], -1e30)
        scores = last if i == 0 else jnp.concatenate([scores[:lo], last], 0)
        top = jnp.max(scores, 0, keepdims=True)
        weights = jnp.exp(scores - top)
        inverse = 1.0 / jnp.sum(weights, 0, keepdims=True)
        return weights, weights.astype(bf16), inverse

    order_of = list(reversed(range(LENGTH // BLOCK)))
    ahead = products(order_of[0])
    for j, i in enumerate(order_of):
        lo, n = i * BLOCK, (i + 1) * BLOCK
        here, seen = slice(lo, n), slice(0, n)
        scores, grad_p = ahead
        if j + 1 < len(order_of):
            ahead = products(order_of[j + 1])
        weights, weights_b, inverse = softmax(i, scores)
        att = dot_nn(v_t[:, seen], weights_b) * inverse
        do_f = do_t[:, here].astype(f32)
        delta = jnp.sum(weights * grad_p, 0, keepdims=True) * inverse
        grad_s = (weights * (grad_p - delta)).astype(bf16)
        dv = dot_nt((do_f * inverse).astype(bf16), weights_b)
        att_t[:, here] = att
        dq_t[:, here] = dot_nn(k_t[:, seen], grad_s) * (inverse * HEAD_DIM**-0.5)
        dk = dot_nt((q_t[:, here].astype(f32) * inverse).astype(bf16), grad_s)
        if n == LENGTH:
            dk_t[...], dv_t[...] = dk, dv
        else:
            dk_t[:, seen] += dk
            dv_t[:, seen] += dv
    half = ROT // 2
    cosine, sine = table[:half, :], table[half:, :]
    for part in (dq_t, dk_t):
        first, second = part[:half, :], part[half:ROT, :]
        part[:half, :] = first * cosine + second * sine
        part[half:ROT, :] = second * cosine - first * sine
    turn[...] = cols[...].T.astype(bf16)
    for g in range(groups):
        at = pl.multiple_of(order[g] * GROUP, GROUP)
        out_ref[g * GROUP : (g + 1) * GROUP, :] = turn[pl.ds(at, GROUP), :]


def position_table():
    half = ROT // 2
    angles = 10000.0 ** (-np.arange(half)[:, None] * (2.0 / ROT)) * np.arange(LENGTH)
    return jnp.asarray(np.concatenate([np.cos(angles), np.sin(angles)]), f32)


def attention(order, packed, first=()):
    size = 4 * HEAD_DIM
    return pl.pallas_call(
        attention_kernel,
        out_shape=jax.ShapeDtypeStruct((LENGTH, size), bf16),
        in_specs=[ANY] * len(first) + [SMEM] + [VMEM] * 2,
        out_specs=VMEM,
        scratch_shapes=[
            pltpu.VMEM((LENGTH, size), bf16),
            pltpu.VMEM((size, LENGTH), bf16),
            pltpu.VMEM((size, LENGTH), f32),
            pltpu.VMEM((LENGTH, size), bf16),
        ],
        compiler_params=params(60),
        cost_estimate=cost(15, 8, LENGTH * LENGTH // 2),
        name="attention",
    )(*first, order, packed, position_table())


def cut_kernel(w_qkv, w_gate, w_up, out_qkv, out_gu, wide_qkv, wide_gu, sems):
    here = lax.axis_index("seq")
    first = here * FF_LOCAL
    tile = jnp.minimum(first // 128, (FF - 384) // 128) * 128
    copies = []
    for i in range(3):
        lanes = pl.ds(pl.multiple_of(here // 2 * 128 + i * WIDTH, 128), 128)
        to = wide_qkv.at[:, i * 128 : (i + 1) * 128]
        copies.append(pltpu.make_async_copy(w_qkv.at[:, lanes], to, sems.at[i]))
    for i, source in enumerate((w_gate, w_up)):
        lanes = pl.ds(pl.multiple_of(tile, 128), 384)
        copies.append(pltpu.make_async_copy(source.at[:, lanes], wide_gu.at[i], sems.at[3 + i]))
    for copy in copies:
        copy.start()
    row = lax.broadcasted_iota(jnp.int32, (384, 256), 0)
    lane = lax.broadcasted_iota(jnp.int32, (384, 256), 1)
    source = lane // HEAD_DIM * 128 + here % 2 * HEAD_DIM + lane % HEAD_DIM
    pick_qkv = (row == source).astype(bf16)[:, : 3 * HEAD_DIM]
    pick_gu = (row == lane + (first - tile)).astype(bf16)[:, :FF_LOCAL]
    for copy in copies:
        copy.wait()
    out_qkv[...] = dot_tt(pick_qkv, wide_qkv[...]).astype(bf16)
    out_gu[:FF_LOCAL, :] = dot_tt(pick_gu, wide_gu[0]).astype(bf16)
    out_gu[FF_LOCAL:, :] = dot_tt(pick_gu, wide_gu[1]).astype(bf16)


def cut_weights(w_qkv, w_gate, w_up):
    return pl.pallas_call(
        cut_kernel,
        out_shape=[
            jax.ShapeDtypeStruct((3 * HEAD_DIM, WIDTH), bf16),
            jax.ShapeDtypeStruct((2 * FF_LOCAL, WIDTH), bf16),
        ],
        in_specs=[ANY] * 3,
        out_specs=[VMEM] * 2,
        scratch_shapes=[
            pltpu.VMEM((WIDTH, 384), bf16),
            pltpu.VMEM((2, WIDTH, 384), bf16),
            pltpu.SemaphoreType.DMA((5,)),
        ],
        compiler_params=params(60),
        cost_estimate=cost(0.001, 0.001),
        name="cut_weights",
    )(w_qkv, w_gate, w_up)


def column(row):
    return jnp.broadcast_to(row, (8, row.shape[1])).T[:, :1]


def slot_of(i):
    here = lax.axis_index("seq")
    across, up = PLACES[i // 2]
    y = lax.rem(lax.div(here, 4) + (4 + up), 4)
    x = lax.rem(lax.div(here, 2) + across, 2)
    return y * 4 + x * 2 + lax.rem(here + i % 2, 2)


def piece_copies(pieces, inputs, x_all, dy, sems):
    return [
        pltpu.make_async_copy(
            inputs[ref].at[pl.ds(at, rows), :],
            (x_all, dy)[which].at[pl.ds(to, rows), :],
            sems.at[i],
        )
        for i, (which, ref, at, rows, to) in enumerate(pieces)
    ]


def down_copy(source, to, sem):
    rows = pl.ds(pl.multiple_of(lax.axis_index("seq") * FF_LOCAL, 16), FF_LOCAL)
    return pltpu.make_async_copy(source.at[rows, :], to, sem)


def gate_blocks(count, x_all, dy, unit, w_gu, w_d, gain, bias, keep):
    total = 0.0
    for i in range(count):
        rows = slice(i * BLOCK, (i + 1) * BLOCK)
        unit_f, _ = normalise(x_all[rows, :])
        hid = (unit_f * gain[...] + bias[...]).astype(bf16)
        unit[rows, :] = unit_f.astype(bf16)
        gu = dot_nt(w_gu[...], hid)
        act, grad_g, grad_u = gated(gu[:FF_LOCAL], gu[FF_LOCAL:], dot_nt(w_d[...], dy[rows, :]))
        grads = jnp.concatenate([grad_g, grad_u], 0)
        keep(i, act, grads)
        total += jnp.sum(grads.astype(f32), 1, keepdims=True)
    return total


def first_kernel(pieces, n_refs, *refs):
    inputs, refs = refs[:n_refs], refs[n_refs:]
    w_gu, w_d_in, gain, bias, unit, acts, grads, sums, x_all, dy, w_d, sems, sem = refs
    copies = piece_copies(pieces, inputs, x_all, dy, sems)
    copies.append(down_copy(w_d_in, w_d, sem))
    for copy in copies:
        copy.start()
    for copy in copies:
        copy.wait()

    def keep(i, act, grad):
        acts[:, i * BLOCK : (i + 1) * BLOCK] = act
        grads[:, i * BLOCK : (i + 1) * BLOCK] = grad

    total = gate_blocks(x_all.shape[0] // BLOCK, x_all, dy, unit, w_gu, w_d, gain, bias, keep)
    sums[...] = jnp.broadcast_to(total, sums.shape)


def first_half(arrays, pieces, w_gu, w_d, gain, bias):
    half = LENGTH // 2
    return pl.pallas_call(
        lambda *refs: first_kernel(pieces, len(arrays), *refs),
        out_shape=[
            jax.ShapeDtypeStruct((half, WIDTH), bf16),
            jax.ShapeDtypeStruct((FF_LOCAL, half), bf16),
            jax.ShapeDtypeStruct((2 * FF_LOCAL, half), bf16),
            jax.ShapeDtypeStruct((2 * FF_LOCAL, 128), f32),
        ],
        in_specs=[ANY] * len(arrays) + [VMEM] + [ANY] + [VMEM] * 2,
        out_specs=[VMEM] * 4,
        scratch_shapes=[
            pltpu.VMEM((half, WIDTH), bf16),
            pltpu.VMEM((half, WIDTH), bf16),
            pltpu.VMEM((FF_LOCAL, WIDTH), bf16),
            pltpu.SemaphoreType.DMA((len(pieces),)),
            pltpu.SemaphoreType.DMA,
        ],
        compiler_params=params(60),
        cost_estimate=cost(0.001, 0.001),
        name="first_half",
    )(*arrays, w_gu, w_d, gain, bias)


def weights_kernel(pieces, n_refs, *refs):
    inputs, refs = refs[:n_refs], refs[n_refs:]
    heads_in, w_qkv, w_gu, w_d_in, gain, bias = refs[:6]
    unit_in, acts_in, grads_in, sums, block_out = refs[6:11]
    x_all, dy, unit, heads, left, right, stage, w_d, block = refs[11:20]
    piece_sems, head_sems, out_sems, first_sems, weight_sem = refs[20:]
    hidden, both = FF_LOCAL, 2 * FF_LOCAL
    here = lax.axis_index("seq")
    half = LENGTH // 2
    late = (dy.at[half:, :], unit.at[half:, :])
    copies = piece_copies(pieces, inputs, x_all, dy, piece_sems)
    now = [copy for copy, piece in zip(copies, pieces) if piece[4] >= half]
    now.append(down_copy(w_d_in, w_d, weight_sem))
    later = [copy for copy, piece in zip(copies, pieces) if piece[0] and piece[4] < half]
    later.append(pltpu.make_async_copy(unit_in, unit.at[:half, :], first_sems.at[0]))
    later.append(pltpu.make_async_copy(acts_in, right.at[:hidden, :half], first_sems.at[1]))
    later.append(pltpu.make_async_copy(grads_in, left.at[:both, :half], first_sems.at[2]))
    for i in range(SEQ):
        rows = pl.ds(pl.multiple_of(slot_of(i) * HERE, HERE), HERE)
        to = heads.at[i * HERE : (i + 1) * HERE, :]
        later.append(pltpu.make_async_copy(heads_in.at[rows, :], to, head_sems.at[i]))
    for copy in now + later:
        copy.start()
    for copy in now:
        copy.wait()

    def keep(i, act, grad):
        at = slice(half + i * BLOCK, half + (i + 1) * BLOCK)
        right[:hidden, at] = act
        left[:both, at] = grad

    total = gate_blocks(half // BLOCK, x_all.at[half:, :], *late, w_gu, w_d, gain, bias, keep)
    total += sums[:, :1]
    for copy in later:
        copy.wait()
    heads_t = heads[...].T
    left[both:, :] = heads_t[: 3 * HEAD_DIM]
    right[hidden:, :] = heads_t[3 * HEAD_DIM :]
    total_h = jnp.sum(heads_t[: 3 * HEAD_DIM].astype(f32), 1, keepdims=True)
    inner = dot_nn(left[...], unit[...])
    total = jnp.concatenate([total, total_h], 0)
    wide = jnp.concatenate([w_gu[...], w_qkv[...]], 0).astype(f32)
    terms = inner * gain[...] + bias[...] * total
    gain_part = jnp.sum(inner * wide, 0, keepdims=True)
    bias_part = jnp.sum(wide * total, 0, keepdims=True)
    at_row = lax.broadcasted_iota(jnp.int32, (192, WIDTH), 0)
    column_at = at_row // HEAD_DIM * WIDTH + here * HEAD_DIM + at_row % HEAD_DIM
    mine = column_at // 24 * 8 == lax.broadcasted_iota(jnp.int32, (192, WIDTH), 1)
    at_lane = lax.broadcasted_iota(jnp.int32, (32, 192), 1)
    column_at = at_lane // HEAD_DIM * WIDTH + here * HEAD_DIM + at_lane % HEAD_DIM
    pick = (column_at % 24 + 2 == lax.broadcasted_iota(jnp.int32, (32, 192), 0)).astype(bf16)
    extra = dot_nn(pick, jnp.where(mine, total_h, 0.0).astype(bf16))
    row32 = lax.broadcasted_iota(jnp.int32, (32, WIDTH), 0)
    extra += jnp.where(row32 == 0, gain_part, jnp.where(row32 == 1, bias_part, 0.0))
    stage[...] = jnp.concatenate([terms[:both], extra, terms[both:]], 0).T
    products = dot_nn(right[...], dy[...])
    down_all, out_all = products[:hidden], products[hidden:]
    outs = []

    def two(s, lanes):
        first, second = (s * ROWS + r) * 8, ((s + 1) * ROWS + r) * 8
        return jnp.concatenate([stage[first : first + 8, lanes], stage[second : second + 8, lanes]], 0)

    for r in range(ROWS):
        for s in range(0, SEQ, 2):
            for i in range(4):
                lanes = slice(i * 128, (i + 1) * 128)
                block[r, i * HERE + s * 8 : i * HERE + s * 8 + 16, :] = two(s, lanes).astype(bf16)
        for s in range(0, SEQ // 2, 2):
            lanes = slice(512, 576)
            block[r, 512 + s * 8 : 528 + s * 8, :] = jnp.concatenate(
                [two(s, lanes), two(s + 8, lanes)], 1
            ).astype(bf16)
        last = jnp.concatenate(
            [out_all[r * 8 : r * 8 + 8], down_all[r * 22 : (r + 1) * 22], jnp.zeros((2, WIDTH), f32)],
            0,
        ).astype(bf16)
        for i in range(8):
            block[r, 576 + i * 32 : 608 + i * 32, :] = last[:, i * 128 : (i + 1) * 128]
        outs.append(pltpu.make_async_copy(block.at[r], block_out.at[r], out_sems.at[r]))
        outs[r].start()
    for copy in outs:
        copy.wait()


def weight_grads(arrays, pieces, heads, w_qkv, w_gu, w_d, gain, bias, first):
    big = (LENGTH, WIDTH)
    return pl.pallas_call(
        lambda *refs: weights_kernel(pieces, len(arrays), *refs),
        out_shape=jax.ShapeDtypeStruct((ROWS, 832, 128), bf16),
        in_specs=[ANY] * (len(arrays) + 1) + [VMEM] * 2 + [ANY] + [VMEM] * 2 + [ANY] * 3 + [VMEM],
        out_specs=ANY,
        scratch_shapes=[pltpu.VMEM(big, bf16)] * 3
        + [
            pltpu.VMEM((LENGTH, 4 * HEAD_DIM), bf16),
            pltpu.VMEM((2 * FF_LOCAL + 3 * HEAD_DIM, LENGTH), bf16),
            pltpu.VMEM((FF_LOCAL + HEAD_DIM, LENGTH), bf16),
            pltpu.VMEM((WIDTH, 576), f32),
            pltpu.VMEM((FF_LOCAL, WIDTH), bf16),
            pltpu.VMEM((ROWS, 832, 128), bf16),
            pltpu.SemaphoreType.DMA((len(pieces),)),
            pltpu.SemaphoreType.DMA((SEQ,)),
            pltpu.SemaphoreType.DMA((ROWS,)),
            pltpu.SemaphoreType.DMA((3,)),
            pltpu.SemaphoreType.DMA,
        ],
        compiler_params=params(60),
        cost_estimate=cost(8, 20),
        name="weight_grads",
    )(*arrays, heads, w_qkv, w_gu, w_d, gain, bias, *first)


def final_kernel(heads, x, dy, part, grad, gain, w_out, w_qkv, out, input_grad, att, rows, total):
    step = pl.program_id(0)

    @pl.when(step == 0)
    def _():
        for h in range(HEADS):
            here = heads[h * HERE : (h + 1) * HERE, :]
            at = h * HEAD_DIM
            for i in range(3):
                lo = i * WIDTH + at
                rows[:, lo : lo + HEAD_DIM] = here[:, i * HEAD_DIM : (i + 1) * HEAD_DIM]
            att[:, at : at + HEAD_DIM] = here[:, 3 * HEAD_DIM :]

    columns = pl.ds(pl.multiple_of(step * BLOCK, BLOCK), BLOCK)
    out[:, columns] = (part[:, columns] + dot_nn(att[...], w_out[...])).astype(bf16)
    total[:, columns] = grad[:, columns] + dot_nt(rows[...], w_qkv[...])

    @pl.when(step == pl.num_programs(0) - 1)
    def _():
        unit, inv_std = normalise(x[...])
        grad_unit = total[...] * gain[...]
        grad_norm = inv_std * (
            grad_unit
            - jnp.mean(grad_unit, 1, keepdims=True)
            - unit * jnp.mean(grad_unit * unit, 1, keepdims=True)
        )
        input_grad[...] = (dy[...].astype(f32) + grad_norm).astype(bf16)


def final_rows(heads, x, dy, part, grad, gain, w_out, w_qkv):
    fixed = lambda shape: pl.BlockSpec(shape, lambda j: (0,) * len(shape))
    own = fixed((HERE, WIDTH))
    return pl.pallas_call(
        final_kernel,
        grid=(WIDTH // BLOCK,),
        out_shape=[jax.ShapeDtypeStruct((HERE, WIDTH), bf16)] * 2,
        in_specs=[fixed((LENGTH, 256)), own, own, own, own, fixed((1, WIDTH))]
        + [pl.BlockSpec((WIDTH, BLOCK), lambda j: (0, j))]
        + [pl.BlockSpec((BLOCK, 3 * WIDTH), lambda j: (j, 0))],
        out_specs=[own, own],
        scratch_shapes=[
            pltpu.VMEM((HERE, WIDTH), bf16),
            pltpu.VMEM((HERE, 3 * WIDTH), bf16),
            pltpu.VMEM((HERE, WIDTH), f32),
        ],
        compiler_params=params(60),
        cost_estimate=cost(1.1, 10),
        name="final_rows",
    )(heads, x, dy, part, grad, gain, w_out, w_qkv)


def sum_kernel(got, send, down, out):
    total = got[0].astype(f32)
    for r in range(1, ROWS):
        total += got[r].astype(f32)
    for i in range(4):
        send[:, i * 128 : (i + 1) * 128] = total[i * HERE : (i + 1) * HERE].astype(bf16)
    left = jnp.concatenate([total[512:576, :64], total[512:576, 64:]], 0)
    send[:, 512:] = jnp.concatenate([left, jnp.zeros((HERE, 64), f32)], 1).astype(bf16)
    for i in range(8):
        lanes = slice(i * 128, (i + 1) * 128)
        out[:, lanes] = total[576 + i * 32 : 584 + i * 32]
        down[:, lanes] = total[584 + i * 32 : 606 + i * 32]


def sum_rows(got):
    return pl.pallas_call(
        sum_kernel,
        out_shape=[
            jax.ShapeDtypeStruct((HERE, 640), bf16),
            jax.ShapeDtypeStruct((22, WIDTH), f32),
            jax.ShapeDtypeStruct((8, WIDTH), f32),
        ],
        in_specs=[VMEM],
        out_specs=[VMEM] * 3,
        compiler_params=params(16),
        cost_estimate=cost(0.001, 2),
        name="sum_rows",
    )(got)


def layout_kernel(mine, qkv, gate, up, gain, bias, sums):
    more = jnp.zeros((8, 128), f32)
    for s in range(SEQ):
        here = mine[s * 8 : (s + 1) * 8, :].astype(f32)
        gate[:, s * FF_LOCAL : (s + 1) * FF_LOCAL] = here[:, :FF_LOCAL]
        up[:, s * FF_LOCAL : (s + 1) * FF_LOCAL] = here[:, FF_LOCAL : 2 * FF_LOCAL]
        for i in range(3):
            lo = i * WIDTH + s * HEAD_DIM
            qkv[:, lo : lo + HEAD_DIM] = here[:, 384 + i * HEAD_DIM : 384 + (i + 1) * HEAD_DIM]
        more += here[:, 256:384]
    turned = more.T
    gain[...] = turned[96:97, :]
    bias[...] = turned[97:98, :]
    sums[...] = more[0:1, 98:122]


def last_layout(mine):
    return pl.pallas_call(
        layout_kernel,
        out_shape=[
            jax.ShapeDtypeStruct((8, 3 * WIDTH), f32),
            jax.ShapeDtypeStruct((8, FF), f32),
            jax.ShapeDtypeStruct((8, FF), f32),
            jax.ShapeDtypeStruct((1, 8), f32),
            jax.ShapeDtypeStruct((1, 8), f32),
            jax.ShapeDtypeStruct((1, 24), f32),
        ],
        in_specs=[VMEM],
        out_specs=[VMEM] * 6,
        compiler_params=params(16),
        cost_estimate=cost(0.001, 1),
        name="last_layout",
    )(mine)


PLACES = [(0, 0), (0, -1), (0, 1), (1, 0), (0, 2), (1, 2), (1, 1), (1, -1)]
CORE = [(i, i ^ 1) for i in range(SEQ)]
PAIR = [(i, i ^ 2) for i in range(SEQ)]
UP = [(i, (i + 4) % SEQ) for i in range(SEQ)]
DOWN = [(i, (i + 12) % SEQ) for i in range(SEQ)]
DOWN_PAIR = [(i, (i + 12) % SEQ ^ 2) for i in range(SEQ)]


def send(value, to):
    return lax.ppermute(value, "seq", to)


def gather(x, dy, exchange, after):
    own = jnp.concatenate([x, dy], 0)
    below = send(own, UP)
    above = send(own, DOWN)
    pair = send(own, PAIR)
    late = exchange((below, above, pair))
    far = send(below, UP)
    opposite = send(above, DOWN_PAIR)
    most = pair[:MOST]
    rest = [far, opposite, send(most, DOWN), send(most, UP)]
    rest.append(send(jnp.concatenate([above[MOST:], below[MOST:]], 0), PAIR))
    first = [both for a in (own, below, above, pair) for both in (a, send(a, CORE))]
    late, rest = after(late, first, rest)
    return first, [both for a in rest for both in (a, send(a, CORE))], late


MOST = 176


def pieces_of(places):
    return [
        (which, i, which * HERE, HERE, i * HERE) for i in range(places) for which in range(2)
    ]


def pieces_late():
    pieces = pieces_of(12)
    for place in range(2):
        for core in range(2):
            to = (12 + 2 * place + core) * HERE
            first, left = 12 + 2 * place + core, 2 * HERE - MOST
            pieces.append((0, first, 0, HERE, to))
            pieces.append((1, first, HERE, MOST - HERE, to))
            pieces.append((1, 16 + core, place * left, left, to + MOST - HERE))
    return pieces


def shards(x, dy, order, ln_gain, ln_bias, w_qkv, b_qkv, w_out, w_gate, w_up, w_down):
    x, dy = x[0], dy[0]
    gain, bias = ln_gain[None, :], ln_bias[None, :]

    table = rotary_tables()
    packed = own_heads(order, x, dy, w_qkv, w_out, b_qkv[None, :], gain, bias, table)
    w_qkv_s, w_gu_s = cut_weights(w_qkv, w_gate, w_up)

    def exchange(first):
        ready, _ = lax.optimization_barrier((packed, (first, w_gu_s)))
        return lax.all_to_all(ready, "seq", 0, 0, tiled=True)

    def attend(packed_here, early, arrays):
        first = first_half(
            early, pieces_of(len(early)), w_gu_s, w_down, gain, bias
        )
        heads = attention(order, packed_here, first)
        (heads, first), arrays = lax.optimization_barrier(((heads, first), arrays))
        return (heads, first), arrays

    early, arrays, (heads, first) = gather(x, dy, exchange, attend)
    heads_here = lax.all_to_all(heads, "seq", 0, 0, tiled=True)
    arrays = early + arrays
    block = weight_grads(
        arrays, pieces_late(), heads, w_qkv_s, w_gu_s, w_down, gain, bias, first
    )
    block, heads_here = lax.optimization_barrier((block, heads_here))
    got = lax.all_to_all(block, "rows", 0, 0, tiled=True)
    x_late, _ = lax.optimization_barrier((x, heads_here))
    part, grad = own_rows(x_late, dy, gain, bias, w_gate, w_up, w_down)
    output, input_grad = final_rows(heads_here, x, dy, part, grad, gain, w_out, w_qkv)
    got, output, input_grad = lax.optimization_barrier((got, output, input_grad))
    outgoing, o_down, o_out = sum_rows(got)
    mine = lax.all_to_all(outgoing, "seq", 0, 0, tiled=True)
    o_qkv, o_gate, o_up, o_gain, o_bias, sums = last_layout(mine)
    return (
        output[None],
        input_grad[None],
        o_qkv,
        o_out,
        o_gate,
        o_up,
        o_down,
        sums[0],
        o_gain[0],
        o_bias[0],
    )


def solution(mesh):
    rows = P("rows", "seq", None)
    both = P(("seq", "rows"), None)
    flat = P(("seq", "rows"))
    return jax.shard_map(
        shards,
        mesh=mesh,
        in_specs=(rows, rows) + (P(),) * 9,
        out_specs=(rows, rows, both, both, both, both, both, flat, flat, flat),
        check_vma=False,
    )
```

```python
import jax
import jax.numpy as jnp
import numpy as np
from jax import lax
from jax.experimental import pallas as pl
from jax.experimental.pallas import tpu as pltpu
from jax.sharding import PartitionSpec as P

HEADS = 16
HEAD_DIM = 64
ROT = 16
GROUP = 64
LENGTH = 2048
WIDTH = 1024
FF = 2816
FF_LOCAL = 176
BLOCK = 256
SEQ = 16
ROWS = 8
HERE = 128
epsilon = 1e-05
f32 = jnp.float32
bf16 = jnp.bfloat16
SMEM = pl.BlockSpec(memory_space=pltpu.SMEM)
VMEM = pl.BlockSpec(memory_space=pltpu.VMEM)
ANY = pl.BlockSpec(memory_space=pl.ANY)


def dot_nn(a, b):
    return lax.dot_general(a, b, (((1,), (0,)), ((), ())), preferred_element_type=f32)


def dot_nt(a, b):
    return lax.dot_general(a, b, (((1,), (1,)), ((), ())), preferred_element_type=f32)


def dot_tn(a, b):
    return lax.dot_general(a, b, (((0,), (0,)), ((), ())), preferred_element_type=f32)


def dot_tt(a, b):
    return lax.dot_general(a, b, (((0,), (1,)), ((), ())), preferred_element_type=f32)


def params(mib):
    return pltpu.CompilerParams(vmem_limit_bytes=mib * 1024 * 1024)


def cost(gflop, mib, exps=0):
    return pl.CostEstimate(
        flops=int(gflop * 1e9), bytes_accessed=int(mib * 2**20), transcendentals=int(exps)
    )


def normalise(rows):
    rows = rows.astype(f32)
    mean = jnp.mean(rows, 1, keepdims=True)
    centred = rows - mean
    inv_std = lax.rsqrt(jnp.mean(centred * centred, 1, keepdims=True) + epsilon)
    return centred * inv_std, inv_std


def gated(gate, up, grad_act):
    sig = 1.0 / (1.0 + jnp.exp(-gate))
    silu = gate * sig
    grad_g = grad_act * up * (sig * (1.0 + gate - silu))
    grad_u = grad_act * silu
    return (silu * up).astype(bf16), grad_g.astype(bf16), grad_u.astype(bf16)


def rotary_tables():
    half = ROT // 2
    lane = np.arange(2 * HEAD_DIM) % HEAD_DIM
    frequency = np.where(lane < ROT, 10000.0 ** (-(lane % half) * (2.0 / ROT)), 0.0)
    groups = np.arange(LENGTH // GROUP)[:, None] * GROUP * frequency
    inside = np.arange(GROUP)[:, None] * frequency
    parts = (np.cos(groups), np.sin(groups), np.cos(inside), np.sin(inside))
    return jnp.asarray(np.concatenate(parts), f32)


def group_rotation(table, group):
    count = LENGTH // GROUP
    cos_g, sin_g = table[pl.ds(group, 1), :], table[pl.ds(group + count, 1), :]
    cos_i = table[2 * count : 2 * count + GROUP, :]
    sin_i = table[2 * count + GROUP :, :]
    return cos_g * cos_i - sin_g * sin_i, sin_g * cos_i + cos_g * sin_i


def own_kernel(x, dy, gain, bias, wg_in, wu_in, wd_in, out, grad, wg, wu, wd, sems):
    groups = ((0, 512), (512, 1280), (1280, 2048), (2048, 2816))
    copies = []
    for i, (lo, hi) in enumerate(groups):
        part = slice(lo, hi)
        pairs = ((wg_in.at[:, part], wg.at[:, part]), (wu_in.at[:, part], wu.at[:, part]))
        pairs += ((wd_in.at[part, :], wd.at[part, :]),)
        copies.append([pltpu.make_async_copy(*pair, sems.at[j, i]) for j, pair in enumerate(pairs)])
        for copy in copies[i]:
            copy.start()
    unit, _ = normalise(x[...])
    hid = (unit * gain[...] + bias[...]).astype(bf16)
    for i, (lo, hi) in enumerate(groups):
        for copy in copies[i]:
            copy.wait()
        part = slice(lo, hi)
        gate, up = dot_nn(hid, wg[:, part]), dot_nn(hid, wu[:, part])
        act, grad_g, grad_u = gated(gate, up, dot_nt(dy[...], wd[part, :]))
        more = dot_nt(grad_g, wg[:, part]) + dot_nt(grad_u, wu[:, part])
        out[...] = (x[...].astype(f32) if i == 0 else out[...]) + dot_nn(act, wd[part, :])
        grad[...] = more if i == 0 else grad[...] + more


def own_rows(x, dy, gain, bias, w_gate, w_up, w_down):
    return pl.pallas_call(
        own_kernel,
        out_shape=[jax.ShapeDtypeStruct((HERE, WIDTH), f32)] * 2,
        in_specs=[VMEM] * 4 + [ANY] * 3,
        out_specs=[VMEM] * 2,
        scratch_shapes=[
            pltpu.VMEM((WIDTH, FF), bf16),
            pltpu.VMEM((WIDTH, FF), bf16),
            pltpu.VMEM((FF, WIDTH), bf16),
            pltpu.SemaphoreType.DMA((3, 4)),
        ],
        compiler_params=params(60),
        cost_estimate=cost(4.5, 18),
        name="own_rows",
    )(x, dy, gain, bias, w_gate, w_up, w_down)


def heads_kernel(
    order, x, dy, w_q, w_k, w_v, w_o, b_q, b_k, b_v, gain, bias,
    table, out, hid, cosine, sine,
):
    lanes = 2 * HEAD_DIM
    lane = lax.broadcasted_iota(jnp.int32, (1, lanes), 1)
    low = lane % HEAD_DIM < ROT // 2
    scale = jnp.where(lane < HEAD_DIM, HEAD_DIM**-0.5, 1.0)

    @pl.when(pl.program_id(0) == 0)
    def _():
        unit, _ = normalise(x[...])
        hid[...] = (unit * gain[...] + bias[...]).astype(bf16)
        for g in range(HERE // GROUP):
            rows = slice(g * GROUP, (g + 1) * GROUP)
            group = order[lax.axis_index("seq") * (HERE // GROUP) + g]
            cosine[rows, :], sine[rows, :] = group_rotation(table, group)

    q = dot_nn(hid[...], w_q[...]) + b_q[...]
    k = dot_nn(hid[...], w_k[...]) + b_k[...]
    v = dot_nn(hid[...], w_v[...]) + b_v[...]
    grad_att = dot_nt(dy[...], w_o[...])
    for h in range(BLOCK // HEAD_DIM):
        part = slice(h * HEAD_DIM, (h + 1) * HEAD_DIM)
        raw = jnp.concatenate([q[:, part], k[:, part]], 1)
        before, after = pltpu.roll(raw, ROT // 2, 1), pltpu.roll(raw, lanes - ROT // 2, 1)
        turned = (raw * cosine[...] + jnp.where(low, -after, before) * sine[...]) * scale
        rows = slice(h * HERE, (h + 1) * HERE)
        out[rows, :lanes] = turned.astype(bf16)
        out[rows, lanes:] = jnp.concatenate([v[:, part], grad_att[:, part]], 1).astype(bf16)


def own_heads(order, x, dy, w_qkv, w_out, b_qkv, gain, bias, table):
    fixed = lambda shape: pl.BlockSpec(shape, lambda j: (0,) * len(shape))
    own, vector = fixed((HERE, WIDTH)), fixed((1, WIDTH))
    steps = WIDTH // BLOCK

    def part(rows, i):
        return pl.BlockSpec((rows, BLOCK), lambda j: (0, i * steps + j))

    return pl.pallas_call(
        heads_kernel,
        grid=(steps,),
        out_shape=jax.ShapeDtypeStruct((LENGTH, 4 * HEAD_DIM), bf16),
        in_specs=[SMEM]
        + [own, own, part(WIDTH, 0), part(WIDTH, 1), part(WIDTH, 2)]
        + [pl.BlockSpec((BLOCK, WIDTH), lambda j: (j, 0)), part(1, 0), part(1, 1), part(1, 2)]
        + [vector, vector, fixed(table.shape)],
        out_specs=pl.BlockSpec((4 * HERE, 4 * HEAD_DIM), lambda j: (j, 0)),
        scratch_shapes=[
            pltpu.VMEM((HERE, WIDTH), bf16),
            pltpu.VMEM((HERE, 2 * HEAD_DIM), f32),
            pltpu.VMEM((HERE, 2 * HEAD_DIM), f32),
        ],
        compiler_params=params(60),
        cost_estimate=cost(1.1, 9),
        name="own_heads",
    )(order, x, dy, w_qkv, w_qkv, w_qkv, w_out, b_qkv, b_qkv, b_qkv, gain, bias, table)


def attention_kernel(*refs):
    order, packed, table, out_ref, rows_in, cols_in, cols, turn = refs[-8:]
    groups = LENGTH // GROUP
    for g in range(groups):
        at = pl.multiple_of(order[g] * GROUP, GROUP)
        rows_in[pl.ds(at, GROUP), :] = packed[g * GROUP : (g + 1) * GROUP, :]
    cols_in[...] = rows_in[...].T
    k = rows_in[:, HEAD_DIM : 2 * HEAD_DIM]
    v = rows_in[:, 2 * HEAD_DIM : 3 * HEAD_DIM]
    q_t, k_t, v_t, do_t = (cols_in.at[i * HEAD_DIM : (i + 1) * HEAD_DIM, :] for i in range(4))
    dq_t, dk_t, dv_t, att_t = (cols.at[i * HEAD_DIM : (i + 1) * HEAD_DIM, :] for i in range(4))
    row = lax.broadcasted_iota(jnp.int32, (BLOCK, BLOCK), 0)
    col = lax.broadcasted_iota(jnp.int32, (BLOCK, BLOCK), 1)
    visible = row <= col
    def products(i):
        here, n = slice(i * BLOCK, (i + 1) * BLOCK), (i + 1) * BLOCK
        return dot_nn(k[:n], q_t[:, here]), dot_nn(v[:n], do_t[:, here])

    def softmax(i, scores):
        lo = i * BLOCK
        last = jnp.where(visible, scores[lo:], -1e30)
        scores = last if i == 0 else jnp.concatenate([scores[:lo], last], 0)
        top = jnp.max(scores, 0, keepdims=True)
        weights = jnp.exp(scores - top)
        inverse = 1.0 / jnp.sum(weights, 0, keepdims=True)
        return weights, weights.astype(bf16), inverse

    order_of = list(reversed(range(LENGTH // BLOCK)))
    ahead = products(order_of[0])
    for j, i in enumerate(order_of):
        lo, n = i * BLOCK, (i + 1) * BLOCK
        here, seen = slice(lo, n), slice(0, n)
        scores, grad_p = ahead
        if j + 1 < len(order_of):
            ahead = products(order_of[j + 1])
        weights, weights_b, inverse = softmax(i, scores)
        att = dot_nn(v_t[:, seen], weights_b) * inverse
        do_f = do_t[:, here].astype(f32)
        delta = jnp.sum(weights * grad_p, 0, keepdims=True) * inverse
        grad_s = (weights * (grad_p - delta)).astype(bf16)
        dv = dot_nt((do_f * inverse).astype(bf16), weights_b)
        att_t[:, here] = att
        dq_t[:, here] = dot_nn(k_t[:, seen], grad_s) * (inverse * HEAD_DIM**-0.5)
        dk = dot_nt((q_t[:, here].astype(f32) * inverse).astype(bf16), grad_s)
        if n == LENGTH:
            dk_t[...], dv_t[...] = dk, dv
        else:
            dk_t[:, seen] += dk
            dv_t[:, seen] += dv
    half = ROT // 2
    cosine, sine = table[:half, :], table[half:, :]
    for part in (dq_t, dk_t):
        first, second = part[:half, :], part[half:ROT, :]
        part[:half, :] = first * cosine + second * sine
        part[half:ROT, :] = second * cosine - first * sine
    turn[...] = cols[...].T.astype(bf16)
    for g in range(groups):
        at = pl.multiple_of(order[g] * GROUP, GROUP)
        out_ref[g * GROUP : (g + 1) * GROUP, :] = turn[pl.ds(at, GROUP), :]


def position_table():
    half = ROT // 2
    angles = 10000.0 ** (-np.arange(half)[:, None] * (2.0 / ROT)) * np.arange(LENGTH)
    return jnp.asarray(np.concatenate([np.cos(angles), np.sin(angles)]), f32)


def attention(order, packed, first=()):
    size = 4 * HEAD_DIM
    return pl.pallas_call(
        attention_kernel,
        out_shape=jax.ShapeDtypeStruct((LENGTH, size), bf16),
        in_specs=[ANY] * len(first) + [SMEM] + [VMEM] * 2,
        out_specs=VMEM,
        scratch_shapes=[
            pltpu.VMEM((LENGTH, size), bf16),
            pltpu.VMEM((size, LENGTH), bf16),
            pltpu.VMEM((size, LENGTH), f32),
            pltpu.VMEM((LENGTH, size), bf16),
        ],
        compiler_params=params(60),
        cost_estimate=cost(15, 8, LENGTH * LENGTH // 2),
        name="attention",
    )(*first, order, packed, position_table())


def cut_kernel(w_qkv, w_gate, w_up, out_qkv, out_gu, wide_qkv, wide_gu, sems):
    here = lax.axis_index("seq")
    first = here * FF_LOCAL
    tile = jnp.minimum(first // 128, (FF - 384) // 128) * 128
    copies = []
    for i in range(3):
        lanes = pl.ds(pl.multiple_of(here // 2 * 128 + i * WIDTH, 128), 128)
        to = wide_qkv.at[:, i * 128 : (i + 1) * 128]
        copies.append(pltpu.make_async_copy(w_qkv.at[:, lanes], to, sems.at[i]))
    for i, source in enumerate((w_gate, w_up)):
        lanes = pl.ds(pl.multiple_of(tile, 128), 384)
        copies.append(pltpu.make_async_copy(source.at[:, lanes], wide_gu.at[i], sems.at[3 + i]))
    for copy in copies:
        copy.start()
    row = lax.broadcasted_iota(jnp.int32, (384, 256), 0)
    lane = lax.broadcasted_iota(jnp.int32, (384, 256), 1)
    source = lane // HEAD_DIM * 128 + here % 2 * HEAD_DIM + lane % HEAD_DIM
    pick_qkv = (row == source).astype(bf16)[:, : 3 * HEAD_DIM]
    pick_gu = (row == lane + (first - tile)).astype(bf16)[:, :FF_LOCAL]
    for copy in copies:
        copy.wait()
    out_qkv[...] = dot_tt(pick_qkv, wide_qkv[...]).astype(bf16)
    out_gu[:FF_LOCAL, :] = dot_tt(pick_gu, wide_gu[0]).astype(bf16)
    out_gu[FF_LOCAL:, :] = dot_tt(pick_gu, wide_gu[1]).astype(bf16)


def cut_weights(w_qkv, w_gate, w_up):
    return pl.pallas_call(
        cut_kernel,
        out_shape=[
            jax.ShapeDtypeStruct((3 * HEAD_DIM, WIDTH), bf16),
            jax.ShapeDtypeStruct((2 * FF_LOCAL, WIDTH), bf16),
        ],
        in_specs=[ANY] * 3,
        out_specs=[VMEM] * 2,
        scratch_shapes=[
            pltpu.VMEM((WIDTH, 384), bf16),
            pltpu.VMEM((2, WIDTH, 384), bf16),
            pltpu.SemaphoreType.DMA((5,)),
        ],
        compiler_params=params(60),
        cost_estimate=cost(0.001, 0.001),
        name="cut_weights",
    )(w_qkv, w_gate, w_up)


def column(row):
    return jnp.broadcast_to(row, (8, row.shape[1])).T[:, :1]


def slot_of(i):
    here = lax.axis_index("seq")
    across, up = PLACES[i // 2]
    y = lax.rem(lax.div(here, 4) + (4 + up), 4)
    x = lax.rem(lax.div(here, 2) + across, 2)
    return y * 4 + x * 2 + lax.rem(here + i % 2, 2)


def piece_copies(pieces, inputs, x_all, dy, sems):
    return [
        pltpu.make_async_copy(
            inputs[ref].at[pl.ds(at, rows), :],
            (x_all, dy)[which].at[pl.ds(to, rows), :],
            sems.at[i],
        )
        for i, (which, ref, at, rows, to) in enumerate(pieces)
    ]


def down_copy(source, to, sem):
    rows = pl.ds(pl.multiple_of(lax.axis_index("seq") * FF_LOCAL, 16), FF_LOCAL)
    return pltpu.make_async_copy(source.at[rows, :], to, sem)


def gate_blocks(count, x_all, dy, unit, w_gu, w_d, gain, bias, keep):
    total = 0.0
    for i in range(count):
        rows = slice(i * BLOCK, (i + 1) * BLOCK)
        unit_f, _ = normalise(x_all[rows, :])
        hid = (unit_f * gain[...] + bias[...]).astype(bf16)
        unit[rows, :] = unit_f.astype(bf16)
        gu = dot_nt(w_gu[...], hid)
        act, grad_g, grad_u = gated(gu[:FF_LOCAL], gu[FF_LOCAL:], dot_nt(w_d[...], dy[rows, :]))
        grads = jnp.concatenate([grad_g, grad_u], 0)
        keep(i, act, grads)
        total += jnp.sum(grads.astype(f32), 1, keepdims=True)
    return total


def first_kernel(pieces, n_refs, *refs):
    inputs, refs = refs[:n_refs], refs[n_refs:]
    w_gu, w_d_in, gain, bias, unit, acts, grads, sums, x_all, dy, w_d, sems, sem = refs
    copies = piece_copies(pieces, inputs, x_all, dy, sems)
    copies.append(down_copy(w_d_in, w_d, sem))
    for copy in copies:
        copy.start()
    for copy in copies:
        copy.wait()

    def keep(i, act, grad):
        acts[:, i * BLOCK : (i + 1) * BLOCK] = act
        grads[:, i * BLOCK : (i + 1) * BLOCK] = grad

    total = gate_blocks(x_all.shape[0] // BLOCK, x_all, dy, unit, w_gu, w_d, gain, bias, keep)
    sums[...] = jnp.broadcast_to(total, sums.shape)


def first_half(arrays, pieces, w_gu, w_d, gain, bias):
    half = LENGTH // 2
    return pl.pallas_call(
        lambda *refs: first_kernel(pieces, len(arrays), *refs),
        out_shape=[
            jax.ShapeDtypeStruct((half, WIDTH), bf16),
            jax.ShapeDtypeStruct((FF_LOCAL, half), bf16),
            jax.ShapeDtypeStruct((2 * FF_LOCAL, half), bf16),
            jax.ShapeDtypeStruct((2 * FF_LOCAL, 128), f32),
        ],
        in_specs=[ANY] * len(arrays) + [VMEM] + [ANY] + [VMEM] * 2,
        out_specs=[VMEM] * 4,
        scratch_shapes=[
            pltpu.VMEM((half, WIDTH), bf16),
            pltpu.VMEM((half, WIDTH), bf16),
            pltpu.VMEM((FF_LOCAL, WIDTH), bf16),
            pltpu.SemaphoreType.DMA((len(pieces),)),
            pltpu.SemaphoreType.DMA,
        ],
        compiler_params=params(60),
        cost_estimate=cost(0.001, 0.001),
        name="first_half",
    )(*arrays, w_gu, w_d, gain, bias)


def weights_kernel(pieces, n_refs, *refs):
    inputs, refs = refs[:n_refs], refs[n_refs:]
    heads_in, w_qkv, w_gu, w_d_in, gain, bias = refs[:6]
    unit_in, acts_in, grads_in, sums, block_out = refs[6:11]
    x_all, dy, unit, heads, left, right, stage, w_d, block = refs[11:20]
    piece_sems, head_sems, out_sems, first_sems, weight_sem = refs[20:]
    hidden, both = FF_LOCAL, 2 * FF_LOCAL
    here = lax.axis_index("seq")
    half = LENGTH // 2
    late = (dy.at[half:, :], unit.at[half:, :])
    copies = piece_copies(pieces, inputs, x_all, dy, piece_sems)
    now = [copy for copy, piece in zip(copies, pieces) if piece[4] >= half]
    now.append(down_copy(w_d_in, w_d, weight_sem))
    later = [copy for copy, piece in zip(copies, pieces) if piece[0] and piece[4] < half]
    later.append(pltpu.make_async_copy(unit_in, unit.at[:half, :], first_sems.at[0]))
    later.append(pltpu.make_async_copy(acts_in, right.at[:hidden, :half], first_sems.at[1]))
    later.append(pltpu.make_async_copy(grads_in, left.at[:both, :half], first_sems.at[2]))
    for i in range(SEQ):
        rows = pl.ds(pl.multiple_of(slot_of(i) * HERE, HERE), HERE)
        to = heads.at[i * HERE : (i + 1) * HERE, :]
        later.append(pltpu.make_async_copy(heads_in.at[rows, :], to, head_sems.at[i]))
    for copy in now + later:
        copy.start()
    for copy in now:
        copy.wait()

    def keep(i, act, grad):
        at = slice(half + i * BLOCK, half + (i + 1) * BLOCK)
        right[:hidden, at] = act
        left[:both, at] = grad

    total = gate_blocks(half // BLOCK, x_all.at[half:, :], *late, w_gu, w_d, gain, bias, keep)
    total += sums[:, :1]
    for copy in later:
        copy.wait()
    heads_t = heads[...].T
    left[both:, :] = heads_t[: 3 * HEAD_DIM]
    right[hidden:, :] = heads_t[3 * HEAD_DIM :]
    total_h = jnp.sum(heads_t[: 3 * HEAD_DIM].astype(f32), 1, keepdims=True)
    inner = dot_nn(left[...], unit[...])
    total = jnp.concatenate([total, total_h], 0)
    wide = jnp.concatenate([w_gu[...], w_qkv[...]], 0).astype(f32)
    terms = inner * gain[...] + bias[...] * total
    gain_part = jnp.sum(inner * wide, 0, keepdims=True)
    bias_part = jnp.sum(wide * total, 0, keepdims=True)
    at_row = lax.broadcasted_iota(jnp.int32, (192, WIDTH), 0)
    column_at = at_row // HEAD_DIM * WIDTH + here * HEAD_DIM + at_row % HEAD_DIM
    mine = column_at // 24 * 8 == lax.broadcasted_iota(jnp.int32, (192, WIDTH), 1)
    at_lane = lax.broadcasted_iota(jnp.int32, (32, 192), 1)
    column_at = at_lane // HEAD_DIM * WIDTH + here * HEAD_DIM + at_lane % HEAD_DIM
    pick = (column_at % 24 + 2 == lax.broadcasted_iota(jnp.int32, (32, 192), 0)).astype(bf16)
    extra = dot_nn(pick, jnp.where(mine, total_h, 0.0).astype(bf16))
    row32 = lax.broadcasted_iota(jnp.int32, (32, WIDTH), 0)
    extra += jnp.where(row32 == 0, gain_part, jnp.where(row32 == 1, bias_part, 0.0))
    stage[...] = jnp.concatenate([terms[:both], extra, terms[both:]], 0).T
    products = dot_nn(right[...], dy[...])
    down_all, out_all = products[:hidden], products[hidden:]
    outs = []

    def two(s, lanes):
        first, second = (s * ROWS + r) * 8, ((s + 1) * ROWS + r) * 8
        return jnp.concatenate([stage[first : first + 8, lanes], stage[second : second + 8, lanes]], 0)

    for r in range(ROWS):
        for s in range(0, SEQ, 2):
            for i in range(4):
                lanes = slice(i * 128, (i + 1) * 128)
                block[r, i * HERE + s * 8 : i * HERE + s * 8 + 16, :] = two(s, lanes).astype(bf16)
        for s in range(0, SEQ // 2, 2):
            lanes = slice(512, 576)
            block[r, 512 + s * 8 : 528 + s * 8, :] = jnp.concatenate(
                [two(s, lanes), two(s + 8, lanes)], 1
            ).astype(bf16)
        last = jnp.concatenate(
            [out_all[r * 8 : r * 8 + 8], down_all[r * 22 : (r + 1) * 22], jnp.zeros((2, WIDTH), f32)],
            0,
        ).astype(bf16)
        for i in range(8):
            block[r, 576 + i * 32 : 608 + i * 32, :] = last[:, i * 128 : (i + 1) * 128]
        outs.append(pltpu.make_async_copy(block.at[r], block_out.at[r], out_sems.at[r]))
        outs[r].start()
    for copy in outs:
        copy.wait()


def weight_grads(arrays, pieces, heads, w_qkv, w_gu, w_d, gain, bias, first):
    big = (LENGTH, WIDTH)
    return pl.pallas_call(
        lambda *refs: weights_kernel(pieces, len(arrays), *refs),
        out_shape=jax.ShapeDtypeStruct((ROWS, 832, 128), bf16),
        in_specs=[ANY] * (len(arrays) + 1) + [VMEM] * 2 + [ANY] + [VMEM] * 2 + [ANY] * 3 + [VMEM],
        out_specs=ANY,
        scratch_shapes=[pltpu.VMEM(big, bf16)] * 3
        + [
            pltpu.VMEM((LENGTH, 4 * HEAD_DIM), bf16),
            pltpu.VMEM((2 * FF_LOCAL + 3 * HEAD_DIM, LENGTH), bf16),
            pltpu.VMEM((FF_LOCAL + HEAD_DIM, LENGTH), bf16),
            pltpu.VMEM((WIDTH, 576), f32),
            pltpu.VMEM((FF_LOCAL, WIDTH), bf16),
            pltpu.VMEM((ROWS, 832, 128), bf16),
            pltpu.SemaphoreType.DMA((len(pieces),)),
            pltpu.SemaphoreType.DMA((SEQ,)),
            pltpu.SemaphoreType.DMA((ROWS,)),
            pltpu.SemaphoreType.DMA((3,)),
            pltpu.SemaphoreType.DMA,
        ],
        compiler_params=params(60),
        cost_estimate=cost(8, 20),
        name="weight_grads",
    )(*arrays, heads, w_qkv, w_gu, w_d, gain, bias, *first)


def final_kernel(heads, x, dy, part, grad, gain, w_out, w_qkv, out, input_grad, att, rows, total):
    step = pl.program_id(0)

    @pl.when(step == 0)
    def _():
        for h in range(HEADS):
            here = heads[h * HERE : (h + 1) * HERE, :]
            at = h * HEAD_DIM
            for i in range(3):
                lo = i * WIDTH + at
                rows[:, lo : lo + HEAD_DIM] = here[:, i * HEAD_DIM : (i + 1) * HEAD_DIM]
            att[:, at : at + HEAD_DIM] = here[:, 3 * HEAD_DIM :]

    columns = pl.ds(pl.multiple_of(step * BLOCK, BLOCK), BLOCK)
    out[:, columns] = (part[:, columns] + dot_nn(att[...], w_out[...])).astype(bf16)
    total[:, columns] = grad[:, columns] + dot_nt(rows[...], w_qkv[...])

    @pl.when(step == pl.num_programs(0) - 1)
    def _():
        unit, inv_std = normalise(x[...])
        grad_unit = total[...] * gain[...]
        grad_norm = inv_std * (
            grad_unit
            - jnp.mean(grad_unit, 1, keepdims=True)
            - unit * jnp.mean(grad_unit * unit, 1, keepdims=True)
        )
        input_grad[...] = (dy[...].astype(f32) + grad_norm).astype(bf16)


def final_rows(heads, x, dy, part, grad, gain, w_out, w_qkv):
    fixed = lambda shape: pl.BlockSpec(shape, lambda j: (0,) * len(shape))
    own = fixed((HERE, WIDTH))
    return pl.pallas_call(
        final_kernel,
        grid=(WIDTH // BLOCK,),
        out_shape=[jax.ShapeDtypeStruct((HERE, WIDTH), bf16)] * 2,
        in_specs=[fixed((LENGTH, 256)), own, own, own, own, fixed((1, WIDTH))]
        + [pl.BlockSpec((WIDTH, BLOCK), lambda j: (0, j))]
        + [pl.BlockSpec((BLOCK, 3 * WIDTH), lambda j: (j, 0))],
        out_specs=[own, own],
        scratch_shapes=[
            pltpu.VMEM((HERE, WIDTH), bf16),
            pltpu.VMEM((HERE, 3 * WIDTH), bf16),
            pltpu.VMEM((HERE, WIDTH), f32),
        ],
        compiler_params=params(60),
        cost_estimate=cost(1.1, 10),
        name="final_rows",
    )(heads, x, dy, part, grad, gain, w_out, w_qkv)


def sum_kernel(got, send, down, out):
    total = got[0].astype(f32)
    for r in range(1, ROWS):
        total += got[r].astype(f32)
    for i in range(4):
        send[:, i * 128 : (i + 1) * 128] = total[i * HERE : (i + 1) * HERE].astype(bf16)
    left = jnp.concatenate([total[512:576, :64], total[512:576, 64:]], 0)
    send[:, 512:] = jnp.concatenate([left, jnp.zeros((HERE, 64), f32)], 1).astype(bf16)
    for i in range(8):
        lanes = slice(i * 128, (i + 1) * 128)
        out[:, lanes] = total[576 + i * 32 : 584 + i * 32]
        down[:, lanes] = total[584 + i * 32 : 606 + i * 32]


def sum_rows(got):
    return pl.pallas_call(
        sum_kernel,
        out_shape=[
            jax.ShapeDtypeStruct((HERE, 640), bf16),
            jax.ShapeDtypeStruct((22, WIDTH), f32),
            jax.ShapeDtypeStruct((8, WIDTH), f32),
        ],
        in_specs=[VMEM],
        out_specs=[VMEM] * 3,
        compiler_params=params(16),
        cost_estimate=cost(0.001, 2),
        name="sum_rows",
    )(got)


def layout_kernel(mine, qkv, gate, up, gain, bias, sums):
    more = jnp.zeros((8, 128), f32)
    for s in range(SEQ):
        here = mine[s * 8 : (s + 1) * 8, :].astype(f32)
        gate[:, s * FF_LOCAL : (s + 1) * FF_LOCAL] = here[:, :FF_LOCAL]
        up[:, s * FF_LOCAL : (s + 1) * FF_LOCAL] = here[:, FF_LOCAL : 2 * FF_LOCAL]
        for i in range(3):
            lo = i * WIDTH + s * HEAD_DIM
            qkv[:, lo : lo + HEAD_DIM] = here[:, 384 + i * HEAD_DIM : 384 + (i + 1) * HEAD_DIM]
        more += here[:, 256:384]
    turned = more.T
    gain[...] = turned[96:97, :]
    bias[...] = turned[97:98, :]
    sums[...] = more[0:1, 98:122]


def last_layout(mine):
    return pl.pallas_call(
        layout_kernel,
        out_shape=[
            jax.ShapeDtypeStruct((8, 3 * WIDTH), f32),
            jax.ShapeDtypeStruct((8, FF), f32),
            jax.ShapeDtypeStruct((8, FF), f32),
            jax.ShapeDtypeStruct((1, 8), f32),
            jax.ShapeDtypeStruct((1, 8), f32),
            jax.ShapeDtypeStruct((1, 24), f32),
        ],
        in_specs=[VMEM],
        out_specs=[VMEM] * 6,
        compiler_params=params(16),
        cost_estimate=cost(0.001, 1),
        name="last_layout",
    )(mine)


PLACES = [(0, 0), (0, -1), (0, 1), (1, 0), (0, 2), (1, 2), (1, 1), (1, -1)]
CORE = [(i, i ^ 1) for i in range(SEQ)]
PAIR = [(i, i ^ 2) for i in range(SEQ)]
UP = [(i, (i + 4) % SEQ) for i in range(SEQ)]
DOWN = [(i, (i + 12) % SEQ) for i in range(SEQ)]
DOWN_PAIR = [(i, (i + 12) % SEQ ^ 2) for i in range(SEQ)]


def send(value, to):
    return lax.ppermute(value, "seq", to)


def gather(x, dy, exchange, after):
    own = jnp.concatenate([x, dy], 0)
    below = send(own, UP)
    above = send(own, DOWN)
    pair = send(own, PAIR)
    late = exchange(below)
    far = send(below, UP)
    opposite = send(above, DOWN_PAIR)
    most = pair[:MOST]
    rest = [far, opposite, send(most, DOWN), send(most, UP)]
    rest.append(send(jnp.concatenate([above[MOST:], below[MOST:]], 0), PAIR))
    first = [both for a in (own, below, above, pair) for both in (a, send(a, CORE))]
    late, rest = after(late, first, rest)
    return first, [both for a in rest for both in (a, send(a, CORE))], late


MOST = 176


def pieces_of(places):
    return [
        (which, i, which * HERE, HERE, i * HERE) for i in range(places) for which in range(2)
    ]


def pieces_late():
    pieces = pieces_of(12)
    for place in range(2):
        for core in range(2):
            to = (12 + 2 * place + core) * HERE
            first, left = 12 + 2 * place + core, 2 * HERE - MOST
            pieces.append((0, first, 0, HERE, to))
            pieces.append((1, first, HERE, MOST - HERE, to))
            pieces.append((1, 16 + core, place * left, left, to + MOST - HERE))
    return pieces


def shards(x, dy, order, ln_gain, ln_bias, w_qkv, b_qkv, w_out, w_gate, w_up, w_down):
    x, dy = x[0], dy[0]
    gain, bias = ln_gain[None, :], ln_bias[None, :]

    table = rotary_tables()
    packed = own_heads(order, x, dy, w_qkv, w_out, b_qkv[None, :], gain, bias, table)
    w_qkv_s, w_gu_s = cut_weights(w_qkv, w_gate, w_up)

    def exchange(first):
        ready, _ = lax.optimization_barrier((packed, first))
        return lax.all_to_all(ready, "seq", 0, 0, tiled=True)

    def attend(packed_here, early, arrays):
        first = first_half(
            early, pieces_of(len(early)), w_gu_s, w_down, gain, bias
        )
        heads = attention(order, packed_here, first)
        return (heads, first), [lax.optimization_barrier((heads, a))[1] for a in arrays]

    early, arrays, (heads, first) = gather(x, dy, exchange, attend)
    heads_here = lax.all_to_all(heads, "seq", 0, 0, tiled=True)
    arrays = early + arrays
    block = weight_grads(
        arrays, pieces_late(), heads, w_qkv_s, w_gu_s, w_down, gain, bias, first
    )
    block, heads_here = lax.optimization_barrier((block, heads_here))
    got = lax.all_to_all(block, "rows", 0, 0, tiled=True)
    x_late, _ = lax.optimization_barrier((x, heads_here))
    part, grad = own_rows(x_late, dy, gain, bias, w_gate, w_up, w_down)
    output, input_grad = final_rows(heads_here, x, dy, part, grad, gain, w_out, w_qkv)
    got, output, input_grad = lax.optimization_barrier((got, output, input_grad))
    outgoing, o_down, o_out = sum_rows(got)
    mine = lax.all_to_all(outgoing, "seq", 0, 0, tiled=True)
    o_qkv, o_gate, o_up, o_gain, o_bias, sums = last_layout(mine)
    return (
        output[None],
        input_grad[None],
        o_qkv,
        o_out,
        o_gate,
        o_up,
        o_down,
        sums[0],
        o_gain[0],
        o_bias[0],
    )


def solution(mesh):
    rows = P("rows", "seq", None)
    both = P(("seq", "rows"), None)
    flat = P(("seq", "rows"))
    return jax.shard_map(
        shards,
        mesh=mesh,
        in_specs=(rows, rows) + (P(),) * 9,
        out_specs=(rows, rows, both, both, both, both, both, flat, flat, flat),
        check_vma=False,
    )
```

```python
import jax
import jax.numpy as jnp
import numpy as np
from jax import lax
from jax.experimental import pallas as pl
from jax.experimental.pallas import tpu as pltpu
from jax.sharding import PartitionSpec as P

HEADS = 16
HEAD_DIM = 64
ROT = 16
GROUP = 64
LENGTH = 2048
WIDTH = 1024
FF = 2816
FF_LOCAL = 176
BLOCK = 256
SEQ = 16
ROWS = 8
HERE = 128
epsilon = 1e-05
f32 = jnp.float32
bf16 = jnp.bfloat16
SMEM = pl.BlockSpec(memory_space=pltpu.SMEM)
VMEM = pl.BlockSpec(memory_space=pltpu.VMEM)
ANY = pl.BlockSpec(memory_space=pl.ANY)


def dot_nn(a, b):
    return lax.dot_general(a, b, (((1,), (0,)), ((), ())), preferred_element_type=f32)


def dot_nt(a, b):
    return lax.dot_general(a, b, (((1,), (1,)), ((), ())), preferred_element_type=f32)


def dot_tn(a, b):
    return lax.dot_general(a, b, (((0,), (0,)), ((), ())), preferred_element_type=f32)


def dot_tt(a, b):
    return lax.dot_general(a, b, (((0,), (1,)), ((), ())), preferred_element_type=f32)


def params(mib):
    return pltpu.CompilerParams(vmem_limit_bytes=mib * 1024 * 1024)


def cost(gflop, mib, exps=0):
    return pl.CostEstimate(
        flops=int(gflop * 1e9), bytes_accessed=int(mib * 2**20), transcendentals=int(exps)
    )


def normalise(rows):
    rows = rows.astype(f32)
    mean = jnp.mean(rows, 1, keepdims=True)
    centred = rows - mean
    inv_std = lax.rsqrt(jnp.mean(centred * centred, 1, keepdims=True) + epsilon)
    return centred * inv_std, inv_std


def gated(gate, up, grad_act):
    sig = 1.0 / (1.0 + jnp.exp(-gate))
    silu = gate * sig
    grad_g = grad_act * up * (sig * (1.0 + gate - silu))
    grad_u = grad_act * silu
    return (silu * up).astype(bf16), grad_g.astype(bf16), grad_u.astype(bf16)


def rotary_tables():
    half = ROT // 2
    lane = np.arange(2 * HEAD_DIM) % HEAD_DIM
    frequency = np.where(lane < ROT, 10000.0 ** (-(lane % half) * (2.0 / ROT)), 0.0)
    groups = np.arange(LENGTH // GROUP)[:, None] * GROUP * frequency
    inside = np.arange(GROUP)[:, None] * frequency
    parts = (np.cos(groups), np.sin(groups), np.cos(inside), np.sin(inside))
    return jnp.asarray(np.concatenate(parts), f32)


def group_rotation(table, group):
    count = LENGTH // GROUP
    cos_g, sin_g = table[pl.ds(group, 1), :], table[pl.ds(group + count, 1), :]
    cos_i = table[2 * count : 2 * count + GROUP, :]
    sin_i = table[2 * count + GROUP :, :]
    return cos_g * cos_i - sin_g * sin_i, sin_g * cos_i + cos_g * sin_i


def own_kernel(x, dy, gain, bias, wg_in, wu_in, wd_in, out, grad, wg, wu, wd, sems):
    groups = ((0, 512), (512, 1280), (1280, 2048), (2048, 2816))
    copies = []
    for i, (lo, hi) in enumerate(groups):
        part = slice(lo, hi)
        pairs = ((wg_in.at[:, part], wg.at[:, part]), (wu_in.at[:, part], wu.at[:, part]))
        pairs += ((wd_in.at[part, :], wd.at[part, :]),)
        copies.append([pltpu.make_async_copy(*pair, sems.at[j, i]) for j, pair in enumerate(pairs)])
        for copy in copies[i]:
            copy.start()
    unit, _ = normalise(x[...])
    hid = (unit * gain[...] + bias[...]).astype(bf16)
    for i, (lo, hi) in enumerate(groups):
        for copy in copies[i]:
            copy.wait()
        part = slice(lo, hi)
        gate, up = dot_nn(hid, wg[:, part]), dot_nn(hid, wu[:, part])
        act, grad_g, grad_u = gated(gate, up, dot_nt(dy[...], wd[part, :]))
        more = dot_nt(grad_g, wg[:, part]) + dot_nt(grad_u, wu[:, part])
        out[...] = (x[...].astype(f32) if i == 0 else out[...]) + dot_nn(act, wd[part, :])
        grad[...] = more if i == 0 else grad[...] + more


def own_rows(x, dy, gain, bias, w_gate, w_up, w_down):
    return pl.pallas_call(
        own_kernel,
        out_shape=[jax.ShapeDtypeStruct((HERE, WIDTH), f32)] * 2,
        in_specs=[VMEM] * 4 + [ANY] * 3,
        out_specs=[VMEM] * 2,
        scratch_shapes=[
            pltpu.VMEM((WIDTH, FF), bf16),
            pltpu.VMEM((WIDTH, FF), bf16),
            pltpu.VMEM((FF, WIDTH), bf16),
            pltpu.SemaphoreType.DMA((3, 4)),
        ],
        compiler_params=params(60),
        cost_estimate=cost(4.5, 18),
        name="own_rows",
    )(x, dy, gain, bias, w_gate, w_up, w_down)


def heads_kernel(
    order, x, dy, w_q, w_k, w_v, w_o, b_q, b_k, b_v, gain, bias,
    table, out, hid, cosine, sine,
):
    lanes = 2 * HEAD_DIM
    lane = lax.broadcasted_iota(jnp.int32, (1, lanes), 1)
    low = lane % HEAD_DIM < ROT // 2
    scale = jnp.where(lane < HEAD_DIM, HEAD_DIM**-0.5, 1.0)

    @pl.when(pl.program_id(0) == 0)
    def _():
        unit, _ = normalise(x[...])
        hid[...] = (unit * gain[...] + bias[...]).astype(bf16)
        for g in range(HERE // GROUP):
            rows = slice(g * GROUP, (g + 1) * GROUP)
            group = order[lax.axis_index("seq") * (HERE // GROUP) + g]
            cosine[rows, :], sine[rows, :] = group_rotation(table, group)

    q = dot_nn(hid[...], w_q[...]) + b_q[...]
    k = dot_nn(hid[...], w_k[...]) + b_k[...]
    v = dot_nn(hid[...], w_v[...]) + b_v[...]
    grad_att = dot_nt(dy[...], w_o[...])
    for h in range(BLOCK // HEAD_DIM):
        part = slice(h * HEAD_DIM, (h + 1) * HEAD_DIM)
        raw = jnp.concatenate([q[:, part], k[:, part]], 1)
        before, after = pltpu.roll(raw, ROT // 2, 1), pltpu.roll(raw, lanes - ROT // 2, 1)
        turned = (raw * cosine[...] + jnp.where(low, -after, before) * sine[...]) * scale
        rows = slice(h * HERE, (h + 1) * HERE)
        out[rows, :lanes] = turned.astype(bf16)
        out[rows, lanes:] = jnp.concatenate([v[:, part], grad_att[:, part]], 1).astype(bf16)


def own_heads(order, x, dy, w_qkv, w_out, b_qkv, gain, bias, table):
    fixed = lambda shape: pl.BlockSpec(shape, lambda j: (0,) * len(shape))
    own, vector = fixed((HERE, WIDTH)), fixed((1, WIDTH))
    steps = WIDTH // BLOCK

    def part(rows, i):
        return pl.BlockSpec((rows, BLOCK), lambda j: (0, i * steps + j))

    return pl.pallas_call(
        heads_kernel,
        grid=(steps,),
        out_shape=jax.ShapeDtypeStruct((LENGTH, 4 * HEAD_DIM), bf16),
        in_specs=[SMEM]
        + [own, own, part(WIDTH, 0), part(WIDTH, 1), part(WIDTH, 2)]
        + [pl.BlockSpec((BLOCK, WIDTH), lambda j: (j, 0)), part(1, 0), part(1, 1), part(1, 2)]
        + [vector, vector, fixed(table.shape)],
        out_specs=pl.BlockSpec((4 * HERE, 4 * HEAD_DIM), lambda j: (j, 0)),
        scratch_shapes=[
            pltpu.VMEM((HERE, WIDTH), bf16),
            pltpu.VMEM((HERE, 2 * HEAD_DIM), f32),
            pltpu.VMEM((HERE, 2 * HEAD_DIM), f32),
        ],
        compiler_params=params(60),
        cost_estimate=cost(1.1, 9),
        name="own_heads",
    )(order, x, dy, w_qkv, w_qkv, w_qkv, w_out, b_qkv, b_qkv, b_qkv, gain, bias, table)


def attention_kernel(*refs):
    order, packed, table, out_ref, rows_in, cols_in, cols, turn = refs[-8:]
    groups = LENGTH // GROUP
    for g in range(groups):
        at = pl.multiple_of(order[g] * GROUP, GROUP)
        rows_in[pl.ds(at, GROUP), :] = packed[g * GROUP : (g + 1) * GROUP, :]
    cols_in[...] = rows_in[...].T
    k = rows_in[:, HEAD_DIM : 2 * HEAD_DIM]
    v = rows_in[:, 2 * HEAD_DIM : 3 * HEAD_DIM]
    q_t, k_t, v_t, do_t = (cols_in.at[i * HEAD_DIM : (i + 1) * HEAD_DIM, :] for i in range(4))
    dq_t, dk_t, dv_t, att_t = (cols.at[i * HEAD_DIM : (i + 1) * HEAD_DIM, :] for i in range(4))
    row = lax.broadcasted_iota(jnp.int32, (BLOCK, BLOCK), 0)
    col = lax.broadcasted_iota(jnp.int32, (BLOCK, BLOCK), 1)
    visible = row <= col
    def products(i):
        here, n = slice(i * BLOCK, (i + 1) * BLOCK), (i + 1) * BLOCK
        return dot_nn(k[:n], q_t[:, here]), dot_nn(v[:n], do_t[:, here])

    def softmax(i, scores):
        lo = i * BLOCK
        last = jnp.where(visible, scores[lo:], -1e30)
        scores = last if i == 0 else jnp.concatenate([scores[:lo], last], 0)
        top = jnp.max(scores, 0, keepdims=True)
        weights = jnp.exp(scores - top)
        inverse = 1.0 / jnp.sum(weights, 0, keepdims=True)
        return weights, weights.astype(bf16), inverse

    order_of = list(reversed(range(LENGTH // BLOCK)))
    ahead = products(order_of[0])
    for j, i in enumerate(order_of):
        lo, n = i * BLOCK, (i + 1) * BLOCK
        here, seen = slice(lo, n), slice(0, n)
        scores, grad_p = ahead
        if j + 1 < len(order_of):
            ahead = products(order_of[j + 1])
        weights, weights_b, inverse = softmax(i, scores)
        att = dot_nn(v_t[:, seen], weights_b) * inverse
        do_f = do_t[:, here].astype(f32)
        delta = jnp.sum(weights * grad_p, 0, keepdims=True) * inverse
        grad_s = (weights * (grad_p - delta)).astype(bf16)
        dv = dot_nt((do_f * inverse).astype(bf16), weights_b)
        att_t[:, here] = att
        dq_t[:, here] = dot_nn(k_t[:, seen], grad_s) * (inverse * HEAD_DIM**-0.5)
        dk = dot_nt((q_t[:, here].astype(f32) * inverse).astype(bf16), grad_s)
        if n == LENGTH:
            dk_t[...], dv_t[...] = dk, dv
        else:
            dk_t[:, seen] += dk
            dv_t[:, seen] += dv
    half = ROT // 2
    cosine, sine = table[:half, :], table[half:, :]
    for part in (dq_t, dk_t):
        first, second = part[:half, :], part[half:ROT, :]
        part[:half, :] = first * cosine + second * sine
        part[half:ROT, :] = second * cosine - first * sine
    turn[...] = cols[...].T.astype(bf16)
    for g in range(groups):
        at = pl.multiple_of(order[g] * GROUP, GROUP)
        out_ref[g * GROUP : (g + 1) * GROUP, :] = turn[pl.ds(at, GROUP), :]


def position_table():
    half = ROT // 2
    angles = 10000.0 ** (-np.arange(half)[:, None] * (2.0 / ROT)) * np.arange(LENGTH)
    return jnp.asarray(np.concatenate([np.cos(angles), np.sin(angles)]), f32)


def attention(order, packed, first=()):
    size = 4 * HEAD_DIM
    return pl.pallas_call(
        attention_kernel,
        out_shape=jax.ShapeDtypeStruct((LENGTH, size), bf16),
        in_specs=[ANY] * len(first) + [SMEM] + [VMEM] * 2,
        out_specs=VMEM,
        scratch_shapes=[
            pltpu.VMEM((LENGTH, size), bf16),
            pltpu.VMEM((size, LENGTH), bf16),
            pltpu.VMEM((size, LENGTH), f32),
            pltpu.VMEM((LENGTH, size), bf16),
        ],
        compiler_params=params(60),
        cost_estimate=cost(15, 8, LENGTH * LENGTH // 2),
        name="attention",
    )(*first, order, packed, position_table())


def cut_kernel(w_qkv, w_gate, w_up, out_qkv, out_gu, wide_qkv, wide_gu, sems):
    here = lax.axis_index("seq")
    first = here * FF_LOCAL
    tile = jnp.minimum(first // 128, (FF - 384) // 128) * 128
    copies = []
    for i in range(3):
        lanes = pl.ds(pl.multiple_of(here // 2 * 128 + i * WIDTH, 128), 128)
        to = wide_qkv.at[:, i * 128 : (i + 1) * 128]
        copies.append(pltpu.make_async_copy(w_qkv.at[:, lanes], to, sems.at[i]))
    for i, source in enumerate((w_gate, w_up)):
        lanes = pl.ds(pl.multiple_of(tile, 128), 384)
        copies.append(pltpu.make_async_copy(source.at[:, lanes], wide_gu.at[i], sems.at[3 + i]))
    for copy in copies:
        copy.start()
    row = lax.broadcasted_iota(jnp.int32, (384, 256), 0)
    lane = lax.broadcasted_iota(jnp.int32, (384, 256), 1)
    source = lane // HEAD_DIM * 128 + here % 2 * HEAD_DIM + lane % HEAD_DIM
    pick_qkv = (row == source).astype(bf16)[:, : 3 * HEAD_DIM]
    pick_gu = (row == lane + (first - tile)).astype(bf16)[:, :FF_LOCAL]
    for copy in copies:
        copy.wait()
    out_qkv[...] = dot_tt(pick_qkv, wide_qkv[...]).astype(bf16)
    out_gu[:FF_LOCAL, :] = dot_tt(pick_gu, wide_gu[0]).astype(bf16)
    out_gu[FF_LOCAL:, :] = dot_tt(pick_gu, wide_gu[1]).astype(bf16)


def cut_weights(w_qkv, w_gate, w_up):
    return pl.pallas_call(
        cut_kernel,
        out_shape=[
            jax.ShapeDtypeStruct((3 * HEAD_DIM, WIDTH), bf16),
            jax.ShapeDtypeStruct((2 * FF_LOCAL, WIDTH), bf16),
        ],
        in_specs=[ANY] * 3,
        out_specs=[VMEM] * 2,
        scratch_shapes=[
            pltpu.VMEM((WIDTH, 384), bf16),
            pltpu.VMEM((2, WIDTH, 384), bf16),
            pltpu.SemaphoreType.DMA((5,)),
        ],
        compiler_params=params(60),
        cost_estimate=cost(0.001, 0.001),
        name="cut_weights",
    )(w_qkv, w_gate, w_up)


def column(row):
    return jnp.broadcast_to(row, (8, row.shape[1])).T[:, :1]


def slot_of(i):
    here = lax.axis_index("seq")
    across, up = PLACES[i // 2]
    y = lax.rem(lax.div(here, 4) + (4 + up), 4)
    x = lax.rem(lax.div(here, 2) + across, 2)
    return y * 4 + x * 2 + lax.rem(here + i % 2, 2)


def piece_copies(pieces, inputs, x_all, dy, sems):
    return [
        pltpu.make_async_copy(
            inputs[ref].at[pl.ds(at, rows), :],
            (x_all, dy)[which].at[pl.ds(to, rows), :],
            sems.at[i],
        )
        for i, (which, ref, at, rows, to) in enumerate(pieces)
    ]


def down_copy(source, to, sem):
    rows = pl.ds(pl.multiple_of(lax.axis_index("seq") * FF_LOCAL, 16), FF_LOCAL)
    return pltpu.make_async_copy(source.at[rows, :], to, sem)


def gate_blocks(count, x_all, dy, unit, w_gu, w_d, gain, bias, keep):
    total = 0.0
    for i in range(count):
        rows = slice(i * BLOCK, (i + 1) * BLOCK)
        unit_f, _ = normalise(x_all[rows, :])
        hid = (unit_f * gain[...] + bias[...]).astype(bf16)
        unit[rows, :] = unit_f.astype(bf16)
        gu = dot_nt(w_gu[...], hid)
        act, grad_g, grad_u = gated(gu[:FF_LOCAL], gu[FF_LOCAL:], dot_nt(w_d[...], dy[rows, :]))
        grads = jnp.concatenate([grad_g, grad_u], 0)
        keep(i, act, grads)
        total += jnp.sum(grads.astype(f32), 1, keepdims=True)
    return total


def first_kernel(pieces, n_refs, *refs):
    inputs, refs = refs[:n_refs], refs[n_refs:]
    w_gu, w_d_in, gain, bias, unit, acts, grads, sums, x_all, dy, w_d, sems, sem = refs
    copies = piece_copies(pieces, inputs, x_all, dy, sems)
    copies.append(down_copy(w_d_in, w_d, sem))
    for copy in copies:
        copy.start()
    for copy in copies:
        copy.wait()

    def keep(i, act, grad):
        acts[:, i * BLOCK : (i + 1) * BLOCK] = act
        grads[:, i * BLOCK : (i + 1) * BLOCK] = grad

    total = gate_blocks(x_all.shape[0] // BLOCK, x_all, dy, unit, w_gu, w_d, gain, bias, keep)
    sums[...] = jnp.broadcast_to(total, sums.shape)


def first_half(arrays, pieces, w_gu, w_d, gain, bias):
    half = LENGTH // 2
    return pl.pallas_call(
        lambda *refs: first_kernel(pieces, len(arrays), *refs),
        out_shape=[
            jax.ShapeDtypeStruct((half, WIDTH), bf16),
            jax.ShapeDtypeStruct((FF_LOCAL, half), bf16),
            jax.ShapeDtypeStruct((2 * FF_LOCAL, half), bf16),
            jax.ShapeDtypeStruct((2 * FF_LOCAL, 128), f32),
        ],
        in_specs=[ANY] * len(arrays) + [VMEM] + [ANY] + [VMEM] * 2,
        out_specs=[VMEM] * 4,
        scratch_shapes=[
            pltpu.VMEM((half, WIDTH), bf16),
            pltpu.VMEM((half, WIDTH), bf16),
            pltpu.VMEM((FF_LOCAL, WIDTH), bf16),
            pltpu.SemaphoreType.DMA((len(pieces),)),
            pltpu.SemaphoreType.DMA,
        ],
        compiler_params=params(60),
        cost_estimate=cost(0.001, 0.001),
        name="first_half",
    )(*arrays, w_gu, w_d, gain, bias)


def weights_kernel(pieces, n_refs, *refs):
    inputs, refs = refs[:n_refs], refs[n_refs:]
    heads_in, w_qkv, w_gu, w_d_in, gain, bias = refs[:6]
    unit_in, acts_in, grads_in, sums, block_out = refs[6:11]
    x_all, dy, unit, heads, left, right, stage, w_d, block = refs[11:20]
    piece_sems, head_sems, out_sems, first_sems, weight_sem = refs[20:]
    hidden, both = FF_LOCAL, 2 * FF_LOCAL
    here = lax.axis_index("seq")
    half = LENGTH // 2
    late = (dy.at[half:, :], unit.at[half:, :])
    copies = piece_copies(pieces, inputs, x_all, dy, piece_sems)
    now = [copy for copy, piece in zip(copies, pieces) if piece[4] >= half]
    now.append(down_copy(w_d_in, w_d, weight_sem))
    later = [copy for copy, piece in zip(copies, pieces) if piece[0] and piece[4] < half]
    later.append(pltpu.make_async_copy(unit_in, unit.at[:half, :], first_sems.at[0]))
    later.append(pltpu.make_async_copy(acts_in, right.at[:hidden, :half], first_sems.at[1]))
    later.append(pltpu.make_async_copy(grads_in, left.at[:both, :half], first_sems.at[2]))
    for i in range(SEQ):
        rows = pl.ds(pl.multiple_of(slot_of(i) * HERE, HERE), HERE)
        to = heads.at[i * HERE : (i + 1) * HERE, :]
        later.append(pltpu.make_async_copy(heads_in.at[rows, :], to, head_sems.at[i]))
    for copy in now + later:
        copy.start()
    for copy in now:
        copy.wait()

    def keep(i, act, grad):
        at = slice(half + i * BLOCK, half + (i + 1) * BLOCK)
        right[:hidden, at] = act
        left[:both, at] = grad

    total = gate_blocks(half // BLOCK, x_all.at[half:, :], *late, w_gu, w_d, gain, bias, keep)
    total += sums[:, :1]
    for copy in later:
        copy.wait()
    heads_t = heads[...].T
    left[both:, :] = heads_t[: 3 * HEAD_DIM]
    right[hidden:, :] = heads_t[3 * HEAD_DIM :]
    total_h = jnp.sum(heads_t[: 3 * HEAD_DIM].astype(f32), 1, keepdims=True)
    inner = dot_nn(left[...], unit[...])
    total = jnp.concatenate([total, total_h], 0)
    wide = jnp.concatenate([w_gu[...], w_qkv[...]], 0).astype(f32)
    terms = inner * gain[...] + bias[...] * total
    gain_part = jnp.sum(inner * wide, 0, keepdims=True)
    bias_part = jnp.sum(wide * total, 0, keepdims=True)
    at_row = lax.broadcasted_iota(jnp.int32, (192, WIDTH), 0)
    column_at = at_row // HEAD_DIM * WIDTH + here * HEAD_DIM + at_row % HEAD_DIM
    mine = column_at // 24 * 8 == lax.broadcasted_iota(jnp.int32, (192, WIDTH), 1)
    at_lane = lax.broadcasted_iota(jnp.int32, (32, 192), 1)
    column_at = at_lane // HEAD_DIM * WIDTH + here * HEAD_DIM + at_lane % HEAD_DIM
    pick = (column_at % 24 + 2 == lax.broadcasted_iota(jnp.int32, (32, 192), 0)).astype(bf16)
    extra = dot_nn(pick, jnp.where(mine, total_h, 0.0).astype(bf16))
    row32 = lax.broadcasted_iota(jnp.int32, (32, WIDTH), 0)
    extra += jnp.where(row32 == 0, gain_part, jnp.where(row32 == 1, bias_part, 0.0))
    stage[...] = jnp.concatenate([terms[:both], extra, terms[both:]], 0).T
    products = dot_nn(right[...], dy[...])
    down_all, out_all = products[:hidden], products[hidden:]
    outs = []

    def two(s, lanes):
        first, second = (s * ROWS + r) * 8, ((s + 1) * ROWS + r) * 8
        return jnp.concatenate([stage[first : first + 8, lanes], stage[second : second + 8, lanes]], 0)

    for r in range(ROWS):
        for s in range(0, SEQ, 2):
            for i in range(4):
                lanes = slice(i * 128, (i + 1) * 128)
                block[r, i * HERE + s * 8 : i * HERE + s * 8 + 16, :] = two(s, lanes).astype(bf16)
        for s in range(0, SEQ // 2, 2):
            lanes = slice(512, 576)
            block[r, 512 + s * 8 : 528 + s * 8, :] = jnp.concatenate(
                [two(s, lanes), two(s + 8, lanes)], 1
            ).astype(bf16)
        last = jnp.concatenate(
            [out_all[r * 8 : r * 8 + 8], down_all[r * 22 : (r + 1) * 22], jnp.zeros((2, WIDTH), f32)],
            0,
        ).astype(bf16)
        for i in range(8):
            block[r, 576 + i * 32 : 608 + i * 32, :] = last[:, i * 128 : (i + 1) * 128]
        outs.append(pltpu.make_async_copy(block.at[r], block_out.at[r], out_sems.at[r]))
        outs[r].start()
    for copy in outs:
        copy.wait()


def weight_grads(arrays, pieces, heads, w_qkv, w_gu, w_d, gain, bias, first):
    big = (LENGTH, WIDTH)
    return pl.pallas_call(
        lambda *refs: weights_kernel(pieces, len(arrays), *refs),
        out_shape=jax.ShapeDtypeStruct((ROWS, 832, 128), bf16),
        in_specs=[ANY] * (len(arrays) + 1) + [VMEM] * 2 + [ANY] + [VMEM] * 2 + [ANY] * 3 + [VMEM],
        out_specs=ANY,
        scratch_shapes=[pltpu.VMEM(big, bf16)] * 3
        + [
            pltpu.VMEM((LENGTH, 4 * HEAD_DIM), bf16),
            pltpu.VMEM((2 * FF_LOCAL + 3 * HEAD_DIM, LENGTH), bf16),
            pltpu.VMEM((FF_LOCAL + HEAD_DIM, LENGTH), bf16),
            pltpu.VMEM((WIDTH, 576), f32),
            pltpu.VMEM((FF_LOCAL, WIDTH), bf16),
            pltpu.VMEM((ROWS, 832, 128), bf16),
            pltpu.SemaphoreType.DMA((len(pieces),)),
            pltpu.SemaphoreType.DMA((SEQ,)),
            pltpu.SemaphoreType.DMA((ROWS,)),
            pltpu.SemaphoreType.DMA((3,)),
            pltpu.SemaphoreType.DMA,
        ],
        compiler_params=params(60),
        cost_estimate=cost(8, 20),
        name="weight_grads",
    )(*arrays, heads, w_qkv, w_gu, w_d, gain, bias, *first)


def final_kernel(heads, x, dy, part, grad, gain, w_out, w_qkv, out, input_grad, att, rows, total):
    step = pl.program_id(0)

    @pl.when(step == 0)
    def _():
        for h in range(HEADS):
            here = heads[h * HERE : (h + 1) * HERE, :]
            at = h * HEAD_DIM
            for i in range(3):
                lo = i * WIDTH + at
                rows[:, lo : lo + HEAD_DIM] = here[:, i * HEAD_DIM : (i + 1) * HEAD_DIM]
            att[:, at : at + HEAD_DIM] = here[:, 3 * HEAD_DIM :]

    columns = pl.ds(pl.multiple_of(step * BLOCK, BLOCK), BLOCK)
    out[:, columns] = (part[:, columns] + dot_nn(att[...], w_out[...])).astype(bf16)
    total[:, columns] = grad[:, columns] + dot_nt(rows[...], w_qkv[...])

    @pl.when(step == pl.num_programs(0) - 1)
    def _():
        unit, inv_std = normalise(x[...])
        grad_unit = total[...] * gain[...]
        grad_norm = inv_std * (
            grad_unit
            - jnp.mean(grad_unit, 1, keepdims=True)
            - unit * jnp.mean(grad_unit * unit, 1, keepdims=True)
        )
        input_grad[...] = (dy[...].astype(f32) + grad_norm).astype(bf16)


def final_rows(heads, x, dy, part, grad, gain, w_out, w_qkv):
    fixed = lambda shape: pl.BlockSpec(shape, lambda j: (0,) * len(shape))
    own = fixed((HERE, WIDTH))
    return pl.pallas_call(
        final_kernel,
        grid=(WIDTH // BLOCK,),
        out_shape=[jax.ShapeDtypeStruct((HERE, WIDTH), bf16)] * 2,
        in_specs=[fixed((LENGTH, 256)), own, own, own, own, fixed((1, WIDTH))]
        + [pl.BlockSpec((WIDTH, BLOCK), lambda j: (0, j))]
        + [pl.BlockSpec((BLOCK, 3 * WIDTH), lambda j: (j, 0))],
        out_specs=[own, own],
        scratch_shapes=[
            pltpu.VMEM((HERE, WIDTH), bf16),
            pltpu.VMEM((HERE, 3 * WIDTH), bf16),
            pltpu.VMEM((HERE, WIDTH), f32),
        ],
        compiler_params=params(60),
        cost_estimate=cost(1.1, 10),
        name="final_rows",
    )(heads, x, dy, part, grad, gain, w_out, w_qkv)


def sum_kernel(got, send, down, out):
    total = got[0].astype(f32)
    for r in range(1, ROWS):
        total += got[r].astype(f32)
    for i in range(4):
        send[:, i * 128 : (i + 1) * 128] = total[i * HERE : (i + 1) * HERE].astype(bf16)
    left = jnp.concatenate([total[512:576, :64], total[512:576, 64:]], 0)
    send[:, 512:] = jnp.concatenate([left, jnp.zeros((HERE, 64), f32)], 1).astype(bf16)
    for i in range(8):
        lanes = slice(i * 128, (i + 1) * 128)
        out[:, lanes] = total[576 + i * 32 : 584 + i * 32]
        down[:, lanes] = total[584 + i * 32 : 606 + i * 32]


def sum_rows(got):
    return pl.pallas_call(
        sum_kernel,
        out_shape=[
            jax.ShapeDtypeStruct((HERE, 640), bf16),
            jax.ShapeDtypeStruct((22, WIDTH), f32),
            jax.ShapeDtypeStruct((8, WIDTH), f32),
        ],
        in_specs=[VMEM],
        out_specs=[VMEM] * 3,
        compiler_params=params(16),
        cost_estimate=cost(0.001, 2),
        name="sum_rows",
    )(got)


def layout_kernel(mine, qkv, gate, up, gain, bias, sums):
    more = jnp.zeros((8, 128), f32)
    for s in range(SEQ):
        here = mine[s * 8 : (s + 1) * 8, :].astype(f32)
        gate[:, s * FF_LOCAL : (s + 1) * FF_LOCAL] = here[:, :FF_LOCAL]
        up[:, s * FF_LOCAL : (s + 1) * FF_LOCAL] = here[:, FF_LOCAL : 2 * FF_LOCAL]
        for i in range(3):
            lo = i * WIDTH + s * HEAD_DIM
            qkv[:, lo : lo + HEAD_DIM] = here[:, 384 + i * HEAD_DIM : 384 + (i + 1) * HEAD_DIM]
        more += here[:, 256:384]
    turned = more.T
    gain[...] = turned[96:97, :]
    bias[...] = turned[97:98, :]
    sums[...] = more[0:1, 98:122]


def last_layout(mine):
    return pl.pallas_call(
        layout_kernel,
        out_shape=[
            jax.ShapeDtypeStruct((8, 3 * WIDTH), f32),
            jax.ShapeDtypeStruct((8, FF), f32),
            jax.ShapeDtypeStruct((8, FF), f32),
            jax.ShapeDtypeStruct((1, 8), f32),
            jax.ShapeDtypeStruct((1, 8), f32),
            jax.ShapeDtypeStruct((1, 24), f32),
        ],
        in_specs=[VMEM],
        out_specs=[VMEM] * 6,
        compiler_params=params(16),
        cost_estimate=cost(0.001, 1),
        name="last_layout",
    )(mine)


PLACES = [(0, 0), (0, -1), (0, 1), (1, 0), (0, 2), (1, 2), (1, 1), (1, -1)]
CORE = [(i, i ^ 1) for i in range(SEQ)]
PAIR = [(i, i ^ 2) for i in range(SEQ)]
UP = [(i, (i + 4) % SEQ) for i in range(SEQ)]
DOWN = [(i, (i + 12) % SEQ) for i in range(SEQ)]
DOWN_PAIR = [(i, (i + 12) % SEQ ^ 2) for i in range(SEQ)]


def send(value, to):
    return lax.ppermute(value, "seq", to)


def gather(x, dy, exchange, after):
    own = jnp.concatenate([x, dy], 0)
    below = send(own, UP)
    above = send(own, DOWN)
    pair = send(own, PAIR)
    late = exchange(below)
    far = send(below, UP)
    opposite = send(above, DOWN_PAIR)
    most = pair[:MOST]
    rest = [far, opposite, send(most, DOWN), send(most, UP)]
    rest.append(send(jnp.concatenate([above[MOST:], below[MOST:]], 0), PAIR))
    first = [both for a in (own, below, above, pair) for both in (a, send(a, CORE))]
    late, rest = after(late, first, rest)
    return first, [both for a in rest for both in (a, send(a, CORE))], late


MOST = 176


def pieces_of(places):
    return [
        (which, i, which * HERE, HERE, i * HERE) for i in range(places) for which in range(2)
    ]


def pieces_late():
    pieces = pieces_of(12)
    for place in range(2):
        for core in range(2):
            to = (12 + 2 * place + core) * HERE
            first, left = 12 + 2 * place + core, 2 * HERE - MOST
            pieces.append((0, first, 0, HERE, to))
            pieces.append((1, first, HERE, MOST - HERE, to))
            pieces.append((1, 16 + core, place * left, left, to + MOST - HERE))
    return pieces


def shards(x, dy, order, ln_gain, ln_bias, w_qkv, b_qkv, w_out, w_gate, w_up, w_down):
    x, dy = x[0], dy[0]
    gain, bias = ln_gain[None, :], ln_bias[None, :]

    table = rotary_tables()
    packed = own_heads(order, x, dy, w_qkv, w_out, b_qkv[None, :], gain, bias, table)
    w_qkv_s, w_gu_s = cut_weights(w_qkv, w_gate, w_up)

    def exchange(first):
        return lax.all_to_all(packed, "seq", 0, 0, tiled=True)

    def attend(packed_here, early, arrays):
        first = first_half(
            early, pieces_of(len(early)), w_gu_s, w_down, gain, bias
        )
        heads = attention(order, packed_here, first)
        return (heads, first), [lax.optimization_barrier((heads, a))[1] for a in arrays]

    early, arrays, (heads, first) = gather(x, dy, exchange, attend)
    heads_here = lax.all_to_all(heads, "seq", 0, 0, tiled=True)
    arrays = early + arrays
    block = weight_grads(
        arrays, pieces_late(), heads, w_qkv_s, w_gu_s, w_down, gain, bias, first
    )
    block, heads_here = lax.optimization_barrier((block, heads_here))
    got = lax.all_to_all(block, "rows", 0, 0, tiled=True)
    x_late, _ = lax.optimization_barrier((x, heads_here))
    part, grad = own_rows(x_late, dy, gain, bias, w_gate, w_up, w_down)
    output, input_grad = final_rows(heads_here, x, dy, part, grad, gain, w_out, w_qkv)
    got, output, input_grad = lax.optimization_barrier((got, output, input_grad))
    outgoing, o_down, o_out = sum_rows(got)
    mine = lax.all_to_all(outgoing, "seq", 0, 0, tiled=True)
    o_qkv, o_gate, o_up, o_gain, o_bias, sums = last_layout(mine)
    return (
        output[None],
        input_grad[None],
        o_qkv,
        o_out,
        o_gate,
        o_up,
        o_down,
        sums[0],
        o_gain[0],
        o_bias[0],
    )


def solution(mesh):
    rows = P("rows", "seq", None)
    both = P(("seq", "rows"), None)
    flat = P(("seq", "rows"))
    return jax.shard_map(
        shards,
        mesh=mesh,
        in_specs=(rows, rows) + (P(),) * 9,
        out_specs=(rows, rows, both, both, both, both, both, flat, flat, flat),
        check_vma=False,
    )
```

```python
import jax
import jax.numpy as jnp
import numpy as np
from jax import lax
from jax.experimental import pallas as pl
from jax.experimental.pallas import tpu as pltpu
from jax.sharding import PartitionSpec as P

HEADS = 16
HEAD_DIM = 64
ROT = 16
GROUP = 64
LENGTH = 2048
WIDTH = 1024
FF = 2816
FF_LOCAL = 176
BLOCK = 256
SEQ = 16
ROWS = 8
HERE = 128
epsilon = 1e-05
f32 = jnp.float32
bf16 = jnp.bfloat16
SMEM = pl.BlockSpec(memory_space=pltpu.SMEM)
VMEM = pl.BlockSpec(memory_space=pltpu.VMEM)
ANY = pl.BlockSpec(memory_space=pl.ANY)


def dot_nn(a, b):
    return lax.dot_general(a, b, (((1,), (0,)), ((), ())), preferred_element_type=f32)


def dot_nt(a, b):
    return lax.dot_general(a, b, (((1,), (1,)), ((), ())), preferred_element_type=f32)


def dot_tn(a, b):
    return lax.dot_general(a, b, (((0,), (0,)), ((), ())), preferred_element_type=f32)


def dot_tt(a, b):
    return lax.dot_general(a, b, (((0,), (1,)), ((), ())), preferred_element_type=f32)


def params(mib):
    return pltpu.CompilerParams(vmem_limit_bytes=mib * 1024 * 1024)


def cost(gflop, mib, exps=0):
    return pl.CostEstimate(
        flops=int(gflop * 1e9), bytes_accessed=int(mib * 2**20), transcendentals=int(exps)
    )


def normalise(rows):
    rows = rows.astype(f32)
    mean = jnp.mean(rows, 1, keepdims=True)
    centred = rows - mean
    inv_std = lax.rsqrt(jnp.mean(centred * centred, 1, keepdims=True) + epsilon)
    return centred * inv_std, inv_std


def gated(gate, up, grad_act):
    sig = 1.0 / (1.0 + jnp.exp(-gate))
    silu = gate * sig
    grad_g = grad_act * up * (sig * (1.0 + gate - silu))
    grad_u = grad_act * silu
    return (silu * up).astype(bf16), grad_g.astype(bf16), grad_u.astype(bf16)


def rotary_tables():
    half = ROT // 2
    lane = np.arange(2 * HEAD_DIM) % HEAD_DIM
    frequency = np.where(lane < ROT, 10000.0 ** (-(lane % half) * (2.0 / ROT)), 0.0)
    groups = np.arange(LENGTH // GROUP)[:, None] * GROUP * frequency
    inside = np.arange(GROUP)[:, None] * frequency
    parts = (np.cos(groups), np.sin(groups), np.cos(inside), np.sin(inside))
    return jnp.asarray(np.concatenate(parts), f32)


def group_rotation(table, group):
    count = LENGTH // GROUP
    cos_g, sin_g = table[pl.ds(group, 1), :], table[pl.ds(group + count, 1), :]
    cos_i = table[2 * count : 2 * count + GROUP, :]
    sin_i = table[2 * count + GROUP :, :]
    return cos_g * cos_i - sin_g * sin_i, sin_g * cos_i + cos_g * sin_i


def own_kernel(x, dy, gain, bias, wg_in, wu_in, wd_in, out, grad, wg, wu, wd, sems):
    groups = ((0, 512), (512, 1280), (1280, 2048), (2048, 2816))
    copies = []
    for i, (lo, hi) in enumerate(groups):
        part = slice(lo, hi)
        pairs = ((wg_in.at[:, part], wg.at[:, part]), (wu_in.at[:, part], wu.at[:, part]))
        pairs += ((wd_in.at[part, :], wd.at[part, :]),)
        copies.append([pltpu.make_async_copy(*pair, sems.at[j, i]) for j, pair in enumerate(pairs)])
        for copy in copies[i]:
            copy.start()
    unit, _ = normalise(x[...])
    hid = (unit * gain[...] + bias[...]).astype(bf16)
    for i, (lo, hi) in enumerate(groups):
        for copy in copies[i]:
            copy.wait()
        part = slice(lo, hi)
        gate, up = dot_nn(hid, wg[:, part]), dot_nn(hid, wu[:, part])
        act, grad_g, grad_u = gated(gate, up, dot_nt(dy[...], wd[part, :]))
        more = dot_nt(grad_g, wg[:, part]) + dot_nt(grad_u, wu[:, part])
        out[...] = (x[...].astype(f32) if i == 0 else out[...]) + dot_nn(act, wd[part, :])
        grad[...] = more if i == 0 else grad[...] + more


def own_rows(x, dy, gain, bias, w_gate, w_up, w_down):
    return pl.pallas_call(
        own_kernel,
        out_shape=[jax.ShapeDtypeStruct((HERE, WIDTH), f32)] * 2,
        in_specs=[VMEM] * 4 + [ANY] * 3,
        out_specs=[VMEM] * 2,
        scratch_shapes=[
            pltpu.VMEM((WIDTH, FF), bf16),
            pltpu.VMEM((WIDTH, FF), bf16),
            pltpu.VMEM((FF, WIDTH), bf16),
            pltpu.SemaphoreType.DMA((3, 4)),
        ],
        compiler_params=params(60),
        cost_estimate=cost(4.5, 18),
        name="own_rows",
    )(x, dy, gain, bias, w_gate, w_up, w_down)


def heads_kernel(order, x, dy, w_in, w_out_in, b_qkv, gain, bias, table, out, *scratch):
    w, w_out, cosine, sine, sems = scratch
    lanes = 2 * HEAD_DIM
    groups = ((0, 256), (256, 512), (512, 1024))
    copies = []
    for i, (lo, hi) in enumerate(groups):
        pairs = [(w_out_in.at[lo:hi, :], w_out.at[lo:hi, :])]
        for j in range(3):
            part = slice(j * WIDTH + lo, j * WIDTH + hi)
            pairs.append((w_in.at[:, part], w.at[:, part]))
        copies.append([pltpu.make_async_copy(*pair, sems.at[i, j]) for j, pair in enumerate(pairs)])
        for copy in copies[i]:
            copy.start()
    lane = lax.broadcasted_iota(jnp.int32, (1, lanes), 1)
    low = lane % HEAD_DIM < ROT // 2
    scale = jnp.where(lane < HEAD_DIM, HEAD_DIM**-0.5, 1.0)
    for g in range(HERE // GROUP):
        rows = slice(g * GROUP, (g + 1) * GROUP)
        group = order[lax.axis_index("seq") * (HERE // GROUP) + g]
        cosine[rows, :], sine[rows, :] = group_rotation(table, group)
    unit, _ = normalise(x[...])
    hid = (unit * gain[...] + bias[...]).astype(bf16)
    for i, (lo, hi) in enumerate(groups):
        for copy in copies[i]:
            copy.wait()
        parts = [slice(j * WIDTH + lo, j * WIDTH + hi) for j in range(3)]
        q, k, v = (dot_nn(hid, w[:, part]) + b_qkv[:, part] for part in parts)
        grad_att = dot_nt(dy[...], w_out[lo:hi, :])
        for h in range((hi - lo) // HEAD_DIM):
            part = slice(h * HEAD_DIM, (h + 1) * HEAD_DIM)
            raw = jnp.concatenate([q[:, part], k[:, part]], 1)
            before, after = pltpu.roll(raw, ROT // 2, 1), pltpu.roll(raw, lanes - ROT // 2, 1)
            turned = (raw * cosine[...] + jnp.where(low, -after, before) * sine[...]) * scale
            at = lo // HEAD_DIM + h
            rows = slice(at * HERE, (at + 1) * HERE)
            out[rows, :lanes] = turned.astype(bf16)
            out[rows, lanes:] = jnp.concatenate([v[:, part], grad_att[:, part]], 1).astype(bf16)


def own_heads(order, x, dy, w_qkv, w_out, b_qkv, gain, bias, table):
    return pl.pallas_call(
        heads_kernel,
        out_shape=jax.ShapeDtypeStruct((LENGTH, 4 * HEAD_DIM), bf16),
        in_specs=[SMEM] + [VMEM] * 2 + [ANY] * 2 + [VMEM] * 4,
        out_specs=VMEM,
        scratch_shapes=[
            pltpu.VMEM((WIDTH, 3 * WIDTH), bf16),
            pltpu.VMEM((WIDTH, WIDTH), bf16),
            pltpu.VMEM((HERE, 2 * HEAD_DIM), f32),
            pltpu.VMEM((HERE, 2 * HEAD_DIM), f32),
            pltpu.SemaphoreType.DMA((3, 4)),
        ],
        compiler_params=params(60),
        cost_estimate=cost(1.1, 9),
        name="own_heads",
    )(order, x, dy, w_qkv, w_out, b_qkv, gain, bias, table)


def attention_kernel(*refs):
    order, packed, table, out_ref, rows_in, cols_in, cols, turn = refs[-8:]
    groups = LENGTH // GROUP
    for g in range(groups):
        at = pl.multiple_of(order[g] * GROUP, GROUP)
        rows_in[pl.ds(at, GROUP), :] = packed[g * GROUP : (g + 1) * GROUP, :]
    cols_in[...] = rows_in[...].T
    k = rows_in[:, HEAD_DIM : 2 * HEAD_DIM]
    v = rows_in[:, 2 * HEAD_DIM : 3 * HEAD_DIM]
    q_t, k_t, v_t, do_t = (cols_in.at[i * HEAD_DIM : (i + 1) * HEAD_DIM, :] for i in range(4))
    dq_t, dk_t, dv_t, att_t = (cols.at[i * HEAD_DIM : (i + 1) * HEAD_DIM, :] for i in range(4))
    row = lax.broadcasted_iota(jnp.int32, (BLOCK, BLOCK), 0)
    col = lax.broadcasted_iota(jnp.int32, (BLOCK, BLOCK), 1)
    visible = row <= col
    def products(i):
        here, n = slice(i * BLOCK, (i + 1) * BLOCK), (i + 1) * BLOCK
        return dot_nn(k[:n], q_t[:, here]), dot_nn(v[:n], do_t[:, here])

    def softmax(i, scores):
        lo = i * BLOCK
        last = jnp.where(visible, scores[lo:], -1e30)
        scores = last if i == 0 else jnp.concatenate([scores[:lo], last], 0)
        top = jnp.max(scores, 0, keepdims=True)
        weights = jnp.exp(scores - top)
        inverse = 1.0 / jnp.sum(weights, 0, keepdims=True)
        return weights, weights.astype(bf16), inverse

    order_of = list(reversed(range(LENGTH // BLOCK)))
    ahead = products(order_of[0])
    for j, i in enumerate(order_of):
        lo, n = i * BLOCK, (i + 1) * BLOCK
        here, seen = slice(lo, n), slice(0, n)
        scores, grad_p = ahead
        if j + 1 < len(order_of):
            ahead = products(order_of[j + 1])
        weights, weights_b, inverse = softmax(i, scores)
        att = dot_nn(v_t[:, seen], weights_b) * inverse
        do_f = do_t[:, here].astype(f32)
        delta = jnp.sum(weights * grad_p, 0, keepdims=True) * inverse
        grad_s = (weights * (grad_p - delta)).astype(bf16)
        dv = dot_nt((do_f * inverse).astype(bf16), weights_b)
        att_t[:, here] = att
        dq_t[:, here] = dot_nn(k_t[:, seen], grad_s) * (inverse * HEAD_DIM**-0.5)
        dk = dot_nt((q_t[:, here].astype(f32) * inverse).astype(bf16), grad_s)
        if n == LENGTH:
            dk_t[...], dv_t[...] = dk, dv
        else:
            dk_t[:, seen] += dk
            dv_t[:, seen] += dv
    half = ROT // 2
    cosine, sine = table[:half, :], table[half:, :]
    for part in (dq_t, dk_t):
        first, second = part[:half, :], part[half:ROT, :]
        part[:half, :] = first * cosine + second * sine
        part[half:ROT, :] = second * cosine - first * sine
    turn[...] = cols[...].T.astype(bf16)
    for g in range(groups):
        at = pl.multiple_of(order[g] * GROUP, GROUP)
        out_ref[g * GROUP : (g + 1) * GROUP, :] = turn[pl.ds(at, GROUP), :]


def position_table():
    half = ROT // 2
    angles = 10000.0 ** (-np.arange(half)[:, None] * (2.0 / ROT)) * np.arange(LENGTH)
    return jnp.asarray(np.concatenate([np.cos(angles), np.sin(angles)]), f32)


def attention(order, packed, first=()):
    size = 4 * HEAD_DIM
    return pl.pallas_call(
        attention_kernel,
        out_shape=jax.ShapeDtypeStruct((LENGTH, size), bf16),
        in_specs=[ANY] * len(first) + [SMEM] + [VMEM] * 2,
        out_specs=VMEM,
        scratch_shapes=[
            pltpu.VMEM((LENGTH, size), bf16),
            pltpu.VMEM((size, LENGTH), bf16),
            pltpu.VMEM((size, LENGTH), f32),
            pltpu.VMEM((LENGTH, size), bf16),
        ],
        compiler_params=params(60),
        cost_estimate=cost(15, 8, LENGTH * LENGTH // 2),
        name="attention",
    )(*first, order, packed, position_table())


def cut_kernel(w_qkv, w_gate, w_up, out_qkv, out_gu, wide_qkv, wide_gu, sems):
    here = lax.axis_index("seq")
    first = here * FF_LOCAL
    tile = jnp.minimum(first // 128, (FF - 384) // 128) * 128
    copies = []
    for i in range(3):
        lanes = pl.ds(pl.multiple_of(here // 2 * 128 + i * WIDTH, 128), 128)
        to = wide_qkv.at[:, i * 128 : (i + 1) * 128]
        copies.append(pltpu.make_async_copy(w_qkv.at[:, lanes], to, sems.at[i]))
    for i, source in enumerate((w_gate, w_up)):
        lanes = pl.ds(pl.multiple_of(tile, 128), 384)
        copies.append(pltpu.make_async_copy(source.at[:, lanes], wide_gu.at[i], sems.at[3 + i]))
    for copy in copies:
        copy.start()
    row = lax.broadcasted_iota(jnp.int32, (384, 256), 0)
    lane = lax.broadcasted_iota(jnp.int32, (384, 256), 1)
    source = lane // HEAD_DIM * 128 + here % 2 * HEAD_DIM + lane % HEAD_DIM
    pick_qkv = (row == source).astype(bf16)[:, : 3 * HEAD_DIM]
    pick_gu = (row == lane + (first - tile)).astype(bf16)[:, :FF_LOCAL]
    for copy in copies:
        copy.wait()
    out_qkv[...] = dot_tt(pick_qkv, wide_qkv[...]).astype(bf16)
    out_gu[:FF_LOCAL, :] = dot_tt(pick_gu, wide_gu[0]).astype(bf16)
    out_gu[FF_LOCAL:, :] = dot_tt(pick_gu, wide_gu[1]).astype(bf16)


def cut_weights(w_qkv, w_gate, w_up):
    return pl.pallas_call(
        cut_kernel,
        out_shape=[
            jax.ShapeDtypeStruct((3 * HEAD_DIM, WIDTH), bf16),
            jax.ShapeDtypeStruct((2 * FF_LOCAL, WIDTH), bf16),
        ],
        in_specs=[ANY] * 3,
        out_specs=[VMEM] * 2,
        scratch_shapes=[
            pltpu.VMEM((WIDTH, 384), bf16),
            pltpu.VMEM((2, WIDTH, 384), bf16),
            pltpu.SemaphoreType.DMA((5,)),
        ],
        compiler_params=params(60),
        cost_estimate=cost(0.001, 0.001),
        name="cut_weights",
    )(w_qkv, w_gate, w_up)


def column(row):
    return jnp.broadcast_to(row, (8, row.shape[1])).T[:, :1]


def slot_of(i):
    here = lax.axis_index("seq")
    across, up = PLACES[i // 2]
    y = lax.rem(lax.div(here, 4) + (4 + up), 4)
    x = lax.rem(lax.div(here, 2) + across, 2)
    return y * 4 + x * 2 + lax.rem(here + i % 2, 2)


def piece_copies(pieces, inputs, x_all, dy, sems):
    return [
        pltpu.make_async_copy(
            inputs[ref].at[pl.ds(at, rows), :],
            (x_all, dy)[which].at[pl.ds(to, rows), :],
            sems.at[i],
        )
        for i, (which, ref, at, rows, to) in enumerate(pieces)
    ]


def down_copy(source, to, sem):
    rows = pl.ds(pl.multiple_of(lax.axis_index("seq") * FF_LOCAL, 16), FF_LOCAL)
    return pltpu.make_async_copy(source.at[rows, :], to, sem)


def gate_blocks(count, x_all, dy, unit, w_gu, w_d, gain, bias, keep):
    total = 0.0
    for i in range(count):
        rows = slice(i * BLOCK, (i + 1) * BLOCK)
        unit_f, _ = normalise(x_all[rows, :])
        hid = (unit_f * gain[...] + bias[...]).astype(bf16)
        unit[rows, :] = unit_f.astype(bf16)
        gu = dot_nt(w_gu[...], hid)
        act, grad_g, grad_u = gated(gu[:FF_LOCAL], gu[FF_LOCAL:], dot_nt(w_d[...], dy[rows, :]))
        grads = jnp.concatenate([grad_g, grad_u], 0)
        keep(i, act, grads)
        total += jnp.sum(grads.astype(f32), 1, keepdims=True)
    return total


def first_kernel(pieces, n_refs, *refs):
    inputs, refs = refs[:n_refs], refs[n_refs:]
    w_gu, w_d_in, gain, bias, unit, acts, grads, sums, x_all, dy, w_d, sems, sem = refs
    copies = piece_copies(pieces, inputs, x_all, dy, sems)
    copies.append(down_copy(w_d_in, w_d, sem))
    for copy in copies:
        copy.start()
    for copy in copies:
        copy.wait()

    def keep(i, act, grad):
        acts[:, i * BLOCK : (i + 1) * BLOCK] = act
        grads[:, i * BLOCK : (i + 1) * BLOCK] = grad

    total = gate_blocks(x_all.shape[0] // BLOCK, x_all, dy, unit, w_gu, w_d, gain, bias, keep)
    sums[...] = jnp.broadcast_to(total, sums.shape)


def first_half(arrays, pieces, w_gu, w_d, gain, bias):
    half = LENGTH // 2
    return pl.pallas_call(
        lambda *refs: first_kernel(pieces, len(arrays), *refs),
        out_shape=[
            jax.ShapeDtypeStruct((half, WIDTH), bf16),
            jax.ShapeDtypeStruct((FF_LOCAL, half), bf16),
            jax.ShapeDtypeStruct((2 * FF_LOCAL, half), bf16),
            jax.ShapeDtypeStruct((2 * FF_LOCAL, 128), f32),
        ],
        in_specs=[ANY] * len(arrays) + [VMEM] + [ANY] + [VMEM] * 2,
        out_specs=[VMEM] * 4,
        scratch_shapes=[
            pltpu.VMEM((half, WIDTH), bf16),
            pltpu.VMEM((half, WIDTH), bf16),
            pltpu.VMEM((FF_LOCAL, WIDTH), bf16),
            pltpu.SemaphoreType.DMA((len(pieces),)),
            pltpu.SemaphoreType.DMA,
        ],
        compiler_params=params(60),
        cost_estimate=cost(0.001, 0.001),
        name="first_half",
    )(*arrays, w_gu, w_d, gain, bias)


def weights_kernel(pieces, n_refs, *refs):
    inputs, refs = refs[:n_refs], refs[n_refs:]
    heads_in, w_qkv, w_gu, w_d_in, gain, bias = refs[:6]
    unit_in, acts_in, grads_in, sums, block_out = refs[6:11]
    x_all, dy, unit, heads, left, right, stage, w_d, block = refs[11:20]
    piece_sems, head_sems, out_sems, first_sems, weight_sem = refs[20:]
    hidden, both = FF_LOCAL, 2 * FF_LOCAL
    here = lax.axis_index("seq")
    half = LENGTH // 2
    late = (dy.at[half:, :], unit.at[half:, :])
    copies = piece_copies(pieces, inputs, x_all, dy, piece_sems)
    now = [copy for copy, piece in zip(copies, pieces) if piece[4] >= half]
    now.append(down_copy(w_d_in, w_d, weight_sem))
    later = [copy for copy, piece in zip(copies, pieces) if piece[0] and piece[4] < half]
    later.append(pltpu.make_async_copy(unit_in, unit.at[:half, :], first_sems.at[0]))
    later.append(pltpu.make_async_copy(acts_in, right.at[:hidden, :half], first_sems.at[1]))
    later.append(pltpu.make_async_copy(grads_in, left.at[:both, :half], first_sems.at[2]))
    for i in range(SEQ):
        rows = pl.ds(pl.multiple_of(slot_of(i) * HERE, HERE), HERE)
        to = heads.at[i * HERE : (i + 1) * HERE, :]
        later.append(pltpu.make_async_copy(heads_in.at[rows, :], to, head_sems.at[i]))
    for copy in now + later:
        copy.start()
    for copy in now:
        copy.wait()

    def keep(i, act, grad):
        at = slice(half + i * BLOCK, half + (i + 1) * BLOCK)
        right[:hidden, at] = act
        left[:both, at] = grad

    total = gate_blocks(half // BLOCK, x_all.at[half:, :], *late, w_gu, w_d, gain, bias, keep)
    total += sums[:, :1]
    for copy in later:
        copy.wait()
    heads_t = heads[...].T
    left[both:, :] = heads_t[: 3 * HEAD_DIM]
    right[hidden:, :] = heads_t[3 * HEAD_DIM :]
    total_h = jnp.sum(heads_t[: 3 * HEAD_DIM].astype(f32), 1, keepdims=True)
    inner = dot_nn(left[...], unit[...])
    total = jnp.concatenate([total, total_h], 0)
    wide = jnp.concatenate([w_gu[...], w_qkv[...]], 0).astype(f32)
    terms = inner * gain[...] + bias[...] * total
    gain_part = jnp.sum(inner * wide, 0, keepdims=True)
    bias_part = jnp.sum(wide * total, 0, keepdims=True)
    at_row = lax.broadcasted_iota(jnp.int32, (192, WIDTH), 0)
    column_at = at_row // HEAD_DIM * WIDTH + here * HEAD_DIM + at_row % HEAD_DIM
    mine = column_at // 24 * 8 == lax.broadcasted_iota(jnp.int32, (192, WIDTH), 1)
    at_lane = lax.broadcasted_iota(jnp.int32, (32, 192), 1)
    column_at = at_lane // HEAD_DIM * WIDTH + here * HEAD_DIM + at_lane % HEAD_DIM
    pick = (column_at % 24 + 2 == lax.broadcasted_iota(jnp.int32, (32, 192), 0)).astype(bf16)
    extra = dot_nn(pick, jnp.where(mine, total_h, 0.0).astype(bf16))
    row32 = lax.broadcasted_iota(jnp.int32, (32, WIDTH), 0)
    extra += jnp.where(row32 == 0, gain_part, jnp.where(row32 == 1, bias_part, 0.0))
    stage[...] = jnp.concatenate([terms[:both], extra, terms[both:]], 0).T
    products = dot_nn(right[...], dy[...])
    down_all, out_all = products[:hidden], products[hidden:]
    outs = []

    def two(s, lanes):
        first, second = (s * ROWS + r) * 8, ((s + 1) * ROWS + r) * 8
        return jnp.concatenate([stage[first : first + 8, lanes], stage[second : second + 8, lanes]], 0)

    for r in range(ROWS):
        for s in range(0, SEQ, 2):
            for i in range(4):
                lanes = slice(i * 128, (i + 1) * 128)
                block[r, i * HERE + s * 8 : i * HERE + s * 8 + 16, :] = two(s, lanes).astype(bf16)
        for s in range(0, SEQ // 2, 2):
            lanes = slice(512, 576)
            block[r, 512 + s * 8 : 528 + s * 8, :] = jnp.concatenate(
                [two(s, lanes), two(s + 8, lanes)], 1
            ).astype(bf16)
        last = jnp.concatenate(
            [out_all[r * 8 : r * 8 + 8], down_all[r * 22 : (r + 1) * 22], jnp.zeros((2, WIDTH), f32)],
            0,
        ).astype(bf16)
        for i in range(8):
            block[r, 576 + i * 32 : 608 + i * 32, :] = last[:, i * 128 : (i + 1) * 128]
        outs.append(pltpu.make_async_copy(block.at[r], block_out.at[r], out_sems.at[r]))
        outs[r].start()
    for copy in outs:
        copy.wait()


def weight_grads(arrays, pieces, heads, w_qkv, w_gu, w_d, gain, bias, first):
    big = (LENGTH, WIDTH)
    return pl.pallas_call(
        lambda *refs: weights_kernel(pieces, len(arrays), *refs),
        out_shape=jax.ShapeDtypeStruct((ROWS, 832, 128), bf16),
        in_specs=[ANY] * (len(arrays) + 1) + [VMEM] * 2 + [ANY] + [VMEM] * 2 + [ANY] * 3 + [VMEM],
        out_specs=ANY,
        scratch_shapes=[pltpu.VMEM(big, bf16)] * 3
        + [
            pltpu.VMEM((LENGTH, 4 * HEAD_DIM), bf16),
            pltpu.VMEM((2 * FF_LOCAL + 3 * HEAD_DIM, LENGTH), bf16),
            pltpu.VMEM((FF_LOCAL + HEAD_DIM, LENGTH), bf16),
            pltpu.VMEM((WIDTH, 576), f32),
            pltpu.VMEM((FF_LOCAL, WIDTH), bf16),
            pltpu.VMEM((ROWS, 832, 128), bf16),
            pltpu.SemaphoreType.DMA((len(pieces),)),
            pltpu.SemaphoreType.DMA((SEQ,)),
            pltpu.SemaphoreType.DMA((ROWS,)),
            pltpu.SemaphoreType.DMA((3,)),
            pltpu.SemaphoreType.DMA,
        ],
        compiler_params=params(60),
        cost_estimate=cost(8, 20),
        name="weight_grads",
    )(*arrays, heads, w_qkv, w_gu, w_d, gain, bias, *first)


def final_kernel(heads, x, dy, part, grad, gain, w_out, w_qkv, out, input_grad, att, rows, total):
    step = pl.program_id(0)

    @pl.when(step == 0)
    def _():
        for h in range(HEADS):
            here = heads[h * HERE : (h + 1) * HERE, :]
            at = h * HEAD_DIM
            for i in range(3):
                lo = i * WIDTH + at
                rows[:, lo : lo + HEAD_DIM] = here[:, i * HEAD_DIM : (i + 1) * HEAD_DIM]
            att[:, at : at + HEAD_DIM] = here[:, 3 * HEAD_DIM :]

    columns = pl.ds(pl.multiple_of(step * BLOCK, BLOCK), BLOCK)
    out[:, columns] = (part[:, columns] + dot_nn(att[...], w_out[...])).astype(bf16)
    total[:, columns] = grad[:, columns] + dot_nt(rows[...], w_qkv[...])

    @pl.when(step == pl.num_programs(0) - 1)
    def _():
        unit, inv_std = normalise(x[...])
        grad_unit = total[...] * gain[...]
        grad_norm = inv_std * (
            grad_unit
            - jnp.mean(grad_unit, 1, keepdims=True)
            - unit * jnp.mean(grad_unit * unit, 1, keepdims=True)
        )
        input_grad[...] = (dy[...].astype(f32) + grad_norm).astype(bf16)


def final_rows(heads, x, dy, part, grad, gain, w_out, w_qkv):
    fixed = lambda shape: pl.BlockSpec(shape, lambda j: (0,) * len(shape))
    own = fixed((HERE, WIDTH))
    return pl.pallas_call(
        final_kernel,
        grid=(WIDTH // BLOCK,),
        out_shape=[jax.ShapeDtypeStruct((HERE, WIDTH), bf16)] * 2,
        in_specs=[fixed((LENGTH, 256)), own, own, own, own, fixed((1, WIDTH))]
        + [pl.BlockSpec((WIDTH, BLOCK), lambda j: (0, j))]
        + [pl.BlockSpec((BLOCK, 3 * WIDTH), lambda j: (j, 0))],
        out_specs=[own, own],
        scratch_shapes=[
            pltpu.VMEM((HERE, WIDTH), bf16),
            pltpu.VMEM((HERE, 3 * WIDTH), bf16),
            pltpu.VMEM((HERE, WIDTH), f32),
        ],
        compiler_params=params(60),
        cost_estimate=cost(1.1, 10),
        name="final_rows",
    )(heads, x, dy, part, grad, gain, w_out, w_qkv)


def sum_kernel(got, send, down, out):
    total = got[0].astype(f32)
    for r in range(1, ROWS):
        total += got[r].astype(f32)
    for i in range(4):
        send[:, i * 128 : (i + 1) * 128] = total[i * HERE : (i + 1) * HERE].astype(bf16)
    left = jnp.concatenate([total[512:576, :64], total[512:576, 64:]], 0)
    send[:, 512:] = jnp.concatenate([left, jnp.zeros((HERE, 64), f32)], 1).astype(bf16)
    for i in range(8):
        lanes = slice(i * 128, (i + 1) * 128)
        out[:, lanes] = total[576 + i * 32 : 584 + i * 32]
        down[:, lanes] = total[584 + i * 32 : 606 + i * 32]


def sum_rows(got):
    return pl.pallas_call(
        sum_kernel,
        out_shape=[
            jax.ShapeDtypeStruct((HERE, 640), bf16),
            jax.ShapeDtypeStruct((22, WIDTH), f32),
            jax.ShapeDtypeStruct((8, WIDTH), f32),
        ],
        in_specs=[VMEM],
        out_specs=[VMEM] * 3,
        compiler_params=params(16),
        cost_estimate=cost(0.001, 2),
        name="sum_rows",
    )(got)


def layout_kernel(mine, qkv, gate, up, gain, bias, sums):
    more = jnp.zeros((8, 128), f32)
    for s in range(SEQ):
        here = mine[s * 8 : (s + 1) * 8, :].astype(f32)
        gate[:, s * FF_LOCAL : (s + 1) * FF_LOCAL] = here[:, :FF_LOCAL]
        up[:, s * FF_LOCAL : (s + 1) * FF_LOCAL] = here[:, FF_LOCAL : 2 * FF_LOCAL]
        for i in range(3):
            lo = i * WIDTH + s * HEAD_DIM
            qkv[:, lo : lo + HEAD_DIM] = here[:, 384 + i * HEAD_DIM : 384 + (i + 1) * HEAD_DIM]
        more += here[:, 256:384]
    turned = more.T
    gain[...] = turned[96:97, :]
    bias[...] = turned[97:98, :]
    sums[...] = more[0:1, 98:122]


def last_layout(mine):
    return pl.pallas_call(
        layout_kernel,
        out_shape=[
            jax.ShapeDtypeStruct((8, 3 * WIDTH), f32),
            jax.ShapeDtypeStruct((8, FF), f32),
            jax.ShapeDtypeStruct((8, FF), f32),
            jax.ShapeDtypeStruct((1, 8), f32),
            jax.ShapeDtypeStruct((1, 8), f32),
            jax.ShapeDtypeStruct((1, 24), f32),
        ],
        in_specs=[VMEM],
        out_specs=[VMEM] * 6,
        compiler_params=params(16),
        cost_estimate=cost(0.001, 1),
        name="last_layout",
    )(mine)


PLACES = [(0, 0), (0, -1), (0, 1), (1, 0), (0, 2), (1, 2), (1, 1), (1, -1)]
CORE = [(i, i ^ 1) for i in range(SEQ)]
PAIR = [(i, i ^ 2) for i in range(SEQ)]
UP = [(i, (i + 4) % SEQ) for i in range(SEQ)]
DOWN = [(i, (i + 12) % SEQ) for i in range(SEQ)]
DOWN_PAIR = [(i, (i + 12) % SEQ ^ 2) for i in range(SEQ)]


def send(value, to):
    return lax.ppermute(value, "seq", to)


def gather(x, dy, exchange, after):
    own = jnp.concatenate([x, dy], 0)
    below = send(own, UP)
    above = send(own, DOWN)
    pair = send(own, PAIR)
    late = exchange(below)
    far = send(below, UP)
    opposite = send(above, DOWN_PAIR)
    most = pair[:MOST]
    rest = [far, opposite, send(most, DOWN), send(most, UP)]
    rest.append(send(jnp.concatenate([above[MOST:], below[MOST:]], 0), PAIR))
    first = [both for a in (own, below, above, pair) for both in (a, send(a, CORE))]
    late, rest = after(late, first, rest)
    return first, [both for a in rest for both in (a, send(a, CORE))], late


MOST = 176


def pieces_of(places):
    return [
        (which, i, which * HERE, HERE, i * HERE) for i in range(places) for which in range(2)
    ]


def pieces_late():
    pieces = pieces_of(12)
    for place in range(2):
        for core in range(2):
            to = (12 + 2 * place + core) * HERE
            first, left = 12 + 2 * place + core, 2 * HERE - MOST
            pieces.append((0, first, 0, HERE, to))
            pieces.append((1, first, HERE, MOST - HERE, to))
            pieces.append((1, 16 + core, place * left, left, to + MOST - HERE))
    return pieces


def shards(x, dy, order, ln_gain, ln_bias, w_qkv, b_qkv, w_out, w_gate, w_up, w_down):
    x, dy = x[0], dy[0]
    gain, bias = ln_gain[None, :], ln_bias[None, :]

    table = rotary_tables()
    packed = own_heads(order, x, dy, w_qkv, w_out, b_qkv[None, :], gain, bias, table)
    w_qkv_s, w_gu_s = cut_weights(w_qkv, w_gate, w_up)

    def exchange(first):
        return lax.all_to_all(packed, "seq", 0, 0, tiled=True)

    def attend(packed_here, early, arrays):
        first = first_half(
            early, pieces_of(len(early)), w_gu_s, w_down, gain, bias
        )
        heads = attention(order, packed_here, first)
        return (heads, first), [lax.optimization_barrier((heads, a))[1] for a in arrays]

    early, arrays, (heads, first) = gather(x, dy, exchange, attend)
    heads_here = lax.all_to_all(heads, "seq", 0, 0, tiled=True)
    arrays = early + arrays
    block = weight_grads(
        arrays, pieces_late(), heads, w_qkv_s, w_gu_s, w_down, gain, bias, first
    )
    block, heads_here = lax.optimization_barrier((block, heads_here))
    got = lax.all_to_all(block, "rows", 0, 0, tiled=True)
    x_late, _ = lax.optimization_barrier((x, heads_here))
    part, grad = own_rows(x_late, dy, gain, bias, w_gate, w_up, w_down)
    output, input_grad = final_rows(heads_here, x, dy, part, grad, gain, w_out, w_qkv)
    got, output, input_grad = lax.optimization_barrier((got, output, input_grad))
    outgoing, o_down, o_out = sum_rows(got)
    mine = lax.all_to_all(outgoing, "seq", 0, 0, tiled=True)
    o_qkv, o_gate, o_up, o_gain, o_bias, sums = last_layout(mine)
    return (
        output[None],
        input_grad[None],
        o_qkv,
        o_out,
        o_gate,
        o_up,
        o_down,
        sums[0],
        o_gain[0],
        o_bias[0],
    )


def solution(mesh):
    rows = P("rows", "seq", None)
    both = P(("seq", "rows"), None)
    flat = P(("seq", "rows"))
    return jax.shard_map(
        shards,
        mesh=mesh,
        in_specs=(rows, rows) + (P(),) * 9,
        out_specs=(rows, rows, both, both, both, both, both, flat, flat, flat),
        check_vma=False,
    )
```
